32 devices in a mesh: fsdp: 2 (over x), dp: 16 (over z, y, core).
Axes of the slice: x: 2, y: 2, z: 4, core: 2. Of those that a mesh axis runs over, the one named last changes fastest.
Arguments:
- tokens: bfloat16 [2, 16, 1024, 768], P('fsdp', 'dp'), may hold values from -6 to 6
- live: int32 [2, 16], P('fsdp', 'dp'), may hold values from 0 to 1, as said below
- norm_gain: bfloat16 [768], P('fsdp'), may hold values from 0.5 to 1.5
- w_in: bfloat16 [768, 3352], P('fsdp'), may hold values from -0.21875 to 0.21875
- conv_weight: bfloat16 [1792, 4], P('fsdp'), may hold values from -3 to 3
- conv_bias: bfloat16 [1792], P('fsdp'), may hold values from -3 to 3
- dt_bias: bfloat16 [24], P('fsdp'), may hold values from -4 to 0
- a_log: bfloat16 [24], P('fsdp'), may hold values from -3 to 1
- d_skip: bfloat16 [24], P('fsdp'), may hold values from 0.5 to 1.5
- inner_gain: bfloat16 [1536], P('fsdp'), may hold values from 0.5 to 1.5
- w_out: bfloat16 [1536, 768], P('fsdp'), may hold values from -0.15625 to 0.15625
- cotangent: bfloat16 [2, 16, 1024, 768], P('fsdp', 'dp'), may hold values from -6 to 6
Outputs:
- block_out: bfloat16 [2, 16, 1024, 768], P('fsdp', 'dp')
- input_grad: float32 [2, 16, 1024, 768], P('fsdp', 'dp')
- norm_gain_grad: float32 [768], P('fsdp')
- w_in_grad: float32 [768, 3352], P('fsdp')
- conv_weight_grad: float32 [1792, 4], P('fsdp')
- conv_bias_grad: float32 [1792], P('fsdp')
- dt_bias_grad: float32 [24], P('fsdp')
- a_log_grad: float32 [24], P('fsdp')
- d_skip_grad: float32 [24], P('fsdp')
- inner_gain_grad: float32 [1536], P('fsdp')
- w_out_grad: float32 [1536, 768], P('fsdp')
The draws below stay inside these ranges and needn't reach their ends.
Inputs may be any that keep to these rules, and one draw needn't show every extreme that they name: `live`: 1 marks a device that holds a sequence; some devices hold none.
All inputs are finite; a program needn't handle non-finite values.
Results may differ from the reference program's by a relative error of at most 0.0097.
Values may be sent and summed in bfloat16 or wider, within the bound.
No kernel may reach another device: no remote copies, remote signals or barrier semaphores. Data moves between devices by JAX's collectives and lax.ppermute only.
A program may use at most 192 MiB of HBM per device.

```python
import jax
import jax.numpy as jnp
from jax import lax

D = 768
INNER = 1536
HEADS = 24
CONV = 4
STRETCH = 256
SEQ_LEN = 1024
CONV_CH = 1792
PROJ = 3352
N_FSDP = 2
N_DP = 16


def draw_live(key, part):
    key = jax.random.fold_in(key, 7)
    picks = jax.random.randint(key, (N_FSDP, N_DP), 0, 5)
    columns = lax.broadcasted_iota(jnp.int32, (N_FSDP, N_DP), 1)
    forced = (columns == 0) | (columns == N_DP // 2) | (columns == N_DP - 1)
    return jnp.where(forced, 1, jnp.where(picks < 3, 1, 0)).astype(jnp.int32)


def shard_levels(stream_key, dims, cuts, smallest, high):
    factor_of, own = 1.0, jax.random.fold_in(stream_key, 6)
    for dim, blocks in cuts:
        steps = jnp.exp(jax.random.uniform(jax.random.fold_in(own, dim), (blocks,), jnp.float32, smallest / len(cuts), high / len(cuts)))
        factor_of = factor_of * jnp.repeat(steps, dims[dim] // blocks).reshape([-1 if axis == dim else 1 for axis in range(len(dims))])
    return factor_of


def bell_draw(key, shape, scale, limit, cuts=(), dtype=jnp.bfloat16):
    level = shard_levels(key, shape, cuts, -0.22, 0.18) if cuts else 1.0
    drawn = jax.random.normal(key, shape, jnp.float32) * scale * level
    return jnp.minimum(jnp.maximum(drawn, -limit), limit).astype(dtype)


def setup_inputs(seed: int = 0) -> dict:
    arg_keys = jax.random.split(jax.random.key(seed), 13)
    tokens = bell_draw(arg_keys[0], (N_FSDP, N_DP, SEQ_LEN, D), 1.0, 6.0, ((0, 2), (1, 16)))
    live = draw_live(jax.random.fold_in(arg_keys[12], 71), 0)
    norm_gain = jnp.clip(1.0 + 0.1 * jax.random.normal(arg_keys[2], (D,), jnp.float32), 0.5, 1.5).astype(jnp.bfloat16)
    w_in = bell_draw(arg_keys[3], (D, PROJ), D ** -0.5, 0.21875, ((0, 2),))
    conv_weight = bell_draw(arg_keys[4], (CONV_CH, CONV), CONV ** -0.5, 3.0, ((0, 2),))
    conv_bias = bell_draw(arg_keys[5], (CONV_CH,), 0.5, 3.0, ((0, 2),))
    dt_bias = jnp.clip(-4.0 + 4.0 * jax.random.uniform(arg_keys[6], (HEADS,), jnp.float32) ** shard_levels(arg_keys[6], (HEADS,), ((0, 2),), -0.2, 0.2), -4.0, 0.0).astype(jnp.bfloat16)
    a_log = jnp.clip(-3.0 + 4.0 * jax.random.uniform(arg_keys[7], (HEADS,), jnp.float32) ** shard_levels(arg_keys[7], (HEADS,), ((0, 2),), -0.2, 0.2), -3.0, 1.0).astype(jnp.bfloat16)
    d_skip = jnp.clip(0.5 + 1.0 * jax.random.uniform(arg_keys[8], (HEADS,), jnp.float32) ** shard_levels(arg_keys[8], (HEADS,), ((0, 2),), -0.2, 0.2), 0.5, 1.5).astype(jnp.bfloat16)
    inner_gain = jnp.clip(1.0 + 0.1 * jax.random.normal(arg_keys[9], (INNER,), jnp.float32), 0.5, 1.5).astype(jnp.bfloat16)
    w_out = bell_draw(arg_keys[10], (INNER, D), INNER ** -0.5, 0.15625, ((0, 2),))
    cotangent = bell_draw(arg_keys[11], (N_FSDP, N_DP, SEQ_LEN, D), 1.0, 6.0, ((0, 2), (1, 16)))
    return {"tokens": tokens, "live": live, "norm_gain": norm_gain, "w_in": w_in, "conv_weight": conv_weight, "conv_bias": conv_bias, "dt_bias": dt_bias, "a_log": a_log, "d_skip": d_skip, "inner_gain": inner_gain, "w_out": w_out, "cotangent": cotangent}


EPSILON = 1e-05
PRECISE = lax.Precision.HIGHEST

@jax.custom_vjp
def low(v):
    return lax.optimization_barrier(v.astype(jnp.bfloat16)).astype(jnp.float32)

@jax.custom_vjp
def low_back(v):
    return v

def low_keep(v):
    return (low(v), None)

def low_pass(kept, grad):
    return (grad,)

def back_keep(v):
    return (v, None)

def back_low(kept, grad):
    return (low(grad),)
low.defvjp(low_keep, low_pass)
low_back.defvjp(back_keep, back_low)

def normalize(seq_input, norm_gain):
    return seq_input * lax.rsqrt(lax.optimization_barrier(jnp.mean(seq_input * seq_input, axis=1, keepdims=True)) + EPSILON) * norm_gain[None, :]

def convolve_inputs(mixed_in, raw_step, conv_weight, conv_bias, dt_bias):
    length = mixed_in.shape[0]
    taps = conv_weight.shape[1]
    padded = jnp.pad(mixed_in, ((taps - 1, 0), (0, 0)))
    summed = conv_bias[None, :] + padded[0:length] * conv_weight[:, 0][None, :]
    for offset in range(1, taps):
        summed = summed + padded[offset:offset + length] * conv_weight[:, offset][None, :]
    activated = jax.nn.silu(summed)
    step_size = jax.nn.softplus(raw_step + dt_bias[None, :])
    return (activated, step_size)

def stretch_recurrence(values, inputs_b, inputs_c, step_size, a_log, d_skip):
    length = values.shape[0]
    heads = values.shape[1]
    head_dim = values.shape[2]
    state_dim = inputs_b.shape[1]
    blocks = length // STRETCH
    rates = -jnp.exp(a_log)
    log_steps = step_size * rates[None, :]

    def per_block(state, members):
        value_block, b_block, c_block, step_block, log_block = members
        cumulated = jnp.cumsum(log_block, axis=0).T
        scores = jnp.dot(c_block, b_block.T, precision=PRECISE)
        row_index = lax.broadcasted_iota(jnp.int32, (STRETCH, STRETCH), 0)
        col_index = lax.broadcasted_iota(jnp.int32, (STRETCH, STRETCH), 1)
        causal = (row_index >= col_index)[None, :, :]
        gaps = jnp.where(causal, cumulated[:, :, None] - cumulated[:, None, :], 0.0)
        decay_factor = jnp.where(causal, jnp.exp(gaps), 0.0)
        weights = scores[None, :, :] * decay_factor * step_block.T[:, None, :]
        intra_part = jnp.einsum('hts,shp->thp', weights, value_block, precision=PRECISE)
        carried = jnp.exp(cumulated).T[:, :, None] * jnp.einsum('hpn,tn->thp', state, c_block, precision=PRECISE)
        stretch_total = cumulated[:, -1]
        factor = jnp.exp(stretch_total[:, None] - cumulated) * step_block.T
        scaled = value_block * factor.T[:, :, None]
        new_state = jnp.exp(stretch_total)[:, None, None] * state + jnp.einsum('shp,sn->hpn', scaled, b_block, precision=PRECISE)
        result = intra_part + carried + d_skip[None, :, None] * value_block
        return (new_state, result)
    members = (values.reshape(blocks, STRETCH, heads, head_dim), inputs_b.reshape(blocks, STRETCH, state_dim), inputs_c.reshape(blocks, STRETCH, state_dim), step_size.reshape(blocks, STRETCH, heads), log_steps.reshape(blocks, STRETCH, heads))
    zero_state = jnp.zeros((heads, head_dim, state_dim), jnp.float32)
    final_state, outputs = lax.scan(jax.checkpoint(per_block), zero_state, members)
    return outputs.reshape(length, heads * head_dim)

def state_scan(rounded, step_size, gate_part, a_log, d_skip, inner_gain):
    length = rounded.shape[0]
    heads = a_log.shape[0]
    inner_width = inner_gain.shape[0]
    state_dim = (rounded.shape[1] - inner_width) // 2
    values = rounded[:, :inner_width].reshape(length, heads, inner_width // heads)
    scanned = stretch_recurrence(values, rounded[:, inner_width:inner_width + state_dim], rounded[:, inner_width + state_dim:], step_size, a_log, d_skip)
    gated = scanned * jax.nn.silu(gate_part)
    return gated * lax.rsqrt(lax.optimization_barrier(jnp.mean(gated * gated, axis=1, keepdims=True)) + EPSILON) * inner_gain[None, :]

def residual_block(seq_input, norm_gain, w_in, conv_weight, conv_bias, dt_bias, a_log, d_skip, inner_gain, w_out):
    inner_width = w_out.shape[0]
    conv_width = conv_weight.shape[0]
    projected = low_back(jnp.dot(low(normalize(seq_input, norm_gain)), w_in, precision=PRECISE))
    gate_part = projected[:, :inner_width]
    mixed_in = projected[:, inner_width:inner_width + conv_width]
    raw_step = projected[:, inner_width + conv_width:]
    activated, step_size = convolve_inputs(mixed_in, raw_step, conv_weight, conv_bias, dt_bias)
    mixed_out = state_scan(low(activated), step_size, gate_part, a_log, d_skip, inner_gain)
    return seq_input + jnp.dot(low(mixed_out), w_out, precision=PRECISE)

def reference(tokens, live, norm_gain, w_in, conv_weight, conv_bias, dt_bias, a_log, d_skip, inner_gain, w_out, cotangent):
    slots = N_FSDP * N_DP
    sequences = tokens.reshape(slots, SEQ_LEN, D).astype(jnp.float32)
    alive = live.reshape(slots).astype(jnp.float32)
    params = (norm_gain.astype(jnp.float32), w_in.astype(jnp.float32), conv_weight.astype(jnp.float32), conv_bias.astype(jnp.float32), dt_bias.astype(jnp.float32), a_log.astype(jnp.float32), d_skip.astype(jnp.float32), inner_gain.astype(jnp.float32), w_out.astype(jnp.float32))

    def forward(sequences, params):

        def per_sequence(carried, members):
            seq_input, flag = members
            return (carried, flag * jax.checkpoint(residual_block)(seq_input, *params))
        ignored, outputs = lax.scan(per_sequence, jnp.zeros((), jnp.float32), (sequences, alive))
        return outputs
    outputs, pullback = jax.vjp(forward, sequences, params)
    d_sequences, d_params = pullback(cotangent.reshape(slots, SEQ_LEN, D).astype(jnp.float32))
    shape = (N_FSDP, N_DP, SEQ_LEN, D)
    return (outputs.reshape(shape).astype(jnp.bfloat16), d_sequences.reshape(shape), d_params[0], d_params[1], d_params[2], d_params[3], d_params[4], d_params[5], d_params[6], d_params[7], d_params[8])
```

```python
import functools
import math

import jax
import jax.numpy as jnp
from jax import lax
from jax.experimental import pallas as pl
from jax.experimental.pallas import tpu as pltpu
from jax.sharding import PartitionSpec as P

EPSILON = 1e-05
LOG2E = math.log2(math.e)
SPAN = 256
STRETCH = 128
GROUP = 8
TILE = 256
LANES = 128
VMEM_LIMIT = 60 * 1024 * 1024

F32 = jnp.float32
BF16 = jnp.bfloat16


def mul_nn(a, b):
    return lax.dot_general(a, b, (((1,), (0,)), ((), ())), preferred_element_type=F32)


def mul_nt(a, b):
    return lax.dot_general(a, b, (((1,), (1,)), ((), ())), preferred_element_type=F32)


def mul_tn(a, b):
    return lax.dot_general(a, b, (((0,), (0,)), ((), ())), preferred_element_type=F32)


def triangle(size, keep):
    rows = lax.broadcasted_iota(jnp.int32, (size, size), 0)
    cols = lax.broadcasted_iota(jnp.int32, (size, size), 1)
    return keep(rows, cols)


def lane_sums(values, matrix):
    high = values.astype(BF16)
    rest = values - high.astype(F32)
    middle = rest.astype(BF16)
    low = (rest - middle.astype(F32)).astype(BF16)
    return mul_nn(high, matrix) + mul_nn(middle, matrix) + mul_nn(low, matrix)


def as_columns(rows):
    heads, span = rows.shape
    return jnp.concatenate([rows, jnp.zeros((LANES - heads, span), F32)], axis=0).T


def later(block, before, shift):
    lane = lax.broadcasted_iota(jnp.int32, (block.shape[0], LANES), 1)
    moved = pltpu.roll(block, shift, 1)
    first = jnp.where(lane < shift, pltpu.roll(before, shift, 1), moved[:, :LANES])
    if block.shape[1] == LANES:
        return first
    return jnp.concatenate([first, moved[:, LANES:]], axis=1)


def earlier(block, after, shift):
    span = block.shape[1]
    lane = lax.broadcasted_iota(jnp.int32, (block.shape[0], LANES), 1)
    moved = pltpu.roll(block, span - shift, 1)
    last = jnp.where(lane >= LANES - shift, pltpu.roll(after, LANES - shift, 1), moved[:, span - LANES :])
    if span == LANES:
        return last
    return jnp.concatenate([moved[:, : span - LANES], last], axis=1)


def fold(block):
    total = block[:, :LANES]
    for first in range(LANES, block.shape[1], LANES):
        total = total + block[:, first : first + LANES]
    return total


def softplus(v):
    return jnp.maximum(v, 0.0) + jnp.log1p(jnp.exp(-jnp.abs(v)))


def sigmoid(v):
    return 1.0 / (1.0 + jnp.exp(-v))


def decays(step, rate2):
    span = step.shape[1]
    upper = triangle(span, lambda r, c: r <= c).astype(BF16)
    cum = lane_sums(step * rate2, upper)
    total = cum[:, span - 1 : span]
    return cum, jnp.exp2(total - cum), jnp.exp2(cum), jnp.exp2(total)


def forward_body(
    sizes,
    skip_ref,
    alive_ref,
    tokens_ref,
    cotangent_ref,
    gain_ref,
    weight_ref,
    out_weight_ref,
    columns_ref,
    heads_ref,
    normed_ref,
    mixed_ref,
    active_ref,
    raw_ref,
    states_ref,
    low_mixed_ref,
    d_gate_ref,
    d_scan_ref,
    row_part_ref,
    skip_part_ref,
    gain_part_ref,
    state,
    tail,
    gate,
    scanned,
    carried,
    scaled,
    gated,
    d_normed,
    update,
    cum_s,
    step_s,
    factor_s,
    ec_s,
    total_s,
):
    inner, conv, heads, state_dim = sizes
    width = inner // heads
    span = tokens_ref.shape[0]
    stretch = min(STRETCH, span)

    @pl.when(pl.program_id(0) == 0)
    def _():
        state[...] = jnp.zeros_like(state)
        tail[...] = jnp.zeros_like(tail)
        gain_part_ref[...] = jnp.zeros_like(gain_part_ref)

    u = tokens_ref[...].astype(F32)
    normed = u * lax.rsqrt(jnp.mean(u * u, axis=1, keepdims=True) + EPSILON) * gain_ref[...]
    normed = normed.astype(BF16)
    normed_ref[...] = normed

    @pl.loop(0, inner // TILE)
    def _(i):
        rows = pl.ds(pl.multiple_of(i * TILE, TILE), TILE)
        gate[rows, :] = mul_nt(weight_ref[rows, :], normed)

    @pl.loop(0, conv // TILE)
    def _(i):
        rows = pl.ds(pl.multiple_of(i * TILE, TILE), TILE)
        block = mul_nt(weight_ref[pl.ds(pl.multiple_of(inner + i * TILE, TILE), TILE), :], normed)
        before = tail[rows, :]
        tail[rows, :] = block[:, span - LANES :]
        mixed_ref[rows, :] = block.astype(BF16)
        cols = columns_ref[rows, :]
        summed = cols[:, 4:5] + block * cols[:, 3:4]
        for shift in range(1, 4):
            summed = summed + later(block, before, shift) * cols[:, 3 - shift : 4 - shift]
        active_ref[rows, :] = (summed * sigmoid(summed)).astype(BF16)

    raw = mul_nt(weight_ref[inner + conv : inner + conv + 32, :], normed)[:heads] + heads_ref[:, 0:1]
    raw_ref[...] = raw
    step_all = softplus(raw)
    rate2 = -jnp.exp(heads_ref[:, 1:2]) * LOG2E
    causal = triangle(stretch, lambda r, c: r <= c)
    for part in range(span // stretch):
        lanes = slice(part * stretch, (part + 1) * stretch)
        step = step_all[:, lanes]
        cum, factor, ec, total = decays(step, rate2)
        cum_s[...] = cum
        step_s[...] = step
        factor_s[...] = factor * step
        ec_s[...] = ec
        total_s[...] = jnp.broadcast_to(total, (heads, LANES))
        b_in = active_ref[inner : inner + state_dim, lanes]
        c_in = active_ref[inner + state_dim : inner + 2 * state_dim, lanes]
        scores = jnp.where(causal, mul_tn(b_in, c_in), 0.0)
        low_state = state[...].astype(BF16)
        states_ref[part] = low_state
        carried[...] = mul_nn(low_state, c_in)

        @pl.loop(0, heads // GROUP)
        def _(group):
            eight = pl.ds(pl.multiple_of(group * GROUP, GROUP), GROUP)
            cum_g, step_g, factor_g, ec_g = cum_s[eight, :], step_s[eight, :], factor_s[eight, :], ec_s[eight, :]
            cum_c = as_columns(cum_g)
            for j in range(GROUP):
                rows = pl.ds(pl.multiple_of((group * GROUP + j) * width, width), width)
                row = slice(j, j + 1)
                values = active_ref[rows, lanes].astype(F32)
                stepped = (values * step_g[row]).astype(BF16)
                decay = jnp.exp2(jnp.minimum(cum_g[row] - cum_c[:, row], 0.0))
                weights = (scores * decay).astype(BF16)
                scanned[rows, lanes] = mul_nn(stepped, weights) + ec_g[row] * carried[rows, :]
                scaled[rows, :] = (values * factor_g[row]).astype(BF16)

        update[...] = mul_nt(scaled[...], b_in)

        @pl.loop(0, heads // GROUP)
        def _(group):
            eight = pl.ds(pl.multiple_of(group * GROUP, GROUP), GROUP)
            total_g = total_s[eight, :]
            for j in range(GROUP):
                rows = pl.ds(pl.multiple_of((group * GROUP + j) * width, width), width)
                state[rows, :] = total_g[j : j + 1] * state[rows, :] + update[rows, :]

    def gated_head(h, squares):
        rows = pl.ds(pl.multiple_of(h * width, width), width)
        z = gate[rows, :]
        y = scanned[rows, :] + skip_ref[h] * active_ref[rows, :].astype(F32)
        v = y * (z * sigmoid(z))
        gated[rows, :] = v
        return squares + (v * v).reshape(width // 8, 8, span).sum(axis=0)

    squares = lax.fori_loop(0, heads, gated_head, jnp.zeros((8, span), F32))
    scale = lax.rsqrt(jnp.sum(squares, axis=0, keepdims=True) / inner + EPSILON)
    incoming = (cotangent_ref[...].astype(F32) * alive_ref[0]).astype(BF16)

    def norm_tile(i, dots):
        rows = pl.ds(pl.multiple_of(i * TILE, TILE), TILE)
        gain = columns_ref[rows, 5:6]
        unit = gated[rows, :] * scale
        low_mixed_ref[rows, :] = (unit * gain).astype(BF16)
        d_mixed = mul_nt(out_weight_ref[rows, :], incoming)
        gain_part_ref[rows, :] += fold(d_mixed * unit)
        d_unit = d_mixed * gain
        d_normed[rows, :] = d_unit
        return dots + (d_unit * unit).reshape(TILE // 8, 8, span).sum(axis=0)

    dots = lax.fori_loop(0, inner // TILE, norm_tile, jnp.zeros((8, span), F32))
    mean_dot = jnp.sum(dots, axis=0, keepdims=True) / inner

    @pl.loop(0, heads // GROUP)
    def _(group):
        eight = pl.ds(pl.multiple_of(group * GROUP, GROUP), GROUP)
        row_parts, skip_parts = [], []
        for j in range(GROUP):
            h = group * GROUP + j
            rows = pl.ds(pl.multiple_of(h * width, width), width)
            z = gate[rows, :]
            sig = sigmoid(z)
            values = active_ref[rows, :].astype(F32)
            pure = scanned[rows, :]
            y = pure + skip_ref[h] * values
            d_gated = scale * (d_normed[rows, :] - gated[rows, :] * (scale * mean_dot))
            d_scan = (d_gated * (z * sig)).astype(BF16)
            d_scan_ref[rows, :] = d_scan
            d_gate_ref[rows, :] = (d_gated * y * (sig * (1.0 + z * (1.0 - sig)))).astype(BF16)
            d_scan = d_scan.astype(F32)
            row_parts.append(jnp.sum(d_scan * pure, axis=0, keepdims=True))
            skip_parts.append(jnp.sum(d_scan * values, axis=0, keepdims=True))
        row_part_ref[eight, :] = jnp.concatenate(row_parts, axis=0)
        skip_part_ref[eight, :] = jnp.concatenate(skip_parts, axis=0)


def backward_body(
    sizes,
    skip_ref,
    active_ref,
    mixed_ref,
    before_ref,
    d_scan_ref,
    raw_ref,
    row_part_ref,
    states_ref,
    columns_ref,
    heads_ref,
    d_rest_ref,
    d_raw_ref,
    rate_part_ref,
    conv_part_ref,
    d_state,
    carry,
    d_active,
    sums,
    from_state,
    scaled,
    d_scaled,
    d_scores,
    state_dots,
    cum_s,
    step_s,
    factor_s,
    ec_s,
    total_s,
    pair_s,
    direct_s,
    ending_s,
):
    inner, conv, heads, state_dim = sizes
    width = inner // heads
    span = active_ref.shape[1]
    stretch = min(STRETCH, span)
    first_block = pl.program_id(0) == pl.num_programs(0) - 1

    @pl.when(pl.program_id(0) == 0)
    def _():
        d_state[...] = jnp.zeros_like(d_state)
        carry[...] = jnp.zeros_like(carry)
        sums[...] = jnp.zeros_like(sums)

    raw = raw_ref[...]
    step_all = softplus(raw)
    slope = sigmoid(raw)
    rate = -jnp.exp(heads_ref[:, 1:2])
    rate2 = rate * LOG2E
    causal = triangle(stretch, lambda r, c: r <= c)
    ending = triangle(stretch, lambda r, c: r >= c).astype(BF16)
    before_it = triangle(stretch, lambda r, c: r < c).astype(BF16)
    for part in reversed(range(span // stretch)):
        lanes = slice(part * stretch, (part + 1) * stretch)
        step = step_all[:, lanes]
        cum, factor, ec, total = decays(step, rate2)
        cum_s[...] = cum
        step_s[...] = step
        factor_s[...] = factor
        ec_s[...] = ec
        total_s[...] = jnp.broadcast_to(total, (heads, LANES))
        b_in = active_ref[inner : inner + state_dim, lanes]
        c_in = active_ref[inner + state_dim : inner + 2 * state_dim, lanes]
        scores = jnp.where(causal, mul_tn(b_in, c_in), 0.0)
        low_d_state = d_state[...].astype(BF16)
        from_state[...] = mul_nn(low_d_state, b_in)
        d_scores[...] = jnp.zeros_like(d_scores)

        @pl.loop(0, heads // GROUP)
        def _(group):
            eight = pl.ds(pl.multiple_of(group * GROUP, GROUP), GROUP)
            cum_g, step_g, factor_g, ec_g = cum_s[eight, :], step_s[eight, :], factor_s[eight, :], ec_s[eight, :]
            cum_c = as_columns(cum_g)
            pairs, directs, endings, dots = [], [], [], []
            d_scores_g = d_scores[...]
            for j in range(GROUP):
                h = group * GROUP + j
                rows = pl.ds(pl.multiple_of(h * width, width), width)
                row = slice(j, j + 1)
                values = active_ref[rows, lanes].astype(F32)
                stepped = (values * step_g[row]).astype(BF16)
                low_d = d_scan_ref[rows, lanes]
                d_scan = low_d.astype(F32)
                decay = jnp.exp2(jnp.minimum(cum_g[row] - cum_c[:, row], 0.0))
                weights = (scores * decay).astype(BF16)
                inside = mul_nt(low_d, weights)
                d_scores_g = d_scores_g + mul_tn(stepped, low_d) * decay
                across = from_state[rows, :] * factor_g[row]
                both = inside + across
                d_active[rows, lanes] = step_g[row] * both + skip_ref[h] * d_scan
                pairs.append(jnp.sum(stepped.astype(F32) * inside, axis=0, keepdims=True))
                directs.append(jnp.sum(values * both, axis=0, keepdims=True))
                endings.append(jnp.sum(values * across, axis=0, keepdims=True))
                scaled[rows, :] = (values * (step_g[row] * factor_g[row])).astype(BF16)
                d_scaled[rows, :] = (d_scan * ec_g[row]).astype(BF16)
                dots.append(jnp.sum(d_state[rows, :] * states_ref[part, rows, :].astype(F32), axis=0, keepdims=True))
            d_scores[...] = d_scores_g
            pair_s[eight, :] = jnp.concatenate(pairs, axis=0)
            direct_s[eight, :] = jnp.concatenate(directs, axis=0)
            ending_s[eight, :] = jnp.concatenate(endings, axis=0)
            state_dots[eight, :] = jnp.concatenate(dots, axis=0)

        low_d_scores = jnp.where(causal, d_scores[...], 0.0).astype(BF16)
        low_state = states_ref[part]
        d_active[inner : inner + state_dim, lanes] = mul_tn(low_d_state, scaled[...]) + mul_nt(c_in, low_d_scores)
        d_active[inner + state_dim : inner + 2 * state_dim, lanes] = mul_tn(low_state, d_scaled[...]) + mul_nn(
            b_in, low_d_scores
        )
        from_state[...] = mul_nt(d_scaled[...], c_in)

        @pl.loop(0, heads // GROUP)
        def _(group):
            eight = pl.ds(pl.multiple_of(group * GROUP, GROUP), GROUP)
            total_g = total_s[eight, :]
            for j in range(GROUP):
                rows = pl.ds(pl.multiple_of((group * GROUP + j) * width, width), width)
                d_state[rows, :] = total_g[j : j + 1] * d_state[rows, :] + from_state[rows, :]

        d_log = (
            lane_sums(row_part_ref[:, lanes] - pair_s[...], ending)
            + lane_sums(step * ending_s[...], before_it)
            + total * jnp.sum(state_dots[...], axis=1, keepdims=True)
        )
        rate_part_ref[:, lanes] = d_log * step * rate
        d_raw_ref[:, lanes] = (direct_s[...] + d_log * rate) * slope[:, lanes]

    @pl.loop(0, conv // TILE)
    def _(i):
        rows = pl.ds(pl.multiple_of(i * TILE, TILE), TILE)
        block = mixed_ref[rows, :].astype(F32)
        before = jnp.where(first_block, 0.0, before_ref[rows, :].astype(F32))
        cols = columns_ref[rows, :]
        moved = [block] + [later(block, before, shift) for shift in range(1, 4)]
        summed = cols[:, 4:5] + block * cols[:, 3:4]
        for shift in range(1, 4):
            summed = summed + moved[shift] * cols[:, 3 - shift : 4 - shift]
        sig = sigmoid(summed)
        d_summed = d_active[rows, :] * (sig * (1.0 + summed * (1.0 - sig)))
        after = carry[rows, :]
        carry[rows, :] = d_summed[:, :LANES]
        d_block = d_summed * cols[:, 3:4]
        for shift in range(1, 4):
            d_block = d_block + earlier(d_summed, after, shift) * cols[:, 3 - shift : 4 - shift]
        d_rest_ref[rows, :] = d_block.astype(BF16)
        for shift in range(4):
            sums[3 - shift, rows, :] += fold(d_summed * moved[shift])
        sums[4, rows, :] += fold(d_summed)

    @pl.when(first_block)
    def _():
        @pl.loop(0, conv // TILE)
        def _(i):
            rows = pl.ds(pl.multiple_of(i * TILE, TILE), TILE)
            lane = lax.broadcasted_iota(jnp.int32, (TILE, LANES), 1)
            result = jnp.zeros((TILE, LANES), F32)
            for k in range(5):
                result = jnp.where(lane == k, jnp.sum(sums[k, rows, :], axis=1, keepdims=True), result)
            conv_part_ref[rows, :] = result


def whole(shape):
    return pl.BlockSpec(shape, lambda c: (0,) * len(shape), pipeline_mode=pl.Buffered(1))


def forward(sizes, skip, alive, tokens, cotangent, gain, weight, out_weight, columns, heads_in):
    inner, conv, heads, state_dim = sizes
    length, model = tokens.shape
    span = min(SPAN, length)
    stretch = min(STRETCH, span)
    parts = span // stretch
    smem = pl.BlockSpec(memory_space=pltpu.SMEM)
    along = lambda rows: pl.BlockSpec((rows, span), lambda c: (0, c))
    down = pl.BlockSpec((span, model), lambda c: (c, 0))
    shape = jax.ShapeDtypeStruct
    return pl.pallas_call(
        functools.partial(forward_body, sizes),
        grid=(length // span,),
        in_specs=[
            smem,
            smem,
            down,
            down,
            whole(gain.shape),
            whole(weight.shape),
            whole(out_weight.shape),
            whole(columns.shape),
            whole(heads_in.shape),
        ],
        out_specs=[
            down,
            along(conv),
            along(conv),
            along(heads),
            pl.BlockSpec((parts, inner, state_dim), lambda c: (c, 0, 0)),
            along(inner),
            along(inner),
            along(inner),
            along(heads),
            along(heads),
            pl.BlockSpec((inner, LANES), lambda c: (0, 0)),
        ],
        out_shape=[
            shape((length, model), BF16),
            shape((conv, length), BF16),
            shape((conv, length), BF16),
            shape((heads, length), F32),
            shape((length // stretch, inner, state_dim), BF16),
            shape((inner, length), BF16),
            shape((inner, length), BF16),
            shape((inner, length), BF16),
            shape((heads, length), F32),
            shape((heads, length), F32),
            shape((inner, LANES), F32),
        ],
        scratch_shapes=[
            pltpu.VMEM((inner, state_dim), F32),
            pltpu.VMEM((conv, LANES), F32),
            pltpu.VMEM((inner, span), F32),
            pltpu.VMEM((inner, span), F32),
            pltpu.VMEM((inner, stretch), F32),
            pltpu.VMEM((inner, stretch), BF16),
            pltpu.VMEM((inner, span), F32),
            pltpu.VMEM((inner, span), F32),
            pltpu.VMEM((inner, state_dim), F32),
            pltpu.VMEM((heads, stretch), F32),
            pltpu.VMEM((heads, stretch), F32),
            pltpu.VMEM((heads, stretch), F32),
            pltpu.VMEM((heads, stretch), F32),
            pltpu.VMEM((heads, LANES), F32),
        ],
        compiler_params=pltpu.CompilerParams(
            dimension_semantics=("arbitrary",), vmem_limit_bytes=VMEM_LIMIT
        ),
        name="block_forward",
    )(skip, alive, tokens, cotangent, gain, weight, out_weight, columns, heads_in)


def backward(sizes, skip, active, mixed, d_scan, raw, row_part, states, columns, heads_in):
    inner, conv, heads, state_dim = sizes
    length = active.shape[1]
    span = min(SPAN, length)
    stretch = min(STRETCH, span)
    parts = span // stretch
    blocks = length // span
    per = span // LANES
    smem = pl.BlockSpec(memory_space=pltpu.SMEM)
    along = lambda rows: pl.BlockSpec((rows, span), lambda c: (0, blocks - 1 - c))
    shape = jax.ShapeDtypeStruct
    return pl.pallas_call(
        functools.partial(backward_body, sizes),
        grid=(blocks,),
        in_specs=[
            smem,
            along(conv),
            along(conv),
            pl.BlockSpec((conv, LANES), lambda c: (0, jnp.maximum((blocks - 1 - c) * per - 1, 0))),
            along(inner),
            along(heads),
            along(heads),
            pl.BlockSpec((parts, inner, state_dim), lambda c: (blocks - 1 - c, 0, 0)),
            whole(columns.shape),
            whole(heads_in.shape),
        ],
        out_specs=[
            along(conv),
            along(heads),
            along(heads),
            pl.BlockSpec((conv, LANES), lambda c: (0, 0)),
        ],
        out_shape=[
            shape((conv, length), BF16),
            shape((heads, length), F32),
            shape((heads, length), F32),
            shape((conv, LANES), F32),
        ],
        scratch_shapes=[
            pltpu.VMEM((inner, state_dim), F32),
            pltpu.VMEM((conv, LANES), F32),
            pltpu.VMEM((conv, span), F32),
            pltpu.VMEM((5, conv, LANES), F32),
            pltpu.VMEM((inner, stretch), F32),
            pltpu.VMEM((inner, stretch), BF16),
            pltpu.VMEM((inner, stretch), BF16),
            pltpu.VMEM((stretch, stretch), F32),
            pltpu.VMEM((heads, state_dim), F32),
            pltpu.VMEM((heads, stretch), F32),
            pltpu.VMEM((heads, stretch), F32),
            pltpu.VMEM((heads, stretch), F32),
            pltpu.VMEM((heads, stretch), F32),
            pltpu.VMEM((heads, LANES), F32),
            pltpu.VMEM((heads, stretch), F32),
            pltpu.VMEM((heads, stretch), F32),
            pltpu.VMEM((heads, stretch), F32),
        ],
        compiler_params=pltpu.CompilerParams(
            dimension_semantics=("arbitrary",), vmem_limit_bytes=VMEM_LIMIT
        ),
        name="block_backward",
    )(skip, active, mixed, mixed, d_scan, raw, row_part, states, columns, heads_in)


def powers_of_two(size):
    bits, bit = [], 1
    while bit < size:
        bits.append(bit)
        bit *= 2
    return bits if bit == size else None


def swap(block, axis, bit):
    pairs = [(k, k ^ bit) for k in range(lax.axis_size(axis))]
    return lax.ppermute(block, axis, pairs)


def halves(block, side):
    rows = block.shape[0] // 2
    keep = lax.dynamic_slice_in_dim(block, side * rows, rows, 0)
    give = lax.dynamic_slice_in_dim(block, (1 - side) * rows, rows, 0)
    return keep, give


def halve(block, axis, bit):
    side = (lax.axis_index(axis) // bit) % 2
    keep, give = halves(block, side)
    return (keep.astype(F32) + swap(give, axis, bit).astype(F32)).astype(block.dtype)


def double(block, axis, bit):
    side = (lax.axis_index(axis) // bit) % 2
    other = swap(block, axis, bit)
    return jnp.where(
        side == 0, jnp.concatenate([block, other], axis=0), jnp.concatenate([other, block], axis=0)
    )


def summed_share(parts):
    groups = parts.shape[0]
    owner_bits, copy_bits = powers_of_two(lax.axis_size("fsdp")), powers_of_two(lax.axis_size("dp"))
    if owner_bits is None or copy_bits is None or parts.shape[1] % (8 * lax.axis_size("dp")):
        total = lax.psum(parts, ("fsdp", "dp"))
        return lax.dynamic_index_in_dim(total, lax.axis_index("fsdp"), 0, False).astype(F32)
    rows, columns = parts.shape[1:]
    block = parts.transpose(1, 0, 2)
    for bit in copy_bits[:1]:
        block = halve(block, "dp", bit)
    block = block.transpose(1, 0, 2)
    for bit in reversed(owner_bits):
        block = halve(block, "fsdp", bit)
    block = block[0]
    for bit in copy_bits[1:]:
        block = halve(block, "dp", bit)
    for bit in reversed(copy_bits):
        block = double(block, "dp", bit)
    return block.astype(F32)


def gathered_rows(block):
    groups, copies = lax.axis_size("fsdp"), lax.axis_size("dp")
    rows = block.shape[0]
    if groups != 2 or copies % 2 or rows % 32:
        return lax.all_gather(block, "fsdp")
    core = lax.axis_index("dp") % 2
    keep, _ = halves(block, core)
    direct = swap(keep, "fsdp", 1)
    relayed = swap(direct, "dp", 1)
    other = jnp.where(
        core == 0, jnp.concatenate([direct, relayed], axis=0), jnp.concatenate([relayed, direct], axis=0)
    )
    mine = lax.axis_index("fsdp")
    return jnp.where(mine == 0, jnp.stack([block, other]), jnp.stack([other, block]))


def shards(
    tokens,
    live,
    norm_gain,
    w_in,
    conv_weight,
    conv_bias,
    dt_bias,
    a_log,
    d_skip,
    inner_gain,
    w_out,
    cotangent,
):
    groups = lax.axis_size("fsdp")
    conv_each, inner_each, model_each, heads_each = (
        conv_weight.shape[0],
        inner_gain.shape[0],
        norm_gain.shape[0],
        dt_bias.shape[0],
    )
    conv, inner, heads = conv_each * groups, inner_each * groups, heads_each * groups
    model = tokens.shape[-1]
    proj = w_in.shape[1]
    sizes = (inner, conv, heads, (conv - inner) // 2)
    rows_padded = -(-proj // 32) * 32

    small_each = jnp.concatenate([norm_gain, dt_bias, a_log, d_skip])
    line = max(conv_each, inner_each, small_each.shape[0])
    fit = lambda v: jnp.pad(v, (0, line - v.shape[0]))[None]
    packed = jnp.concatenate(
        [jnp.pad(conv_weight.T, ((0, 0), (0, line - conv_each))), fit(conv_bias), fit(inner_gain), fit(small_each)],
        axis=0,
    )
    small = lax.all_gather(packed, "fsdp").astype(F32)
    taps = conv_weight.shape[1]
    lined = lambda k, first, each: small[:, k, first : first + each].reshape(1, groups * each)
    gain = lined(taps + 2, 0, model_each)
    first = model_each
    step_bias, log_rate, skip = [lined(taps + 2, first + k * heads_each, heads_each)[0] for k in range(3)]
    columns = jnp.concatenate(
        [lined(k, 0, conv_each) for k in range(taps + 1)]
        + [jnp.pad(lined(taps + 1, 0, inner_each), ((0, 0), (0, conv - inner))), jnp.zeros((2, conv), F32)],
        axis=0,
    ).T
    heads_in = jnp.stack([step_bias, log_rate], axis=1)

    weight = gathered_rows(jnp.pad(w_in.T, ((0, rows_padded - proj), (0, 0))))
    weight = weight.transpose(1, 0, 2).reshape(rows_padded, model)
    out_weight = gathered_rows(w_out).reshape(inner, model)

    alive = live.astype(F32).reshape(1)
    low_tokens, low_cotangent = tokens[0, 0], cotangent[0, 0]
    (
        normed,
        mixed,
        active,
        raw,
        states,
        low_mixed,
        d_gate,
        d_scan,
        row_part,
        skip_part,
        gain_part,
    ) = forward(sizes, skip, alive, low_tokens, low_cotangent, gain, weight, out_weight, columns, heads_in)
    u = low_tokens.astype(F32)
    incoming = low_cotangent.astype(F32) * alive[0]
    low_incoming = incoming.astype(BF16)

    def owned(left):
        product = mul_nn(left, normed).astype(BF16)
        return product.reshape(left.shape[0], groups, model_each).transpose(1, 0, 2)

    out_parts = mul_nn(low_mixed, low_incoming).astype(BF16).reshape(groups, inner_each, model)
    g_out = summed_share(out_parts)
    g_gate = summed_share(owned(d_gate))

    d_rest, d_raw, rate_part, conv_part = backward(
        sizes, skip, active, mixed, d_scan, raw, row_part, states, columns, heads_in
    )
    spare = -(-(proj - inner) // (16 * lax.axis_size("dp"))) * 16 * lax.axis_size("dp") - conv - heads
    d_rest = jnp.concatenate([d_rest, d_raw.astype(BF16), jnp.zeros((spare, d_raw.shape[1]), BF16)], axis=0)
    g_rest = summed_share(owned(d_rest))[: proj - inner]

    block_out = (alive[0] * (u + mul_tn(low_mixed, out_weight))).astype(BF16)
    d_normed = mul_tn(d_gate, weight[:inner]) + mul_tn(d_rest[: proj - inner], weight[inner:proj])
    scale = lax.rsqrt(jnp.mean(u * u, axis=1, keepdims=True) + EPSILON)
    unit = u * scale
    d_unit = d_normed * gain
    input_grad = incoming + scale * (d_unit - unit * jnp.mean(d_unit * unit, axis=1, keepdims=True))

    small_grads = (
        jnp.sum(d_normed * unit, axis=0),
        conv_part[:, :taps],
        conv_part[:, taps],
        jnp.sum(d_raw, axis=1),
        jnp.sum(rate_part, axis=1),
        jnp.sum(skip_part, axis=1),
        jnp.sum(gain_part, axis=1),
    )
    totals = lax.psum(small_grads, ("fsdp", "dp"))
    owner = lax.axis_index("fsdp")
    g_gain, g_conv, g_shift, g_bias, g_rate, g_skip, g_inner = [
        lax.dynamic_slice_in_dim(total, owner * (total.shape[0] // groups), total.shape[0] // groups, 0)
        for total in totals
    ]
    g_proj = jnp.concatenate([g_gate, g_rest], axis=0).T
    return (
        block_out.reshape(tokens.shape),
        input_grad.reshape(cotangent.shape),
        g_gain,
        g_proj,
        g_conv,
        g_shift,
        g_bias,
        g_rate,
        g_skip,
        g_inner,
        g_out,
    )


def solution(mesh):
    by_device = P("fsdp", "dp", None, None)
    lines, tables = P("fsdp"), P("fsdp", None)
    return jax.shard_map(
        shards,
        mesh=mesh,
        in_specs=(
            by_device,
            P("fsdp", "dp"),
            lines,
            tables,
            tables,
            lines,
            lines,
            lines,
            lines,
            lines,
            tables,
            by_device,
        ),
        out_specs=(by_device, by_device, lines, tables, tables, lines, lines, lines, lines, lines, tables),
        check_vma=False,
    )
```

```python
import functools
import math

import jax
import jax.numpy as jnp
from jax import lax
from jax.experimental import pallas as pl
from jax.experimental.pallas import tpu as pltpu
from jax.sharding import PartitionSpec as P

EPSILON = 1e-05
LOG2E = math.log2(math.e)
SPAN = 256
STRETCH = 128
GROUP = 8
TILE = 256
LANES = 128
TILES_ABREAST = 7
HEADS_ABREAST = 2
HEAD_RANGES = ((0, 16), (16, 8))
VMEM_LIMIT = 60 * 1024 * 1024

F32 = jnp.float32
BF16 = jnp.bfloat16


def mul_nn(a, b):
    return lax.dot_general(a, b, (((1,), (0,)), ((), ())), preferred_element_type=F32)


def mul_nt(a, b):
    return lax.dot_general(a, b, (((1,), (1,)), ((), ())), preferred_element_type=F32)


def mul_tn(a, b):
    return lax.dot_general(a, b, (((0,), (0,)), ((), ())), preferred_element_type=F32)


def triangle(size, keep):
    rows = lax.broadcasted_iota(jnp.int32, (size, size), 0)
    cols = lax.broadcasted_iota(jnp.int32, (size, size), 1)
    return keep(rows, cols)


def lane_sums(values, matrix):
    high = values.astype(BF16)
    rest = values - high.astype(F32)
    middle = rest.astype(BF16)
    low = (rest - middle.astype(F32)).astype(BF16)
    return mul_nn(high, matrix) + mul_nn(middle, matrix) + mul_nn(low, matrix)


def as_columns(rows):
    heads, span = rows.shape
    return jnp.concatenate([rows, jnp.zeros((LANES - heads, span), F32)], axis=0).T


def fold(block):
    total = block[:, :LANES]
    for first in range(LANES, block.shape[1], LANES):
        total = total + block[:, first : first + LANES]
    return total


def eighths(block):
    return block.reshape(block.shape[0] // 8, 8, block.shape[1]).sum(axis=0)


def softplus(v):
    return jnp.maximum(v, 0.0) + jnp.log1p(jnp.exp(-jnp.abs(v)))


def sigmoid(v):
    return 0.5 * jnp.tanh(0.5 * v) + 0.5


def decays(step, rate2):
    span = step.shape[1]
    upper = triangle(span, lambda r, c: r <= c).astype(BF16)
    cum = lane_sums(step * rate2, upper)
    total = cum[:, span - 1 : span]
    return cum, jnp.exp2(total - cum), jnp.exp2(cum), jnp.exp2(total)


def piece_copies(places_ref, lengths, pieces, whole_ref, sems):
    copies = []
    for k, piece in enumerate(pieces):
        rows, columns = lengths[k], piece.shape[1]
        target = whole_ref.at[
            pl.ds(pl.multiple_of(places_ref[2 * k], 16), rows),
            pl.ds(pl.multiple_of(places_ref[2 * k + 1], LANES), columns),
        ]
        copies.append(pltpu.make_async_copy(piece.at[pl.ds(0, rows), :], target, sems.at[k]))
    return copies


def forward_body(sizes, lengths, places_ref, tokens_ref, gain_ref, raw_weight_ref, taps_ref, heads_ref, *refs):
    n_pieces = len(lengths)
    pieces, refs = refs[:n_pieces], refs[n_pieces:]
    (
        normed_ref,
        mixed_ref,
        active_ref,
        raw_ref,
        states_ref,
        gate_ref,
        scanned_ref,
        weight_ref,
        weight,
        state,
        extended,
        carried,
        scaled,
        update,
        cum_s,
        step_s,
        factor_s,
        ec_s,
        total_s,
        sems,
    ) = refs
    inner, conv, heads, state_dim = sizes
    width = inner // heads
    span = tokens_ref.shape[0]
    stretch = min(STRETCH, span)
    copies = piece_copies(places_ref, lengths, pieces, weight, sems)
    kept = pltpu.make_async_copy(weight, weight_ref, sems.at[n_pieces])

    @pl.when(pl.program_id(0) == 0)
    def _():
        for copy in copies:
            copy.start()
        state[...] = jnp.zeros_like(state)
        extended[:, span:, :] = jnp.zeros((conv // LANES, 8, LANES), F32)

    u = tokens_ref[...].astype(F32)
    normed = u * lax.rsqrt(jnp.mean(u * u, axis=1, keepdims=True) + EPSILON) * gain_ref[...]
    normed = normed.astype(BF16)
    normed_ref[...] = normed

    @pl.when(pl.program_id(0) == 0)
    def _():
        for copy in copies:
            copy.wait()
        kept.start()

    @pl.loop(0, inner // TILE, unroll=3)
    def _(i):
        rows = pl.ds(pl.multiple_of(i * TILE, TILE), TILE)
        gate_ref[rows, :] = mul_nt(weight[rows, :], normed)

    @pl.loop(0, conv // TILE, unroll=TILES_ABREAST)
    def _(i):
        first = pl.multiple_of(i * TILE, TILE)
        wide = mul_nt(normed, weight[pl.ds(pl.multiple_of(inner + first, TILE), TILE), :])
        for k in range(TILE // LANES):
            index = i * (TILE // LANES) + k
            block = wide[:, k * LANES : (k + 1) * LANES]
            extended[index, :8, :] = extended[index, span:, :]
            extended[index, 8:, :] = block
            taps = taps_ref[index]
            summed = taps[4:5] + block * taps[3:4]
            for shift in range(1, 4):
                summed = summed + extended[index, 8 - shift : 8 - shift + span, :] * taps[3 - shift : 4 - shift]
            lanes = pl.ds(pl.multiple_of(first + k * LANES, LANES), LANES)
            mixed_ref[:, lanes] = block.astype(BF16)
            active_ref[lanes, :] = (summed * sigmoid(summed)).T.astype(BF16)

    raw = mul_nt(raw_weight_ref[...], normed)[:heads] + heads_ref[:, 0:1]
    raw_ref[...] = raw
    step_all = softplus(raw)
    rate2 = -jnp.exp(heads_ref[:, 1:2]) * LOG2E
    causal = triangle(stretch, lambda r, c: r <= c)
    for part in range(span // stretch):
        lanes = slice(part * stretch, (part + 1) * stretch)
        step = step_all[:, lanes]
        cum, factor, ec, total = decays(step, rate2)
        cum_s[...] = cum
        step_s[...] = step
        factor_s[...] = factor * step
        ec_s[...] = ec
        total_s[...] = jnp.broadcast_to(total, (heads, LANES))
        b_in = active_ref[inner : inner + state_dim, lanes]
        c_in = active_ref[inner + state_dim : inner + 2 * state_dim, lanes]
        scores = jnp.where(causal, mul_tn(b_in, c_in), 0.0)
        low_state = state[...].astype(BF16)
        states_ref[part] = low_state
        carried[...] = mul_nn(low_state, c_in)

        @pl.loop(0, heads // GROUP, unroll=HEADS_ABREAST)
        def _(group):
            eight = pl.ds(pl.multiple_of(group * GROUP, GROUP), GROUP)
            cum_g, step_g, factor_g, ec_g = cum_s[eight, :], step_s[eight, :], factor_s[eight, :], ec_s[eight, :]
            cum_c = as_columns(cum_g)
            for j in range(GROUP):
                rows = pl.ds(pl.multiple_of((group * GROUP + j) * width, width), width)
                row = slice(j, j + 1)
                values = active_ref[rows, lanes].astype(F32)
                stepped = (values * step_g[row]).astype(BF16)
                decay = jnp.exp2(jnp.minimum(cum_g[row] - cum_c[:, row], 0.0))
                weights = (scores * decay).astype(BF16)
                scanned_ref[rows, lanes] = mul_nn(stepped, weights) + ec_g[row] * carried[rows, :]
                scaled[rows, :] = (values * factor_g[row]).astype(BF16)

        update[...] = mul_nt(scaled[...], b_in)

        @pl.loop(0, heads // GROUP, unroll=HEADS_ABREAST)
        def _(group):
            eight = pl.ds(pl.multiple_of(group * GROUP, GROUP), GROUP)
            total_g = total_s[eight, :]
            for j in range(GROUP):
                rows = pl.ds(pl.multiple_of((group * GROUP + j) * width, width), width)
                state[rows, :] = total_g[j : j + 1] * state[rows, :] + update[rows, :]

    @pl.when(pl.program_id(0) == pl.num_programs(0) - 1)
    def _():
        kept.wait()


def gated_body(sizes, lengths, places_ref, skip_ref, alive_ref, cotangent_ref, inner_gain_ref, *refs):
    n_pieces = len(lengths)
    gate, scanned, values_ref = refs[:3]
    pieces, refs = refs[3 : 3 + n_pieces], refs[3 + n_pieces :]
    (
        low_mixed_ref,
        d_gate_ref,
        d_scan_ref,
        row_part_ref,
        skip_part_ref,
        gain_part_ref,
        out_weight_ref,
        out_weight,
        gated,
        d_normed,
        sems,
    ) = refs
    inner, conv, heads, state_dim = sizes
    width = inner // heads
    span = cotangent_ref.shape[0]
    copies = piece_copies(places_ref, lengths, pieces, out_weight, sems)
    kept = pltpu.make_async_copy(out_weight, out_weight_ref, sems.at[n_pieces])

    @pl.when(pl.program_id(0) == 0)
    def _():
        for copy in copies:
            copy.start()
        gain_part_ref[...] = jnp.zeros_like(gain_part_ref)

    def gated_head(h, squares):
        rows = pl.ds(pl.multiple_of(h * width, width), width)
        z = gate[rows, :]
        y = scanned[rows, :] + skip_ref[h] * values_ref[rows, :].astype(F32)
        v = y * (z * sigmoid(z))
        gated[rows, :] = v
        return squares + eighths(v * v)

    squares = lax.fori_loop(0, heads, gated_head, jnp.zeros((8, span), F32), unroll=4)
    scale = lax.rsqrt(jnp.sum(squares, axis=0, keepdims=True) / inner + EPSILON)

    @pl.when(pl.program_id(0) == 0)
    def _():
        for copy in copies:
            copy.wait()
        kept.start()

    incoming = (cotangent_ref[...].astype(F32) * alive_ref[0]).astype(BF16)

    def norm_tile(i, dots):
        rows = pl.ds(pl.multiple_of(i * TILE, TILE), TILE)
        gain = inner_gain_ref[rows, :]
        unit = gated[rows, :] * scale
        low_mixed_ref[rows, :] = (unit * gain).astype(BF16)
        d_mixed = mul_nt(out_weight[rows, :], incoming)
        gain_part_ref[rows, :] += fold(d_mixed * unit)
        d_unit = d_mixed * gain
        d_normed[rows, :] = d_unit
        return dots + eighths(d_unit * unit)

    dots = lax.fori_loop(0, inner // TILE, norm_tile, jnp.zeros((8, span), F32), unroll=3)
    mean_dot = jnp.sum(dots, axis=0, keepdims=True) / inner

    @pl.loop(0, heads // GROUP, unroll=HEADS_ABREAST)
    def _(group):
        eight = pl.ds(pl.multiple_of(group * GROUP, GROUP), GROUP)
        row_parts, skip_parts = [], []
        for j in range(GROUP):
            h = group * GROUP + j
            rows = pl.ds(pl.multiple_of(h * width, width), width)
            z = gate[rows, :]
            sig = sigmoid(z)
            values = values_ref[rows, :].astype(F32)
            pure = scanned[rows, :]
            y = pure + skip_ref[h] * values
            d_gated = scale * (d_normed[rows, :] - gated[rows, :] * (scale * mean_dot))
            d_scan = (d_gated * (z * sig)).astype(BF16)
            d_scan_ref[rows, :] = d_scan
            d_gate_ref[rows, :] = (d_gated * y * (sig * (1.0 + z * (1.0 - sig)))).astype(BF16)
            d_scan = d_scan.astype(F32)
            row_parts.append(jnp.sum(d_scan * pure, axis=0, keepdims=True))
            skip_parts.append(jnp.sum(d_scan * values, axis=0, keepdims=True))
        row_part_ref[eight, :] = jnp.concatenate(row_parts, axis=0)
        skip_part_ref[eight, :] = jnp.concatenate(skip_parts, axis=0)

    @pl.when(pl.program_id(0) == pl.num_programs(0) - 1)
    def _():
        kept.wait()


def backward_body(sizes, first_head, last, *refs):
    refs = list(refs)
    take = lambda n: [refs.pop(0) for _ in range(n)]
    skip_ref, active_ref, low_bc_ref = take(3)
    mixed_refs = take(2 if last else 1)
    before_refs = take(2 if last else 1)
    d_scan_ref, raw_ref, row_part_ref, states_ref, taps_ref, heads_ref = take(6)
    bc_part_ref = take(1)[0] if last else None
    d_rest_refs = take(2 if last else 1)
    d_raw_ref, rate_part_ref, conv_part_ref = take(3)
    bc_out_ref = None if last else take(1)[0]
    (
        d_state,
        extended,
        d_extended,
        d_active,
        sums,
        from_state,
        scaled,
        d_scaled,
        d_scores,
        state_dots,
        cum_s,
        step_s,
        factor_s,
        ec_s,
        total_s,
        pair_s,
        direct_s,
        ending_s,
    ) = refs
    all_inner, conv, all_heads, state_dim = sizes
    inner, span = active_ref.shape
    width = all_inner // all_heads
    heads = inner // width
    tiles = [(ref, before, out, t) for ref, before, out in zip(mixed_refs, before_refs, d_rest_refs) for t in range(ref.shape[1] // LANES)]
    first_tiles = [first_head * width // LANES, all_inner // LANES]
    stretch = min(STRETCH, span)
    first_block = pl.program_id(0) == pl.num_programs(0) - 1

    @pl.when(pl.program_id(0) == 0)
    def _():
        d_state[...] = jnp.zeros_like(d_state)
        d_extended[:, :8, :] = jnp.zeros((len(tiles), 8, LANES), F32)
        sums[...] = jnp.zeros_like(sums)

    raw = raw_ref[...]
    step_all = softplus(raw)
    slope = sigmoid(raw)
    rate = -jnp.exp(heads_ref[first_head : first_head + heads, 1:2])
    rate2 = rate * LOG2E
    causal = triangle(stretch, lambda r, c: r <= c)
    ending = triangle(stretch, lambda r, c: r >= c).astype(BF16)
    before_it = triangle(stretch, lambda r, c: r < c).astype(BF16)
    for part in reversed(range(span // stretch)):
        lanes = slice(part * stretch, (part + 1) * stretch)
        step = step_all[:, lanes]
        cum, factor, ec, total = decays(step, rate2)
        cum_s[...] = cum
        step_s[...] = step
        factor_s[...] = factor
        ec_s[...] = ec
        total_s[...] = jnp.broadcast_to(total, (heads, LANES))
        b_in = low_bc_ref[:state_dim, lanes]
        c_in = low_bc_ref[state_dim:, lanes]
        scores = jnp.where(causal, mul_tn(b_in, c_in), 0.0)
        low_d_state = d_state[...].astype(BF16)
        from_state[...] = mul_nn(low_d_state, b_in)
        d_scores[...] = jnp.zeros_like(d_scores)

        @pl.loop(0, heads // GROUP, unroll=HEADS_ABREAST)
        def _(group):
            eight = pl.ds(pl.multiple_of(group * GROUP, GROUP), GROUP)
            cum_g, step_g, factor_g, ec_g = cum_s[eight, :], step_s[eight, :], factor_s[eight, :], ec_s[eight, :]
            cum_c = as_columns(cum_g)
            pairs, directs, endings, dots = [], [], [], []
            d_scores_g = d_scores[...]
            for j in range(GROUP):
                h = group * GROUP + j
                rows = pl.ds(pl.multiple_of(h * width, width), width)
                row = slice(j, j + 1)
                values = active_ref[rows, lanes].astype(F32)
                stepped = (values * step_g[row]).astype(BF16)
                low_d = d_scan_ref[rows, lanes]
                d_scan = low_d.astype(F32)
                decay = jnp.exp2(jnp.minimum(cum_g[row] - cum_c[:, row], 0.0))
                weights = (scores * decay).astype(BF16)
                inside = mul_nt(low_d, weights)
                d_scores_g = d_scores_g + mul_tn(stepped, low_d) * decay
                across = from_state[rows, :] * factor_g[row]
                both = inside + across
                d_active[rows, lanes] = step_g[row] * both + skip_ref[first_head + h] * d_scan
                pairs.append(jnp.sum(stepped.astype(F32) * inside, axis=0, keepdims=True))
                directs.append(jnp.sum(values * both, axis=0, keepdims=True))
                endings.append(jnp.sum(values * across, axis=0, keepdims=True))
                scaled[rows, :] = (values * (step_g[row] * factor_g[row])).astype(BF16)
                d_scaled[rows, :] = (d_scan * ec_g[row]).astype(BF16)
                dots.append(jnp.sum(d_state[rows, :] * states_ref[part, rows, :].astype(F32), axis=0, keepdims=True))
            d_scores[...] = d_scores_g
            pair_s[eight, :] = jnp.concatenate(pairs, axis=0)
            direct_s[eight, :] = jnp.concatenate(directs, axis=0)
            ending_s[eight, :] = jnp.concatenate(endings, axis=0)
            state_dots[eight, :] = jnp.concatenate(dots, axis=0)

        low_d_scores = jnp.where(causal, d_scores[...], 0.0).astype(BF16)
        low_state = states_ref[part]
        d_b = mul_tn(low_d_state, scaled[...]) + mul_nt(c_in, low_d_scores)
        d_c = mul_tn(low_state, d_scaled[...]) + mul_nn(b_in, low_d_scores)
        if last:
            d_active[inner : inner + state_dim, lanes] = d_b + bc_part_ref[:state_dim, lanes]
            d_active[inner + state_dim :, lanes] = d_c + bc_part_ref[state_dim:, lanes]
        else:
            bc_out_ref[:state_dim, lanes] = d_b
            bc_out_ref[state_dim:, lanes] = d_c
        from_state[...] = mul_nt(d_scaled[...], c_in)

        @pl.loop(0, heads // GROUP, unroll=HEADS_ABREAST)
        def _(group):
            eight = pl.ds(pl.multiple_of(group * GROUP, GROUP), GROUP)
            total_g = total_s[eight, :]
            for j in range(GROUP):
                rows = pl.ds(pl.multiple_of((group * GROUP + j) * width, width), width)
                d_state[rows, :] = total_g[j : j + 1] * d_state[rows, :] + from_state[rows, :]

        d_log = (
            lane_sums(row_part_ref[:, lanes] - pair_s[...], ending)
            + lane_sums(step * ending_s[...], before_it)
            + total * jnp.sum(state_dots[...], axis=1, keepdims=True)
        )
        rate_part_ref[:, lanes] = d_log * step * rate
        d_raw_ref[:, lanes] = (direct_s[...] + d_log * rate) * slope[:, lanes]

    for index, (mixed_ref, before_ref, d_rest_ref, tile) in enumerate(tiles):
        lanes = slice(tile * LANES, (tile + 1) * LANES)
        active_rows = slice(index * LANES, (index + 1) * LANES)
        before = before_ref[:, lanes].astype(F32)[8:]
        extended[index, :8, :] = jnp.where(first_block, 0.0, before)
        extended[index, 8:, :] = mixed_ref[:, lanes].astype(F32)
        taps = taps_ref[first_tiles[0] + index if mixed_ref is mixed_refs[0] else first_tiles[1] + tile]
        moved = [extended[index, 8 - shift : 8 - shift + span, :] for shift in range(4)]
        summed = taps[4:5] + moved[0] * taps[3:4]
        for shift in range(1, 4):
            summed = summed + moved[shift] * taps[3 - shift : 4 - shift]
        sig = sigmoid(summed)
        d_summed = d_active[active_rows, :].T * (sig * (1.0 + summed * (1.0 - sig)))
        d_extended[index, span:, :] = d_extended[index, :8, :]
        d_extended[index, :span, :] = d_summed
        d_block = d_summed * taps[3:4]
        for shift in range(1, 4):
            d_block = d_block + d_extended[index, shift : shift + span, :] * taps[3 - shift : 4 - shift]
        d_rest_ref[:, lanes] = d_block.astype(BF16)
        for shift in range(4):
            sums[3 - shift, index] += eighths(d_summed * moved[shift])
        sums[4, index] += eighths(d_summed)

    @pl.when(first_block)
    def _():
        for k in range(5):
            conv_part_ref[k] = jnp.sum(sums[k], axis=1)


def whole(shape):
    return pl.BlockSpec(shape, lambda c: (0,) * len(shape), pipeline_mode=pl.Buffered(1))


ANYWHERE = pl.BlockSpec(memory_space=pl.ANY)
SCALARS = pl.BlockSpec(memory_space=pltpu.SMEM)


def kernel_options(microseconds):
    return dict(
        compiler_params=pltpu.CompilerParams(
            dimension_semantics=("arbitrary",), vmem_limit_bytes=VMEM_LIMIT
        ),
        cost_estimate=pl.CostEstimate(
            flops=microseconds * 10**9, bytes_accessed=microseconds * 10**6, transcendentals=0
        ),
    )


def forward(sizes, places, tokens, gain, raw_weight, taps, heads_in, pieces, lengths):
    inner, conv, heads, state_dim = sizes
    length, model = tokens.shape
    span = min(SPAN, length)
    stretch = min(STRETCH, span)
    parts = span // stretch
    along = lambda rows: pl.BlockSpec((rows, span), lambda c: (0, c))
    down = lambda columns: pl.BlockSpec((span, columns), lambda c: (c, 0))
    shape = jax.ShapeDtypeStruct
    return pl.pallas_call(
        functools.partial(forward_body, sizes, tuple(lengths)),
        grid=(length // span,),
        in_specs=[
            SCALARS,
            down(model),
            whole(gain.shape),
            whole(raw_weight.shape),
            whole(taps.shape),
            whole(heads_in.shape),
        ]
        + [ANYWHERE] * len(pieces),
        out_specs=[
            down(model),
            down(conv),
            along(conv),
            along(heads),
            pl.BlockSpec((parts, inner, state_dim), lambda c: (c, 0, 0)),
            along(inner),
            along(inner),
            ANYWHERE,
        ],
        out_shape=[
            shape((length, model), BF16),
            shape((length, conv), BF16),
            shape((conv, length), BF16),
            shape((heads, length), F32),
            shape((length // stretch, inner, state_dim), BF16),
            shape((inner, length), F32),
            shape((inner, length), F32),
            shape((inner + conv, model), BF16),
        ],
        scratch_shapes=[
            pltpu.VMEM((inner + conv, model), BF16),
            pltpu.VMEM((inner, state_dim), F32),
            pltpu.VMEM((conv // LANES, span + 8, LANES), F32),
            pltpu.VMEM((inner, stretch), F32),
            pltpu.VMEM((inner, stretch), BF16),
            pltpu.VMEM((inner, state_dim), F32),
            pltpu.VMEM((heads, stretch), F32),
            pltpu.VMEM((heads, stretch), F32),
            pltpu.VMEM((heads, stretch), F32),
            pltpu.VMEM((heads, stretch), F32),
            pltpu.VMEM((heads, LANES), F32),
            pltpu.SemaphoreType.DMA((len(pieces) + 1,)),
        ],
        name="block_forward",
        **kernel_options(30),
    )(places, tokens, gain, raw_weight, taps, heads_in, *pieces)


def gated(sizes, places, skip, alive, cotangent, inner_gain, gate, scanned, active, pieces, lengths):
    inner, conv, heads, state_dim = sizes
    length, model = cotangent.shape
    span = min(SPAN, length)
    along = lambda rows: pl.BlockSpec((rows, span), lambda c: (0, c))
    shape = jax.ShapeDtypeStruct
    return pl.pallas_call(
        functools.partial(gated_body, sizes, tuple(lengths)),
        grid=(length // span,),
        in_specs=[
            SCALARS,
            SCALARS,
            SCALARS,
            pl.BlockSpec((span, model), lambda c: (c, 0)),
            whole(inner_gain.shape),
            along(inner),
            along(inner),
            along(inner),
        ]
        + [ANYWHERE] * len(pieces),
        out_specs=[
            along(inner),
            along(inner),
            along(inner),
            along(heads),
            along(heads),
            pl.BlockSpec((inner, LANES), lambda c: (0, 0)),
            ANYWHERE,
        ],
        out_shape=[
            shape((inner, length), BF16),
            shape((inner, length), BF16),
            shape((inner, length), BF16),
            shape((heads, length), F32),
            shape((heads, length), F32),
            shape((inner, LANES), F32),
            shape((inner, model), BF16),
        ],
        scratch_shapes=[
            pltpu.VMEM((inner, model), BF16),
            pltpu.VMEM((inner, span), F32),
            pltpu.VMEM((inner, span), F32),
            pltpu.SemaphoreType.DMA((len(pieces) + 1,)),
        ],
        name="block_gated",
        **kernel_options(15),
    )(places, skip, alive, cotangent, inner_gain, gate, scanned, active, *pieces)


def backward(sizes, first_head, heads, skip, active, mixed, d_scan, raw, row_part, states, taps, heads_in, bc_part):
    all_inner, conv, all_heads, state_dim = sizes
    width = all_inner // all_heads
    inner = heads * width
    last = first_head + heads == all_heads
    length = active.shape[1]
    span = min(SPAN, length)
    stretch = min(STRETCH, span)
    parts = span // stretch
    blocks = length // span
    per = span // 16
    at = first_head // heads
    bc = conv - all_inner
    bc_at = all_inner // bc
    along = lambda rows, index: pl.BlockSpec((rows, span), lambda c: (index, blocks - 1 - c))
    down = lambda columns, index: pl.BlockSpec((span, columns), lambda c: (blocks - 1 - c, index))
    ahead = lambda columns, index: pl.BlockSpec(
        (16, columns), lambda c: (jnp.maximum((blocks - 1 - c) * per - 1, 0), index)
    )
    shape = jax.ShapeDtypeStruct
    tiles = (inner + (bc if last else 0)) // LANES
    results = pl.pallas_call(
        functools.partial(backward_body, sizes, first_head, last),
        grid=(blocks,),
        in_specs=[SCALARS, along(inner, at), along(bc, bc_at), down(inner, at)]
        + [down(bc, bc_at)] * last
        + [ahead(inner, at)]
        + [ahead(bc, bc_at)] * last
        + [
            along(inner, at),
            along(heads, at),
            along(heads, at),
            pl.BlockSpec((parts, inner, state_dim), lambda c: (blocks - 1 - c, at, 0)),
            whole(taps.shape),
            whole(heads_in.shape),
        ]
        + [along(bc, 0)] * last,
        out_specs=[down(inner, 0)]
        + [down(bc, 0)] * last
        + [along(heads, 0), along(heads, 0), pl.BlockSpec((5, tiles, LANES), lambda c: (0, 0, 0))]
        + [along(bc, 0)] * (not last),
        out_shape=[shape((length, inner), BF16)]
        + [shape((length, bc), BF16)] * last
        + [shape((heads, length), F32), shape((heads, length), F32), shape((5, tiles, LANES), F32)]
        + [shape((bc, length), F32)] * (not last),
        scratch_shapes=[
            pltpu.VMEM((inner, state_dim), F32),
            pltpu.VMEM((tiles, span + 8, LANES), F32),
            pltpu.VMEM((tiles, span + 8, LANES), F32),
            pltpu.VMEM((tiles * LANES, span), F32),
            pltpu.VMEM((5, tiles, 8, LANES), F32),
            pltpu.VMEM((inner, stretch), F32),
            pltpu.VMEM((inner, stretch), BF16),
            pltpu.VMEM((inner, stretch), BF16),
            pltpu.VMEM((stretch, stretch), F32),
            pltpu.VMEM((heads, state_dim), F32),
            pltpu.VMEM((heads, stretch), F32),
            pltpu.VMEM((heads, stretch), F32),
            pltpu.VMEM((heads, stretch), F32),
            pltpu.VMEM((heads, stretch), F32),
            pltpu.VMEM((heads, LANES), F32),
            pltpu.VMEM((heads, stretch), F32),
            pltpu.VMEM((heads, stretch), F32),
            pltpu.VMEM((heads, stretch), F32),
        ],
        name="block_backward",
        **kernel_options(4 + heads),
    )(
        skip,
        active,
        active,
        *[mixed] * (2 + 2 * last),
        d_scan,
        raw,
        row_part,
        states,
        taps,
        heads_in,
        *([bc_part] * last),
    )
    return results


def powers_of_two(size):
    bits, bit = [], 1
    while bit < size:
        bits.append(bit)
        bit *= 2
    return bits if bit == size else None


def swap(block, axis, bit):
    pairs = [(k, k ^ bit) for k in range(lax.axis_size(axis))]
    return lax.ppermute(block, axis, pairs)


def cut(block, index, pieces, axis=0):
    size = block.shape[axis] // pieces
    return lax.dynamic_slice_in_dim(block, index * size, size, axis)


def halve(block, axis, bit):
    side = (lax.axis_index(axis) // bit) % 2
    got = swap(cut(block, 1 - side, 2), axis, bit)
    return (cut(block, side, 2).astype(F32) + got.astype(F32)).astype(block.dtype)


def double(block, axis, bit):
    side = (lax.axis_index(axis) // bit) % 2
    other = swap(block, axis, bit)
    return jnp.where(
        side == 0, jnp.concatenate([block, other], axis=0), jnp.concatenate([other, block], axis=0)
    )


def pair_sum(product, core):
    return added(product(core), swap(product(1 - core).astype(BF16), "dp", 1))


def after(value, *earlier):
    return lax.optimization_barrier((value, *earlier))[0]


def added(keep, got):
    return (keep.astype(F32) + got.astype(F32)).astype(BF16)


def together(*arrays):
    return lax.optimization_barrier(arrays)


def sides(block, axis, bit):
    side = (lax.axis_index(axis) // bit) % 2
    return cut(block, side, 2), cut(block, 1 - side, 2)


def joined(block, other, side, axis=0):
    return jnp.where(
        side == 0, jnp.concatenate([block, other], axis), jnp.concatenate([other, block], axis)
    )


def pair_sum(product, core):
    return added(product(core), swap(product(1 - core).astype(BF16), "dp", 1))


def after(value, *earlier):
    return lax.optimization_barrier((value, *earlier))[0]


def added(keep, got):
    return (keep.astype(F32) + got.astype(F32)).astype(BF16)


class Chain:
    def __init__(self, keep, give, axis, bit):
        self.keep, self.give, self.axis, self.bit = keep, give, axis, bit

    def start(self):
        self.got = swap(self.give, self.axis, self.bit)
        return self.give

    def finish(self, *beside):
        return added(self.keep, after(self.got, *beside) if beside else self.got)


def halving(block, axis, bit):
    side = (lax.axis_index(axis) // bit) % 2
    return Chain(cut(block, side, 2), cut(block, 1 - side, 2), axis, bit)


def spread(block, bits):
    for bit in reversed(bits):
        block = double(block, "dp", bit)
    return block


class Plain:
    def __init__(self):
        self.groups = lax.axis_size("fsdp")
        self.mine = lax.axis_index("fsdp")

    def gather(self, w_in, packed, w_out, main, prepare):
        by_group = lax.all_gather(w_in.T, "fsdp")
        weight = by_group.transpose(1, 0, 2).reshape(by_group.shape[1], -1)
        out_weight = lax.all_gather(w_out, "fsdp", tiled=True)
        here = jnp.zeros((2,), jnp.int32)
        sizes = [main], [out_weight.shape[0]]
        return (
            ([weight], here, sizes[0]),
            weight[main:],
            prepare(lax.all_gather(packed, "fsdp")),
            ([out_weight], here, sizes[1]),
        )

    def late(self, pieces, places, lengths, earlier):
        return pieces, places, lengths

    def own(self, total, axis):
        return cut(total, self.mine, self.groups, axis).astype(F32)

    def sums(self, low_mixed, incoming, d_gate, normed, kernels):
        everywhere = lambda term, axis: self.own(lax.psum(term.astype(BF16), ("fsdp", "dp")), axis)
        g_out = everywhere(mul_nn(low_mixed, incoming), 0)
        g_rows, results = [everywhere(mul_nn(d_gate, normed), 1)], []
        for kernel in kernels:
            results.append(kernel(results))
            g_rows += [everywhere(mul_tn(rest, normed), 1) for rest in results[-1][0]]
        return g_out, g_rows, results, d_gate, d_gate

    def sum_small(self, by_owner):
        return cut(lax.psum(by_owner, ("fsdp", "dp")), self.mine, self.groups)[0]


class Paired:
    def __init__(self):
        self.mine = lax.axis_index("fsdp")
        self.core = lax.axis_index("dp") % 2
        self.bits = powers_of_two(lax.axis_size("dp"))

    def gather(self, w_in, packed, w_out, main, prepare):
        mine, core = self.mine, self.core
        rows = w_in.T
        columns = rows.shape[1]
        last = jnp.pad(rows[main:], ((0, 32 - (rows.shape[0] - main)), (0, 0)))
        half = main // 2
        outer = half // 48 * 16
        middle = half - 2 * outer
        near = self.bits[1]
        side = (lax.axis_index("dp") // near) % 2
        first_row = core * half
        row = lambda where: first_row + jnp.where(side == where, 0, outer + middle)
        part = lambda start, count: lax.dynamic_slice_in_dim(rows, start, count, 0)
        other_packed = swap(packed, "fsdp", 1)
        mine_outer = swap(jnp.concatenate([part(row(0), outer), last], axis=0), "fsdp", 1)
        mine_middle = swap(after(part(first_row + outer, middle), mine_outer), "fsdp", 1)
        near_outer = swap(mine_outer, "dp", near)
        in_order = lambda a, b, axis: jnp.where(
            mine == 0, jnp.concatenate([a, b], axis), jnp.concatenate([b, a], axis)
        )
        raw_weight = in_order(last, mine_outer[outer:], 1)
        prepared = prepare(in_order(packed[None], other_packed[None], 0))
        raw_weight, *prepared = together(raw_weight, *prepared, mine_middle)[:-1]
        core_outer = swap(after(mine_outer, near_outer, mine_middle, raw_weight, *prepared), "dp", 1)
        core_middle = swap(mine_middle, "dp", 1)
        core_near = swap(near_outer, "dp", 1)
        there = (1 - mine) * columns
        across = half - 2 * first_row
        places = [0, mine * columns]
        for start in (row(0), first_row + outer, row(1)):
            places += [start, there, start + across, there]
        places = jnp.stack(places).astype(jnp.int32)
        pieces = [rows, mine_outer, core_outer, mine_middle, core_middle, near_outer, core_near]
        lengths = [main, outer, outer, middle, middle, outer, outer]
        relayed = core_near

        each = w_out.shape[0]
        direct_out = swap(after(cut(w_out, core, 2), relayed), "fsdp", 1)
        other = (1 - mine) * each
        places_out = jnp.stack(
            [mine * each, 0, other + core * (each // 2), 0, other + (1 - core) * (each // 2), 0]
        ).astype(jnp.int32)
        return (
            (pieces, places, lengths),
            raw_weight,
            prepared,
            ([w_out, direct_out], places_out, [each, each // 2, each // 2]),
        )

    def late(self, pieces, places, lengths, earlier):
        own, direct = pieces
        direct = after(direct, earlier)
        return [own, direct, swap(direct, "dp", 1)], places, lengths

    def sums(self, low_mixed, incoming, d_gate, normed, kernels):
        mine, core, (near, *far) = self.mine, self.core, self.bits[1:]
        near_side = (lax.axis_index("dp") // near) % 2
        owned = lambda block: (cut(block, mine, 2, 1), cut(block, 1 - mine, 2, 1))
        across = lambda give: swap(give, "fsdp", 1)
        over = lambda give, bit: swap(give, "dp", bit)

        out_block = pair_sum(lambda c: mul_nn(low_mixed, cut(incoming, c, 2, 1)), core)
        gate_block = pair_sum(lambda c: mul_nn(cut(d_gate, c, 2), normed), core)
        gate_keep, gate_give = owned(gate_block)
        keep_a = jnp.concatenate([cut(out_block, mine, 2), gate_keep], axis=0)
        give_a = jnp.concatenate([cut(out_block, 1 - mine, 2), gate_give], axis=0)
        got_a = across(give_a)
        first = kernels[0]([], give_a)
        got_a, _ = together(got_a, first[0][0])
        keep_a, give_a = sides(added(keep_a, got_a), "dp", near)
        got_a = over(give_a, near)
        second = kernels[1]([first], give_a)
        got_a, *last_rests = together(got_a, *second[0])
        rests = [*first[0], *last_rests]

        product = lambda c: jnp.concatenate([mul_tn(cut(left, c, 2, 1), normed) for left in rests], axis=0)
        block_b = pair_sum(product, core)
        keep_b, give_b = owned(block_b)
        got_b = across(give_b)
        mark = give_b
        block_a = added(keep_a, after(got_a, give_b))
        keep_a, give_a = sides(block_a, "dp", far[0])
        got_a = over(give_a, far[0])
        block_a = added(keep_a, got_a)
        for bit in far[1:]:
            keep_a, give_a = sides(block_a, "dp", bit)
            block_a = added(keep_a, over(give_a, bit))
        block_a, got_b = together(block_a, got_b)
        block_b = added(keep_b, got_b)
        left_a = [*reversed(far), near]
        steps = [("halve", bit) for bit in (near, *far)] + [("double", bit) for bit in reversed(far)]
        for kind, bit in steps:
            side = (lax.axis_index("dp") // bit) % 2
            if kind == "halve":
                keep_b, give_b = sides(block_b, "dp", bit)
                sent = [over(give_b, bit)]
            else:
                sent = [over(block_b, bit)]
            if left_a:
                sent.append(over(block_a, left_a[0]))
            sent = list(together(*sent))
            got_b = sent.pop(0)
            block_b = added(keep_b, got_b) if kind == "halve" else joined(block_b, got_b, side)
            if left_a:
                block_a = joined(block_a, sent.pop(0), (lax.axis_index("dp") // left_a.pop(0)) % 2)
        block_b = joined(block_b, over(block_b, near), near_side)
        size = out_block.shape[0] // 2
        swapped_a, swapped_b = swap(block_a, "dp", 1), swap(block_b, "dp", 1)
        g_out = joined(block_a[:size], swapped_a[:size], core, 1).astype(F32)
        g_rows, first_row = [joined(block_a[size:], swapped_a[size:], core)], 0
        for left in rests:
            part = slice(first_row, first_row + left.shape[1] // 2)
            g_rows.append(joined(block_b[part], swapped_b[part], core))
            first_row = part.stop
        return g_out, [rows.astype(F32) for rows in g_rows], [first, second], mark, got_b

    def sum_small(self, by_owner):
        for bit in self.bits:
            by_owner = by_owner + swap(by_owner, "dp", bit)
        return cut(by_owner, self.mine, 2)[0] + swap(cut(by_owner, 1 - self.mine, 2)[0], "fsdp", 1)


def shards(
    tokens,
    live,
    norm_gain,
    w_in,
    conv_weight,
    conv_bias,
    dt_bias,
    a_log,
    d_skip,
    inner_gain,
    w_out,
    cotangent,
):
    groups, copies = lax.axis_size("fsdp"), lax.axis_size("dp")
    taps = conv_weight.shape[1]
    heads = dt_bias.shape[0] * groups
    inner, conv = inner_gain.shape[0] * groups, conv_bias.shape[0] * groups
    model = tokens.shape[-1]
    proj = w_in.shape[1]
    main = inner + conv
    sizes = (inner, conv, heads, (conv - inner) // 2)
    paired = groups == 2 and powers_of_two(copies) and copies > 2 and main % 32 == 0
    links = Paired() if paired else Plain()

    rest = jnp.concatenate([norm_gain, dt_bias, a_log, d_skip])
    line = max(conv_bias.shape[0], inner_gain.shape[0], rest.shape[0])
    lined = lambda table: jnp.pad(table, ((0, 0), (0, line - table.shape[1])))
    packed = jnp.concatenate([lined(conv_weight.T), lined(conv_bias[None]), lined(inner_gain[None]), lined(rest[None])])

    def prepare(packed):
        packed = packed.astype(F32)
        pick = lambda row, first, each: packed[:, row, first : first + each].reshape(-1)
        model_each, heads_each = norm_gain.shape[0], dt_bias.shape[0]
        table = packed[:, : taps + 1, : conv // groups].transpose(1, 0, 2).reshape(taps + 1, conv)
        table = jnp.concatenate([table, jnp.zeros((7 - taps, conv), F32)], axis=0)
        taps_in = table.reshape(8, conv // LANES, LANES).transpose(1, 0, 2)
        inner_all = pick(taps + 1, 0, inner // groups)[:, None]
        gain_all = pick(taps + 2, 0, model_each)[None]
        by_head = [pick(taps + 2, model_each + k * heads_each, heads_each) for k in range(3)]
        return [taps_in, inner_all, gain_all, jnp.stack(by_head[:2], axis=1), by_head[2]]

    in_pieces, raw_weight, prepared, out_pieces = links.gather(w_in, packed, w_out, main, prepare)
    raw_weight = jnp.pad(raw_weight, ((0, 32 - raw_weight.shape[0]), (0, 0)))
    taps_in, inner_all, gain_all, heads_in, skip = prepared

    alive = live.astype(F32).reshape(1)
    low_tokens, low_cotangent = tokens[0, 0], cotangent[0, 0]
    normed, mixed, active, raw, states, gate, scanned, weight = forward(
        sizes, in_pieces[1], low_tokens, gain_all, raw_weight, taps_in, heads_in, in_pieces[0], in_pieces[2]
    )
    out_pieces = links.late(*out_pieces, normed)
    low_mixed, d_gate, d_scan, row_part, skip_part, gain_part, out_weight = gated(
        sizes, out_pieces[1], skip, alive, low_cotangent, inner_all, gate, scanned, active, out_pieces[0], out_pieces[2]
    )
    u = low_tokens.astype(F32)
    incoming = low_cotangent.astype(F32) * alive[0]

    def backward_step(first, count):
        def step(earlier, *sent):
            scan = after(d_scan, *sent) if sent else d_scan
            bc_part = earlier[-1][-1] if earlier else None
            results = backward(
                sizes, first, count, skip, active, mixed, scan, raw, row_part, states, taps_in, heads_in, bc_part
            )
            if first + count < heads:
                return [results[:1], *results[1:]]
            return [results[:2], *results[2:]]

        return step

    kernels = [backward_step(first, count) for first, count in HEAD_RANGES]
    g_out, g_rows, results, mark, later_mark = links.sums(low_mixed, incoming.astype(BF16), d_gate, normed, kernels)
    d_rest = [rest for result in results for rest in result[0]]
    d_raw, rate_part, conv_part = [[result[k] for result in results] for k in range(1, 4)]
    count = len(d_rest)
    d_gate, *others = together(d_gate, *d_rest, *d_raw, *rate_part, *conv_part, mark)[:-1]
    d_rest, others = others[:count], others[count:]
    d_raw, rate_part, conv_part = [
        jnp.concatenate(others[k * len(results) : (k + 1) * len(results)], axis=k // 2) for k in range(3)
    ]
    conv_part = conv_part.reshape(taps + 1, conv)
    low_d_raw = d_raw.astype(BF16)
    low_mixed = after(low_mixed, later_mark)

    d_normed = mul_tn(d_gate, weight[:inner]) + mul_tn(low_d_raw, raw_weight[:heads])
    first = inner
    for rest in d_rest:
        d_normed = d_normed + mul_nn(rest, weight[first : first + rest.shape[1]])
        first += rest.shape[1]
    scale = lax.rsqrt(jnp.mean(u * u, axis=1, keepdims=True) + EPSILON)
    unit = u * scale
    d_unit = d_normed * gain_all
    input_grad = incoming + scale * (d_unit - unit * jnp.mean(d_unit * unit, axis=1, keepdims=True))

    block_out = (alive[0] * (u + mul_tn(low_mixed, out_weight))).astype(BF16)

    terms = [
        mul_nn(low_d_raw, normed),
        conv_part,
        jnp.sum(gain_part, axis=1)[None],
        jnp.sum(d_normed * unit, axis=0)[None],
        jnp.sum(d_raw, axis=1)[None],
        jnp.sum(rate_part, axis=1)[None],
        jnp.sum(skip_part, axis=1)[None],
    ]
    by_owner = [
        jnp.moveaxis(term.reshape(term.shape[0], groups, -1), 1, 0).reshape(groups, -1) for term in terms
    ]
    count = sum(term.shape[1] for term in by_owner)
    by_owner.append(jnp.zeros((groups, -count % (8 * LANES)), F32))
    total = links.sum_small(jnp.concatenate(by_owner, axis=1).reshape(groups, -1, LANES)).reshape(-1)
    first, g_small = 0, []
    for term in terms:
        size = term.size // groups
        g_small.append(total[first : first + size].reshape(term.shape[0], -1))
        first += size
    g_raw, g_conv, g_inner, g_gain, g_bias, g_rate, g_skip = g_small
    g_proj = jnp.concatenate(g_rows + [g_raw], axis=0).T
    return (
        block_out.reshape(tokens.shape),
        input_grad.reshape(cotangent.shape),
        g_gain[0],
        g_proj,
        g_conv[:taps].T,
        g_conv[taps],
        g_bias[0],
        g_rate[0],
        g_skip[0],
        g_inner[0],
        g_out,
    )


def solution(mesh):
    by_device = P("fsdp", "dp", None, None)
    lines, tables = P("fsdp"), P("fsdp", None)
    return jax.shard_map(
        shards,
        mesh=mesh,
        in_specs=(
            by_device,
            P("fsdp", "dp"),
            lines,
            tables,
            tables,
            lines,
            lines,
            lines,
            lines,
            lines,
            tables,
            by_device,
        ),
        out_specs=(by_device, by_device, lines, tables, tables, lines, lines, lines, lines, lines, tables),
        check_vma=False,
    )
```

```python
import functools
import math

import jax
import jax.numpy as jnp
from jax import lax
from jax.experimental import pallas as pl
from jax.experimental.pallas import tpu as pltpu
from jax.sharding import PartitionSpec as P

EPSILON = 1e-05
LOG2E = math.log2(math.e)
SPAN = 256
STRETCH = 128
GROUP = 8
TILE = 256
LANES = 128
SPARE = 256
TILES_ABREAST = 7
HEADS_ABREAST = 2
HEAD_RANGES = ((0, 16), (16, 8))
VMEM_LIMIT = 60 * 1024 * 1024

F32 = jnp.float32
BF16 = jnp.bfloat16


def mul_nn(a, b):
    return lax.dot_general(a, b, (((1,), (0,)), ((), ())), preferred_element_type=F32)


def mul_nt(a, b):
    return lax.dot_general(a, b, (((1,), (1,)), ((), ())), preferred_element_type=F32)


def mul_tn(a, b):
    return lax.dot_general(a, b, (((0,), (0,)), ((), ())), preferred_element_type=F32)


def triangle(size, keep):
    rows = lax.broadcasted_iota(jnp.int32, (size, size), 0)
    cols = lax.broadcasted_iota(jnp.int32, (size, size), 1)
    return keep(rows, cols)


def lane_sums(values, matrix):
    high = values.astype(BF16)
    rest = values - high.astype(F32)
    middle = rest.astype(BF16)
    low = (rest - middle.astype(F32)).astype(BF16)
    return mul_nn(high, matrix) + mul_nn(middle, matrix) + mul_nn(low, matrix)


def as_columns(rows):
    heads, span = rows.shape
    return jnp.concatenate([rows, jnp.zeros((LANES - heads, span), F32)], axis=0).T


def fold(block):
    total = block[:, :LANES]
    for first in range(LANES, block.shape[1], LANES):
        total = total + block[:, first : first + LANES]
    return total


def eighths(block):
    return block.reshape(block.shape[0] // 8, 8, block.shape[1]).sum(axis=0)


def softplus(v):
    return jnp.maximum(v, 0.0) + jnp.log1p(jnp.exp(-jnp.abs(v)))


def sigmoid(v):
    return 0.5 * jnp.tanh(0.5 * v) + 0.5


def decays(step, rate2):
    span = step.shape[1]
    upper = triangle(span, lambda r, c: r <= c).astype(BF16)
    cum = lane_sums(step * rate2, upper)
    total = cum[:, span - 1 : span]
    return cum, jnp.exp2(total - cum), jnp.exp2(cum), jnp.exp2(total)


def piece_copies(places_ref, lengths, pieces, whole_ref, sems):
    copies = []
    for k, piece in enumerate(pieces):
        rows, columns = lengths[k], piece.shape[1]
        target = whole_ref.at[
            pl.ds(pl.multiple_of(places_ref[2 * k], 16), rows),
            pl.ds(pl.multiple_of(places_ref[2 * k + 1], LANES), columns),
        ]
        copies.append(pltpu.make_async_copy(piece.at[pl.ds(0, rows), :], target, sems.at[k]))
    return copies


def forward_body(sizes, lengths, places_ref, tokens_ref, gain_ref, raw_weight_ref, taps_ref, heads_ref, *refs):
    n_pieces = len(lengths)
    pieces, refs = refs[:n_pieces], refs[n_pieces:]
    (
        normed_ref,
        mixed_ref,
        active_ref,
        raw_ref,
        states_ref,
        gate_ref,
        scanned_ref,
        weight_ref,
        weight,
        state,
        extended,
        carried,
        scaled,
        update,
        cum_s,
        step_s,
        factor_s,
        ec_s,
        total_s,
        sems,
    ) = refs
    inner, conv, heads, state_dim = sizes
    width = inner // heads
    span = tokens_ref.shape[0]
    stretch = min(STRETCH, span)
    copies = piece_copies(places_ref, lengths, pieces, weight, sems)
    kept = pltpu.make_async_copy(weight, weight_ref, sems.at[n_pieces])

    @pl.when(pl.program_id(0) == 0)
    def _():
        for copy in copies:
            copy.start()
        state[...] = jnp.zeros_like(state)
        extended[:, span:, :] = jnp.zeros((conv // LANES, 8, LANES), F32)

    u = tokens_ref[...].astype(F32)
    normed = u * lax.rsqrt(jnp.mean(u * u, axis=1, keepdims=True) + EPSILON) * gain_ref[...]
    normed = normed.astype(BF16)
    normed_ref[...] = normed

    @pl.when(pl.program_id(0) == 0)
    def _():
        for copy in copies:
            copy.wait()
        steps = raw_weight_ref.shape[0]
        weight[inner + conv : inner + conv + steps, :] = raw_weight_ref[...]
        weight[inner + conv + steps :, :] = jnp.zeros((SPARE - steps, weight.shape[1]), BF16)
        kept.start()

    @pl.loop(0, inner // TILE, unroll=3)
    def _(i):
        rows = pl.ds(pl.multiple_of(i * TILE, TILE), TILE)
        gate_ref[rows, :] = mul_nt(weight[rows, :], normed)

    @pl.loop(0, conv // TILE, unroll=TILES_ABREAST)
    def _(i):
        first = pl.multiple_of(i * TILE, TILE)
        wide = mul_nt(normed, weight[pl.ds(pl.multiple_of(inner + first, TILE), TILE), :])
        for k in range(TILE // LANES):
            index = i * (TILE // LANES) + k
            block = wide[:, k * LANES : (k + 1) * LANES]
            extended[index, :8, :] = extended[index, span:, :]
            extended[index, 8:, :] = block
            taps = taps_ref[index]
            summed = taps[4:5] + block * taps[3:4]
            for shift in range(1, 4):
                summed = summed + extended[index, 8 - shift : 8 - shift + span, :] * taps[3 - shift : 4 - shift]
            lanes = pl.ds(pl.multiple_of(first + k * LANES, LANES), LANES)
            mixed_ref[:, lanes] = block.astype(BF16)
            active_ref[lanes, :] = (summed * sigmoid(summed)).T.astype(BF16)

    raw = mul_nt(raw_weight_ref[...], normed)[:heads] + heads_ref[:, 0:1]
    raw_ref[...] = raw
    step_all = softplus(raw)
    rate2 = -jnp.exp(heads_ref[:, 1:2]) * LOG2E
    causal = triangle(stretch, lambda r, c: r <= c)
    for part in range(span // stretch):
        lanes = slice(part * stretch, (part + 1) * stretch)
        step = step_all[:, lanes]
        cum, factor, ec, total = decays(step, rate2)
        cum_s[...] = cum
        step_s[...] = step
        factor_s[...] = factor * step
        ec_s[...] = ec
        total_s[...] = jnp.broadcast_to(total, (heads, LANES))
        b_in = active_ref[inner : inner + state_dim, lanes]
        c_in = active_ref[inner + state_dim : inner + 2 * state_dim, lanes]
        scores = jnp.where(causal, mul_tn(b_in, c_in), 0.0)
        low_state = state[...].astype(BF16)
        states_ref[part] = low_state
        carried[...] = mul_nn(low_state, c_in)

        @pl.loop(0, heads // GROUP, unroll=HEADS_ABREAST)
        def _(group):
            eight = pl.ds(pl.multiple_of(group * GROUP, GROUP), GROUP)
            cum_g, step_g, factor_g, ec_g = cum_s[eight, :], step_s[eight, :], factor_s[eight, :], ec_s[eight, :]
            cum_c = as_columns(cum_g)
            for j in range(GROUP):
                rows = pl.ds(pl.multiple_of((group * GROUP + j) * width, width), width)
                row = slice(j, j + 1)
                values = active_ref[rows, lanes].astype(F32)
                stepped = (values * step_g[row]).astype(BF16)
                decay = jnp.exp2(jnp.minimum(cum_g[row] - cum_c[:, row], 0.0))
                weights = (scores * decay).astype(BF16)
                scanned_ref[rows, lanes] = mul_nn(stepped, weights) + ec_g[row] * carried[rows, :]
                scaled[rows, :] = (values * factor_g[row]).astype(BF16)

        update[...] = mul_nt(scaled[...], b_in)

        @pl.loop(0, heads // GROUP, unroll=HEADS_ABREAST)
        def _(group):
            eight = pl.ds(pl.multiple_of(group * GROUP, GROUP), GROUP)
            total_g = total_s[eight, :]
            for j in range(GROUP):
                rows = pl.ds(pl.multiple_of((group * GROUP + j) * width, width), width)
                state[rows, :] = total_g[j : j + 1] * state[rows, :] + update[rows, :]

    @pl.when(pl.program_id(0) == pl.num_programs(0) - 1)
    def _():
        kept.wait()


def gated_body(sizes, lengths, places_ref, skip_ref, alive_ref, cotangent_ref, inner_gain_ref, *refs):
    n_pieces = len(lengths)
    gate, scanned, values_ref = refs[:3]
    pieces, refs = refs[3 : 3 + n_pieces], refs[3 + n_pieces :]
    (
        low_mixed_ref,
        d_gate_ref,
        d_scan_ref,
        row_part_ref,
        skip_part_ref,
        gain_part_ref,
        out_weight_ref,
        out_weight,
        gated,
        d_normed,
        sems,
    ) = refs
    inner, conv, heads, state_dim = sizes
    width = inner // heads
    span = cotangent_ref.shape[0]
    copies = piece_copies(places_ref, lengths, pieces, out_weight, sems)
    kept = pltpu.make_async_copy(out_weight, out_weight_ref, sems.at[n_pieces])

    @pl.when(pl.program_id(0) == 0)
    def _():
        for copy in copies:
            copy.start()
        gain_part_ref[...] = jnp.zeros_like(gain_part_ref)

    def gated_head(h, squares):
        rows = pl.ds(pl.multiple_of(h * width, width), width)
        z = gate[rows, :]
        y = scanned[rows, :] + skip_ref[h] * values_ref[rows, :].astype(F32)
        v = y * (z * sigmoid(z))
        gated[rows, :] = v
        return squares + eighths(v * v)

    squares = lax.fori_loop(0, heads, gated_head, jnp.zeros((8, span), F32), unroll=4)
    scale = lax.rsqrt(jnp.sum(squares, axis=0, keepdims=True) / inner + EPSILON)

    @pl.when(pl.program_id(0) == 0)
    def _():
        for copy in copies:
            copy.wait()
        kept.start()

    incoming = (cotangent_ref[...].astype(F32) * alive_ref[0]).astype(BF16)

    def norm_tile(i, dots):
        rows = pl.ds(pl.multiple_of(i * TILE, TILE), TILE)
        gain = inner_gain_ref[rows, :]
        unit = gated[rows, :] * scale
        low_mixed_ref[rows, :] = (unit * gain).astype(BF16)
        d_mixed = mul_nt(out_weight[rows, :], incoming)
        gain_part_ref[rows, :] += fold(d_mixed * unit)
        d_unit = d_mixed * gain
        d_normed[rows, :] = d_unit
        return dots + eighths(d_unit * unit)

    dots = lax.fori_loop(0, inner // TILE, norm_tile, jnp.zeros((8, span), F32), unroll=3)
    mean_dot = jnp.sum(dots, axis=0, keepdims=True) / inner

    @pl.loop(0, heads // GROUP, unroll=HEADS_ABREAST)
    def _(group):
        eight = pl.ds(pl.multiple_of(group * GROUP, GROUP), GROUP)
        row_parts, skip_parts, d_gates = [], [], []
        for j in range(GROUP):
            h = group * GROUP + j
            rows = pl.ds(pl.multiple_of(h * width, width), width)
            z = gate[rows, :]
            sig = sigmoid(z)
            values = values_ref[rows, :].astype(F32)
            pure = scanned[rows, :]
            y = pure + skip_ref[h] * values
            d_gated = scale * (d_normed[rows, :] - gated[rows, :] * (scale * mean_dot))
            d_scan = (d_gated * (z * sig)).astype(BF16)
            d_scan_ref[rows, :] = d_scan
            d_gates.append(d_gated * y * (sig * (1.0 + z * (1.0 - sig))))
            if len(d_gates) * width == LANES:
                lanes = pl.ds(pl.multiple_of((h + 1) * width - LANES, LANES), LANES)
                d_gate_ref[:, lanes] = jnp.concatenate(d_gates, axis=0).T.astype(BF16)
                d_gates = []
            d_scan = d_scan.astype(F32)
            row_parts.append(jnp.sum(d_scan * pure, axis=0, keepdims=True))
            skip_parts.append(jnp.sum(d_scan * values, axis=0, keepdims=True))
        row_part_ref[eight, :] = jnp.concatenate(row_parts, axis=0)
        skip_part_ref[eight, :] = jnp.concatenate(skip_parts, axis=0)

    @pl.when(pl.program_id(0) == pl.num_programs(0) - 1)
    def _():
        kept.wait()


def backward_body(sizes, first_head, last, *refs):
    refs = list(refs)
    take = lambda n: [refs.pop(0) for _ in range(n)]
    skip_ref, active_ref, low_bc_ref = take(3)
    mixed_refs = take(2 if last else 1)
    before_refs = take(2 if last else 1)
    d_scan_ref, raw_ref, row_part_ref, states_ref, taps_ref, heads_ref = take(6)
    bc_part_ref, d_raw_before_ref, _ = take(3) if last else (None, None, None)
    d_rest_ref = take(1)[0]
    d_raw_ref, rate_part_ref, conv_part_ref = take(3)
    bc_out_ref = None if last else take(1)[0]
    (
        d_state,
        extended,
        d_extended,
        d_active,
        sums,
        from_state,
        scaled,
        d_scaled,
        d_scores,
        state_dots,
        cum_s,
        step_s,
        factor_s,
        ec_s,
        total_s,
        pair_s,
        direct_s,
        ending_s,
    ) = refs
    all_inner, conv, all_heads, state_dim = sizes
    inner, span = active_ref.shape
    width = all_inner // all_heads
    heads = inner // width
    tiles = [(ref, before, t) for ref, before in zip(mixed_refs, before_refs) for t in range(ref.shape[1] // LANES)]
    first_tiles = [first_head * width // LANES, all_inner // LANES]
    stretch = min(STRETCH, span)
    first_block = pl.program_id(0) == pl.num_programs(0) - 1

    @pl.when(pl.program_id(0) == 0)
    def _():
        d_state[...] = jnp.zeros_like(d_state)
        d_extended[:, :8, :] = jnp.zeros((len(tiles), 8, LANES), F32)
        sums[...] = jnp.zeros_like(sums)

    raw = raw_ref[...]
    step_all = softplus(raw)
    slope = sigmoid(raw)
    rate = -jnp.exp(heads_ref[first_head : first_head + heads, 1:2])
    rate2 = rate * LOG2E
    causal = triangle(stretch, lambda r, c: r <= c)
    ending = triangle(stretch, lambda r, c: r >= c).astype(BF16)
    before_it = triangle(stretch, lambda r, c: r < c).astype(BF16)
    for part in reversed(range(span // stretch)):
        lanes = slice(part * stretch, (part + 1) * stretch)
        step = step_all[:, lanes]
        cum, factor, ec, total = decays(step, rate2)
        cum_s[...] = cum
        step_s[...] = step
        factor_s[...] = factor
        ec_s[...] = ec
        total_s[...] = jnp.broadcast_to(total, (heads, LANES))
        b_in = low_bc_ref[:state_dim, lanes]
        c_in = low_bc_ref[state_dim:, lanes]
        scores = jnp.where(causal, mul_tn(b_in, c_in), 0.0)
        low_d_state = d_state[...].astype(BF16)
        from_state[...] = mul_nn(low_d_state, b_in)
        d_scores[...] = jnp.zeros_like(d_scores)

        @pl.loop(0, heads // GROUP, unroll=HEADS_ABREAST)
        def _(group):
            eight = pl.ds(pl.multiple_of(group * GROUP, GROUP), GROUP)
            cum_g, step_g, factor_g, ec_g = cum_s[eight, :], step_s[eight, :], factor_s[eight, :], ec_s[eight, :]
            cum_c = as_columns(cum_g)
            pairs, directs, endings, dots = [], [], [], []
            d_scores_g = d_scores[...]
            for j in range(GROUP):
                h = group * GROUP + j
                rows = pl.ds(pl.multiple_of(h * width, width), width)
                row = slice(j, j + 1)
                values = active_ref[rows, lanes].astype(F32)
                stepped = (values * step_g[row]).astype(BF16)
                low_d = d_scan_ref[rows, lanes]
                d_scan = low_d.astype(F32)
                decay = jnp.exp2(jnp.minimum(cum_g[row] - cum_c[:, row], 0.0))
                weights = (scores * decay).astype(BF16)
                inside = mul_nt(low_d, weights)
                d_scores_g = d_scores_g + mul_tn(stepped, low_d) * decay
                across = from_state[rows, :] * factor_g[row]
                both = inside + across
                d_active[rows, lanes] = step_g[row] * both + skip_ref[first_head + h] * d_scan
                pairs.append(jnp.sum(stepped.astype(F32) * inside, axis=0, keepdims=True))
                directs.append(jnp.sum(values * both, axis=0, keepdims=True))
                endings.append(jnp.sum(values * across, axis=0, keepdims=True))
                scaled[rows, :] = (values * (step_g[row] * factor_g[row])).astype(BF16)
                d_scaled[rows, :] = (d_scan * ec_g[row]).astype(BF16)
                dots.append(jnp.sum(d_state[rows, :] * states_ref[part, rows, :].astype(F32), axis=0, keepdims=True))
            d_scores[...] = d_scores_g
            pair_s[eight, :] = jnp.concatenate(pairs, axis=0)
            direct_s[eight, :] = jnp.concatenate(directs, axis=0)
            ending_s[eight, :] = jnp.concatenate(endings, axis=0)
            state_dots[eight, :] = jnp.concatenate(dots, axis=0)

        low_d_scores = jnp.where(causal, d_scores[...], 0.0).astype(BF16)
        low_state = states_ref[part]
        d_b = mul_tn(low_d_state, scaled[...]) + mul_nt(c_in, low_d_scores)
        d_c = mul_tn(low_state, d_scaled[...]) + mul_nn(b_in, low_d_scores)
        if last:
            d_active[inner : inner + state_dim, lanes] = d_b + bc_part_ref[:state_dim, lanes]
            d_active[inner + state_dim :, lanes] = d_c + bc_part_ref[state_dim:, lanes]
        else:
            bc_out_ref[:state_dim, lanes] = d_b
            bc_out_ref[state_dim:, lanes] = d_c
        from_state[...] = mul_nt(d_scaled[...], c_in)

        @pl.loop(0, heads // GROUP, unroll=HEADS_ABREAST)
        def _(group):
            eight = pl.ds(pl.multiple_of(group * GROUP, GROUP), GROUP)
            total_g = total_s[eight, :]
            for j in range(GROUP):
                rows = pl.ds(pl.multiple_of((group * GROUP + j) * width, width), width)
                d_state[rows, :] = total_g[j : j + 1] * d_state[rows, :] + from_state[rows, :]

        d_log = (
            lane_sums(row_part_ref[:, lanes] - pair_s[...], ending)
            + lane_sums(step * ending_s[...], before_it)
            + total * jnp.sum(state_dots[...], axis=1, keepdims=True)
        )
        rate_part_ref[:, lanes] = d_log * step * rate
        d_raw_ref[:, lanes] = (direct_s[...] + d_log * rate) * slope[:, lanes]

    for index, (mixed_ref, before_ref, tile) in enumerate(tiles):
        lanes = slice(tile * LANES, (tile + 1) * LANES)
        active_rows = slice(index * LANES, (index + 1) * LANES)
        before = before_ref[:, lanes].astype(F32)[8:]
        extended[index, :8, :] = jnp.where(first_block, 0.0, before)
        extended[index, 8:, :] = mixed_ref[:, lanes].astype(F32)
        taps = taps_ref[first_tiles[0] + index if mixed_ref is mixed_refs[0] else first_tiles[1] + tile]
        moved = [extended[index, 8 - shift : 8 - shift + span, :] for shift in range(4)]
        summed = taps[4:5] + moved[0] * taps[3:4]
        for shift in range(1, 4):
            summed = summed + moved[shift] * taps[3 - shift : 4 - shift]
        sig = sigmoid(summed)
        d_summed = d_active[active_rows, :].T * (sig * (1.0 + summed * (1.0 - sig)))
        d_extended[index, span:, :] = d_extended[index, :8, :]
        d_extended[index, :span, :] = d_summed
        d_block = d_summed * taps[3:4]
        for shift in range(1, 4):
            d_block = d_block + d_extended[index, shift : shift + span, :] * taps[3 - shift : 4 - shift]
        d_rest_ref[:, active_rows] = d_block.astype(BF16)
        for shift in range(4):
            sums[3 - shift, index] += eighths(d_summed * moved[shift])
        sums[4, index] += eighths(d_summed)

    if last:
        d_raw = jnp.concatenate([d_raw_before_ref[...], d_raw_ref[...]], axis=0)
        done = len(tiles) * LANES
        d_rest_ref[:, done : done + LANES] = as_columns(d_raw).astype(BF16)
        d_rest_ref[:, done + LANES :] = jnp.zeros((span, d_rest_ref.shape[1] - done - LANES), BF16)

    @pl.when(first_block)
    def _():
        for k in range(5):
            conv_part_ref[k] = jnp.sum(sums[k], axis=1)


def whole(shape):
    return pl.BlockSpec(shape, lambda c: (0,) * len(shape), pipeline_mode=pl.Buffered(1))


ANYWHERE = pl.BlockSpec(memory_space=pl.ANY)
SCALARS = pl.BlockSpec(memory_space=pltpu.SMEM)


def kernel_options(microseconds):
    return dict(
        compiler_params=pltpu.CompilerParams(
            dimension_semantics=("arbitrary",), vmem_limit_bytes=VMEM_LIMIT
        ),
        cost_estimate=pl.CostEstimate(
            flops=microseconds * 10**9, bytes_accessed=microseconds * 10**6, transcendentals=0
        ),
    )


def forward(sizes, places, tokens, gain, raw_weight, taps, heads_in, pieces, lengths):
    inner, conv, heads, state_dim = sizes
    length, model = tokens.shape
    span = min(SPAN, length)
    stretch = min(STRETCH, span)
    parts = span // stretch
    along = lambda rows: pl.BlockSpec((rows, span), lambda c: (0, c))
    down = lambda columns: pl.BlockSpec((span, columns), lambda c: (c, 0))
    shape = jax.ShapeDtypeStruct
    return pl.pallas_call(
        functools.partial(forward_body, sizes, tuple(lengths)),
        grid=(length // span,),
        in_specs=[
            SCALARS,
            down(model),
            whole(gain.shape),
            whole(raw_weight.shape),
            whole(taps.shape),
            whole(heads_in.shape),
        ]
        + [ANYWHERE] * len(pieces),
        out_specs=[
            down(model),
            down(conv),
            along(conv),
            along(heads),
            pl.BlockSpec((parts, inner, state_dim), lambda c: (c, 0, 0)),
            along(inner),
            along(inner),
            ANYWHERE,
        ],
        out_shape=[
            shape((length, model), BF16),
            shape((length, conv), BF16),
            shape((conv, length), BF16),
            shape((heads, length), F32),
            shape((length // stretch, inner, state_dim), BF16),
            shape((inner, length), F32),
            shape((inner, length), F32),
            shape((inner + conv + SPARE, model), BF16),
        ],
        scratch_shapes=[
            pltpu.VMEM((inner + conv + SPARE, model), BF16),
            pltpu.VMEM((inner, state_dim), F32),
            pltpu.VMEM((conv // LANES, span + 8, LANES), F32),
            pltpu.VMEM((inner, stretch), F32),
            pltpu.VMEM((inner, stretch), BF16),
            pltpu.VMEM((inner, state_dim), F32),
            pltpu.VMEM((heads, stretch), F32),
            pltpu.VMEM((heads, stretch), F32),
            pltpu.VMEM((heads, stretch), F32),
            pltpu.VMEM((heads, stretch), F32),
            pltpu.VMEM((heads, LANES), F32),
            pltpu.SemaphoreType.DMA((len(pieces) + 1,)),
        ],
        name="block_forward",
        **kernel_options(30),
    )(places, tokens, gain, raw_weight, taps, heads_in, *pieces)


def gated(sizes, places, skip, alive, cotangent, inner_gain, gate, scanned, active, pieces, lengths):
    inner, conv, heads, state_dim = sizes
    length, model = cotangent.shape
    span = min(SPAN, length)
    along = lambda rows: pl.BlockSpec((rows, span), lambda c: (0, c))
    shape = jax.ShapeDtypeStruct
    return pl.pallas_call(
        functools.partial(gated_body, sizes, tuple(lengths)),
        grid=(length // span,),
        in_specs=[
            SCALARS,
            SCALARS,
            SCALARS,
            pl.BlockSpec((span, model), lambda c: (c, 0)),
            whole(inner_gain.shape),
            along(inner),
            along(inner),
            along(inner),
        ]
        + [ANYWHERE] * len(pieces),
        out_specs=[
            along(inner),
            pl.BlockSpec((span, inner), lambda c: (c, 0)),
            along(inner),
            along(heads),
            along(heads),
            pl.BlockSpec((inner, LANES), lambda c: (0, 0)),
            ANYWHERE,
        ],
        out_shape=[
            shape((inner, length), BF16),
            shape((length, inner), BF16),
            shape((inner, length), BF16),
            shape((heads, length), F32),
            shape((heads, length), F32),
            shape((inner, LANES), F32),
            shape((inner, model), BF16),
        ],
        scratch_shapes=[
            pltpu.VMEM((inner, model), BF16),
            pltpu.VMEM((inner, span), F32),
            pltpu.VMEM((inner, span), F32),
            pltpu.SemaphoreType.DMA((len(pieces) + 1,)),
        ],
        name="block_gated",
        **kernel_options(15),
    )(places, skip, alive, cotangent, inner_gain, gate, scanned, active, *pieces)


def backward(sizes, first_head, heads, skip, active, mixed, d_scan, raw, row_part, states, taps, heads_in, earlier):
    all_inner, conv, all_heads, state_dim = sizes
    width = all_inner // all_heads
    inner = heads * width
    last = first_head + heads == all_heads
    length = active.shape[1]
    span = min(SPAN, length)
    stretch = min(STRETCH, span)
    parts = span // stretch
    blocks = length // span
    per = span // 16
    at = first_head // heads
    bc = conv - all_inner
    bc_at = all_inner // bc
    along = lambda rows, index: pl.BlockSpec((rows, span), lambda c: (index, blocks - 1 - c))
    down = lambda columns, index: pl.BlockSpec((span, columns), lambda c: (blocks - 1 - c, index))
    ahead = lambda columns, index: pl.BlockSpec(
        (16, columns), lambda c: (jnp.maximum((blocks - 1 - c) * per - 1, 0), index)
    )
    shape = jax.ShapeDtypeStruct
    tiles = (inner + (bc if last else 0)) // LANES
    share = first_head * width if last else inner
    results = pl.pallas_call(
        functools.partial(backward_body, sizes, first_head, last),
        grid=(blocks,),
        in_specs=[SCALARS, along(inner, at), along(bc, bc_at), down(inner, at)]
        + [down(bc, bc_at)] * last
        + [ahead(inner, at)]
        + [ahead(bc, bc_at)] * last
        + [
            along(inner, at),
            along(heads, at),
            along(heads, at),
            pl.BlockSpec((parts, inner, state_dim), lambda c: (blocks - 1 - c, at, 0)),
            whole(taps.shape),
            whole(heads_in.shape),
        ]
        + [along(bc, 0), along(first_head, 0), ANYWHERE] * last,
        out_specs=[down(share, 1 if last else 0)]
        + [along(heads, 0), along(heads, 0), pl.BlockSpec((5, tiles, LANES), lambda c: (0, 0, 0))]
        + [along(bc, 0)] * (not last),
        out_shape=[shape((length, 2 * share), BF16)]
        + [shape((heads, length), F32), shape((heads, length), F32), shape((5, tiles, LANES), F32)]
        + [shape((bc, length), F32)] * (not last),
        scratch_shapes=[
            pltpu.VMEM((inner, state_dim), F32),
            pltpu.VMEM((tiles, span + 8, LANES), F32),
            pltpu.VMEM((tiles, span + 8, LANES), F32),
            pltpu.VMEM((tiles * LANES, span), F32),
            pltpu.VMEM((5, tiles, 8, LANES), F32),
            pltpu.VMEM((inner, stretch), F32),
            pltpu.VMEM((inner, stretch), BF16),
            pltpu.VMEM((inner, stretch), BF16),
            pltpu.VMEM((stretch, stretch), F32),
            pltpu.VMEM((heads, state_dim), F32),
            pltpu.VMEM((heads, stretch), F32),
            pltpu.VMEM((heads, stretch), F32),
            pltpu.VMEM((heads, stretch), F32),
            pltpu.VMEM((heads, stretch), F32),
            pltpu.VMEM((heads, LANES), F32),
            pltpu.VMEM((heads, stretch), F32),
            pltpu.VMEM((heads, stretch), F32),
            pltpu.VMEM((heads, stretch), F32),
        ],
        input_output_aliases={3 + 2 * 2 + 6 + 2: 0} if last else {},
        name="block_backward",
        **kernel_options(4 + heads),
    )(
        skip,
        active,
        active,
        *[mixed] * (2 + 2 * last),
        d_scan,
        raw,
        row_part,
        states,
        taps,
        heads_in,
        *((earlier[-1], earlier[1], earlier[0]) if last else ()),
    )
    return results


def powers_of_two(size):
    bits, bit = [], 1
    while bit < size:
        bits.append(bit)
        bit *= 2
    return bits if bit == size else None


def swap(block, axis, bit):
    pairs = [(k, k ^ bit) for k in range(lax.axis_size(axis))]
    return lax.ppermute(block, axis, pairs)


def cut(block, index, pieces, axis=0):
    size = block.shape[axis] // pieces
    return lax.dynamic_slice_in_dim(block, index * size, size, axis)


def halve(block, axis, bit):
    side = (lax.axis_index(axis) // bit) % 2
    got = swap(cut(block, 1 - side, 2), axis, bit)
    return (cut(block, side, 2).astype(F32) + got.astype(F32)).astype(block.dtype)


def double(block, axis, bit):
    side = (lax.axis_index(axis) // bit) % 2
    other = swap(block, axis, bit)
    return jnp.where(
        side == 0, jnp.concatenate([block, other], axis=0), jnp.concatenate([other, block], axis=0)
    )


def pair_sum(product, core):
    return added(product(core), swap(product(1 - core).astype(BF16), "dp", 1))


def after(value, *earlier):
    return lax.optimization_barrier((value, *earlier))[0]


def added(keep, got):
    return (keep.astype(F32) + got.astype(F32)).astype(BF16)


def together(*arrays):
    return lax.optimization_barrier(arrays)


def sides(block, axis, bit):
    side = (lax.axis_index(axis) // bit) % 2
    return cut(block, side, 2), cut(block, 1 - side, 2)


def joined(block, other, side, axis=0):
    return jnp.where(
        side == 0, jnp.concatenate([block, other], axis), jnp.concatenate([other, block], axis)
    )


def pair_sum(product, core):
    return added(product(core), swap(product(1 - core).astype(BF16), "dp", 1))


def after(value, *earlier):
    return lax.optimization_barrier((value, *earlier))[0]


def added(keep, got):
    return (keep.astype(F32) + got.astype(F32)).astype(BF16)


class Chain:
    def __init__(self, keep, give, axis, bit):
        self.keep, self.give, self.axis, self.bit = keep, give, axis, bit

    def start(self):
        self.got = swap(self.give, self.axis, self.bit)
        return self.give

    def finish(self, *beside):
        return added(self.keep, after(self.got, *beside) if beside else self.got)


def halving(block, axis, bit):
    side = (lax.axis_index(axis) // bit) % 2
    return Chain(cut(block, side, 2), cut(block, 1 - side, 2), axis, bit)


def spread(block, bits):
    for bit in reversed(bits):
        block = double(block, "dp", bit)
    return block


class Plain:
    def __init__(self):
        self.groups = lax.axis_size("fsdp")
        self.mine = lax.axis_index("fsdp")

    def gather(self, w_in, packed, w_out, main, prepare):
        by_group = lax.all_gather(w_in.T, "fsdp")
        weight = by_group.transpose(1, 0, 2).reshape(by_group.shape[1], -1)
        out_weight = lax.all_gather(w_out, "fsdp", tiled=True)
        here = jnp.zeros((2,), jnp.int32)
        sizes = [main], [out_weight.shape[0]]
        return (
            ([weight], here, sizes[0]),
            weight[main:],
            prepare(lax.all_gather(packed, "fsdp")),
            ([out_weight], here, sizes[1]),
        )

    def late(self, pieces, places, lengths, earlier):
        return pieces, places, lengths

    def own(self, total, axis):
        return cut(total, self.mine, self.groups, axis).astype(F32)

    def sums(self, low_mixed, incoming, d_gate, normed, kernels, columns, fillers):
        everywhere = lambda term, axis: self.own(lax.psum(term.astype(BF16), ("fsdp", "dp")), axis)
        g_out = everywhere(mul_nn(low_mixed, incoming), 0)
        g_rows, results = [everywhere(mul_tn(d_gate, normed), 1)], []
        for kernel in kernels:
            results.append(kernel(results))
        rest = results[-1][0]
        g_rows.append(everywhere(mul_tn(rest[:, :columns], normed), 1))
        part = fillers[0](results, d_gate)
        input_grad, small = fillers[1](results, rest, part, d_gate)
        block_out = fillers[2](d_gate)
        total = cut(lax.psum(small, ("fsdp", "dp")), self.mine, self.groups)[0]
        return g_out, g_rows, total, input_grad, block_out


class Paired:
    def __init__(self):
        self.mine = lax.axis_index("fsdp")
        self.core = lax.axis_index("dp") % 2
        self.bits = powers_of_two(lax.axis_size("dp"))

    def gather(self, w_in, packed, w_out, main, prepare):
        mine, core = self.mine, self.core
        rows = w_in.T
        columns = rows.shape[1]
        last = jnp.pad(rows[main:], ((0, 32 - (rows.shape[0] - main)), (0, 0)))
        half = main // 2
        outer = half // 48 * 16
        middle = half - 2 * outer
        near = self.bits[1]
        side = (lax.axis_index("dp") // near) % 2
        first_row = core * half
        row = lambda where: first_row + jnp.where(side == where, 0, outer + middle)
        part = lambda start, count: lax.dynamic_slice_in_dim(rows, start, count, 0)
        other_packed = swap(packed, "fsdp", 1)
        mine_outer = swap(jnp.concatenate([part(row(0), outer), last], axis=0), "fsdp", 1)
        mine_middle = swap(after(part(first_row + outer, middle), mine_outer), "fsdp", 1)
        near_outer = swap(mine_outer, "dp", near)
        in_order = lambda a, b, axis: jnp.where(
            mine == 0, jnp.concatenate([a, b], axis), jnp.concatenate([b, a], axis)
        )
        raw_weight = in_order(last, mine_outer[outer:], 1)
        prepared = prepare(in_order(packed[None], other_packed[None], 0))
        raw_weight, *prepared = together(raw_weight, *prepared, mine_middle)[:-1]
        core_outer = swap(after(mine_outer, near_outer, mine_middle, raw_weight, *prepared), "dp", 1)
        core_middle = swap(mine_middle, "dp", 1)
        core_near = swap(near_outer, "dp", 1)
        there = (1 - mine) * columns
        across = half - 2 * first_row
        places = [0, mine * columns]
        for start in (row(0), first_row + outer, row(1)):
            places += [start, there, start + across, there]
        places = jnp.stack(places).astype(jnp.int32)
        pieces = [rows, mine_outer, core_outer, mine_middle, core_middle, near_outer, core_near]
        lengths = [main, outer, outer, middle, middle, outer, outer]
        relayed = core_near

        each = w_out.shape[0]
        direct_out = swap(after(cut(w_out, core, 2), relayed), "fsdp", 1)
        other = (1 - mine) * each
        places_out = jnp.stack(
            [mine * each, 0, other + core * (each // 2), 0, other + (1 - core) * (each // 2), 0]
        ).astype(jnp.int32)
        return (
            (pieces, places, lengths),
            raw_weight,
            prepared,
            ([w_out, direct_out], places_out, [each, each // 2, each // 2]),
        )

    def late(self, pieces, places, lengths, earlier):
        own, direct = pieces
        direct = after(direct, earlier)
        return [own, direct, swap(direct, "dp", 1)], places, lengths

    def sums(self, low_mixed, incoming, d_gate, normed, kernels, columns, fillers):
        mine, core, (near, *far) = self.mine, self.core, self.bits[1:]
        near_side = (lax.axis_index("dp") // near) % 2
        owned = lambda block: (cut(block, mine, 2, 1), cut(block, 1 - mine, 2, 1))
        across = lambda give: swap(give, "fsdp", 1)
        over = lambda give, bit: swap(give, "dp", bit)

        out_block = pair_sum(lambda c: mul_nn(low_mixed, cut(incoming, c, 2, 1)), core)
        gate_block = pair_sum(lambda c: mul_tn(cut(d_gate, c, 2, 1), normed), core)
        gate_keep, gate_give = owned(gate_block)
        keep_a = jnp.concatenate([cut(out_block, mine, 2), gate_keep], axis=0)
        give_a = jnp.concatenate([cut(out_block, 1 - mine, 2), gate_give], axis=0)
        got_a = across(give_a)
        first = kernels[0]([], give_a)
        got_a, _ = together(got_a, first[-1])
        keep_a, give_a = sides(added(keep_a, got_a), "dp", near)
        got_a = over(give_a, near)
        second = kernels[1]([first], give_a)
        got_a, rest = together(got_a, second[0])
        part = lambda c: lax.dynamic_slice_in_dim(rest, c * (columns // 2), columns // 2, 1)
        block_b = pair_sum(lambda c: mul_tn(part(c), normed), core)
        keep_b, give_b = owned(block_b)
        got_b = across(give_b)
        side = lambda bit: (lax.axis_index("dp") // bit) % 2
        results = [first, second]
        turn, wide = far[0], far[1:]

        keep_a, give_a = sides(added(keep_a, after(got_a, give_b)), "dp", turn)
        got_a = over(give_a, turn)
        part = fillers[0](results, after(give_b, give_a))
        got_a, part = together(got_a, part)
        block_a = added(keep_a, got_a)
        sent_a = [over(block_a, bit) for bit in wide[:1]]
        input_grad, small = fillers[1](results, rest, part, block_a)
        for bit in wide[1:]:
            block_a = added(block_a, sent_a.pop())
            sent_a = [over(block_a, bit)]
        *sent_a, got_b, small = together(*sent_a, got_b, small)
        if sent_a:
            block_a = added(block_a, sent_a[0])
        block_b = added(keep_b, got_b)

        keep_b, give_b = sides(block_b, "dp", near)
        moved = over(give_b, near), over(block_a, turn), over(small, 1)
        block_out = fillers[2](together(give_b, block_a, small)[0])
        got_b, got_a, got_s, block_out = together(*moved, block_out)
        block_a, small = joined(block_a, got_a, side(turn)), small + got_s
        spread_a = over(block_a, near)
        keep_b, give_b = sides(added(keep_b, got_b), "dp", turn)
        got_b, got_s = together(over(give_b, turn), over(small, near))
        block_b, small = added(keep_b, got_b), small + got_s
        for bit in wide:
            got_b, got_s = together(over(block_b, bit), over(small, bit))
            block_b, small = added(block_b, got_b), small + got_s
        got_b, got_s, spread_a = together(over(block_b, turn), over(small, turn), spread_a)
        block_b, small = joined(block_b, got_b, side(turn)), small + got_s
        block_a = joined(block_a, spread_a, side(near))
        got_b, got_s = together(over(block_b, near), across(cut(small, 1 - mine, 2)[0]))
        block_b, total = joined(block_b, got_b, side(near)), cut(small, mine, 2)[0] + got_s
        size = out_block.shape[0] // 2
        swapped_a, swapped_b = swap(block_a, "dp", 1), swap(block_b, "dp", 1)
        g_out = joined(block_a[:size], swapped_a[:size], core, 1).astype(F32)
        g_rows = [joined(block_a[size:], swapped_a[size:], core), joined(block_b, swapped_b, core)]
        return g_out, [rows.astype(F32) for rows in g_rows], total, input_grad, block_out


def shards(
    tokens,
    live,
    norm_gain,
    w_in,
    conv_weight,
    conv_bias,
    dt_bias,
    a_log,
    d_skip,
    inner_gain,
    w_out,
    cotangent,
):
    groups, copies = lax.axis_size("fsdp"), lax.axis_size("dp")
    taps = conv_weight.shape[1]
    heads = dt_bias.shape[0] * groups
    inner, conv = inner_gain.shape[0] * groups, conv_bias.shape[0] * groups
    model = tokens.shape[-1]
    proj = w_in.shape[1]
    main = inner + conv
    sizes = (inner, conv, heads, (conv - inner) // 2)
    paired = groups == 2 and powers_of_two(copies) and copies > 2 and main % 32 == 0
    links = Paired() if paired else Plain()

    rest = jnp.concatenate([norm_gain, dt_bias, a_log, d_skip])
    line = max(conv_bias.shape[0], inner_gain.shape[0], rest.shape[0])
    lined = lambda table: jnp.pad(table, ((0, 0), (0, line - table.shape[1])))
    packed = jnp.concatenate([lined(conv_weight.T), lined(conv_bias[None]), lined(inner_gain[None]), lined(rest[None])])

    def prepare(packed):
        packed = packed.astype(F32)
        pick = lambda row, first, each: packed[:, row, first : first + each].reshape(-1)
        model_each, heads_each = norm_gain.shape[0], dt_bias.shape[0]
        table = packed[:, : taps + 1, : conv // groups].transpose(1, 0, 2).reshape(taps + 1, conv)
        table = jnp.concatenate([table, jnp.zeros((7 - taps, conv), F32)], axis=0)
        taps_in = table.reshape(8, conv // LANES, LANES).transpose(1, 0, 2)
        inner_all = pick(taps + 1, 0, inner // groups)[:, None]
        gain_all = pick(taps + 2, 0, model_each)[None]
        by_head = [pick(taps + 2, model_each + k * heads_each, heads_each) for k in range(3)]
        return [taps_in, inner_all, gain_all, jnp.stack(by_head[:2], axis=1), by_head[2]]

    in_pieces, raw_weight, prepared, out_pieces = links.gather(w_in, packed, w_out, main, prepare)
    raw_weight = jnp.pad(raw_weight, ((0, 32 - raw_weight.shape[0]), (0, 0)))
    taps_in, inner_all, gain_all, heads_in, skip = prepared

    alive = live.astype(F32).reshape(1)
    low_tokens, low_cotangent = tokens[0, 0], cotangent[0, 0]
    normed, mixed, active, raw, states, gate, scanned, weight = forward(
        sizes, in_pieces[1], low_tokens, gain_all, raw_weight, taps_in, heads_in, in_pieces[0], in_pieces[2]
    )
    out_pieces = links.late(*out_pieces, normed)
    low_mixed, d_gate, d_scan, row_part, skip_part, gain_part, out_weight = gated(
        sizes, out_pieces[1], skip, alive, low_cotangent, inner_all, gate, scanned, active, out_pieces[0], out_pieces[2]
    )
    u = low_tokens.astype(F32)
    incoming = low_cotangent.astype(F32) * alive[0]

    def backward_step(first, count):
        def step(earlier, *sent):
            scan = after(d_scan, *sent) if sent else d_scan
            return backward(
                sizes,
                first,
                count,
                skip,
                active,
                mixed,
                scan,
                raw,
                row_part,
                states,
                taps_in,
                heads_in,
                earlier[-1] if earlier else None,
            )

        return step

    kernels = [backward_step(first, count) for first, count in HEAD_RANGES]

    step = 64
    rest_columns = -(-(proj - inner) // step) * step

    def gate_part(results, tie):
        return mul_nn(after(d_gate, tie), weight[:inner])

    def input_part(results, rest, d_normed, tie):
        rest = after(rest, tie)
        d_raw, rate_part = [jnp.concatenate([result[k] for result in results], axis=0) for k in (1, 2)]
        conv_part = jnp.concatenate([result[3] for result in results], axis=1).reshape(taps + 1, conv)
        d_normed = d_normed + mul_nn(rest, weight[inner : inner + rest.shape[1]])
        scale = lax.rsqrt(jnp.mean(u * u, axis=1, keepdims=True) + EPSILON)
        unit = u * scale
        d_unit = d_normed * gain_all
        input_grad = incoming + scale * (d_unit - unit * jnp.mean(d_unit * unit, axis=1, keepdims=True))
        terms = [
            conv_part,
            jnp.sum(gain_part, axis=1)[None],
            jnp.sum(d_normed * unit, axis=0)[None],
            jnp.sum(d_raw, axis=1)[None],
            jnp.sum(rate_part, axis=1)[None],
            jnp.sum(skip_part, axis=1)[None],
        ]
        by_owner = [
            jnp.moveaxis(term.reshape(term.shape[0], groups, -1), 1, 0).reshape(groups, -1) for term in terms
        ]
        count = sum(term.shape[1] for term in by_owner)
        by_owner.append(jnp.zeros((groups, -count % (8 * LANES)), F32))
        return input_grad, jnp.concatenate(by_owner, axis=1).reshape(groups, -1, LANES)

    def out_part(tie):
        branch = mul_tn(after(low_mixed, tie), out_weight)
        return (alive[0] * (u + branch)).astype(BF16)

    g_out, g_rows, total, input_grad, block_out = links.sums(
        low_mixed, incoming.astype(BF16), d_gate, normed, kernels, rest_columns, [gate_part, input_part, out_part]
    )
    total = total.reshape(-1)
    shapes = [(taps + 1, conv), (1, inner), (1, model), (1, heads), (1, heads), (1, heads)]
    first, g_small = 0, []
    for lines, line in shapes:
        size = lines * line // groups
        g_small.append(total[first : first + size].reshape(lines, -1))
        first += size
    g_conv, g_inner, g_gain, g_bias, g_rate, g_skip = g_small
    g_proj = jnp.concatenate([g_rows[0], g_rows[1][: proj - inner]], axis=0).T
    return (
        block_out.reshape(tokens.shape),
        input_grad.reshape(cotangent.shape),
        g_gain[0],
        g_proj,
        g_conv[:taps].T,
        g_conv[taps],
        g_bias[0],
        g_rate[0],
        g_skip[0],
        g_inner[0],
        g_out,
    )


def solution(mesh):
    by_device = P("fsdp", "dp", None, None)
    lines, tables = P("fsdp"), P("fsdp", None)
    return jax.shard_map(
        shards,
        mesh=mesh,
        in_specs=(
            by_device,
            P("fsdp", "dp"),
            lines,
            tables,
            tables,
            lines,
            lines,
            lines,
            lines,
            lines,
            tables,
            by_device,
        ),
        out_specs=(by_device, by_device, lines, tables, tables, lines, lines, lines, lines, lines, tables),
        check_vma=False,
    )
```

```python
import functools
import math

import jax
import jax.numpy as jnp
from jax import lax
from jax.experimental import pallas as pl
from jax.experimental.pallas import tpu as pltpu
from jax.sharding import PartitionSpec as P

EPSILON = 1e-05
LOG2E = math.log2(math.e)
SPAN = 256
STRETCH = 128
GROUP = 8
TILE = 256
LANES = 128
SPARE = 256
TILES_ABREAST = 7
HEADS_ABREAST = 2
HEAD_RANGES = ((0, 16), (16, 8))
VMEM_LIMIT = 60 * 1024 * 1024

F32 = jnp.float32
BF16 = jnp.bfloat16


def mul_nn(a, b):
    return lax.dot_general(a, b, (((1,), (0,)), ((), ())), preferred_element_type=F32)


def mul_nt(a, b):
    return lax.dot_general(a, b, (((1,), (1,)), ((), ())), preferred_element_type=F32)


def mul_tn(a, b):
    return lax.dot_general(a, b, (((0,), (0,)), ((), ())), preferred_element_type=F32)


def triangle(size, keep):
    rows = lax.broadcasted_iota(jnp.int32, (size, size), 0)
    cols = lax.broadcasted_iota(jnp.int32, (size, size), 1)
    return keep(rows, cols)


def lane_sums(values, matrix):
    high = values.astype(BF16)
    rest = values - high.astype(F32)
    middle = rest.astype(BF16)
    low = (rest - middle.astype(F32)).astype(BF16)
    return mul_nn(high, matrix) + mul_nn(middle, matrix) + mul_nn(low, matrix)


def as_columns(rows):
    heads, span = rows.shape
    return jnp.concatenate([rows, jnp.zeros((LANES - heads, span), F32)], axis=0).T


def fold(block):
    total = block[:, :LANES]
    for first in range(LANES, block.shape[1], LANES):
        total = total + block[:, first : first + LANES]
    return total


def eighths(block):
    return block.reshape(block.shape[0] // 8, 8, block.shape[1]).sum(axis=0)


def softplus(v):
    return jnp.maximum(v, 0.0) + jnp.log1p(jnp.exp(-jnp.abs(v)))


def sigmoid(v):
    return 0.5 * jnp.tanh(0.5 * v) + 0.5


def decays(step, rate2):
    span = step.shape[1]
    upper = triangle(span, lambda r, c: r <= c).astype(BF16)
    cum = lane_sums(step * rate2, upper)
    total = cum[:, span - 1 : span]
    return cum, jnp.exp2(total - cum), jnp.exp2(cum), jnp.exp2(total)


def piece_copies(places_ref, lengths, pieces, whole_ref, sems):
    copies = []
    for k, piece in enumerate(pieces):
        rows, columns = lengths[k], piece.shape[1]
        target = whole_ref.at[
            pl.ds(pl.multiple_of(places_ref[2 * k], 16), rows),
            pl.ds(pl.multiple_of(places_ref[2 * k + 1], LANES), columns),
        ]
        copies.append(pltpu.make_async_copy(piece.at[pl.ds(0, rows), :], target, sems.at[k]))
    return copies


def forward_body(sizes, lengths, places_ref, tokens_ref, gain_ref, raw_weight_ref, taps_ref, heads_ref, *refs):
    n_pieces = len(lengths)
    pieces, refs = refs[:n_pieces], refs[n_pieces:]
    (
        normed_ref,
        mixed_ref,
        active_ref,
        raw_ref,
        states_ref,
        gate_ref,
        scanned_ref,
        weight_ref,
        weight,
        state,
        extended,
        carried,
        scaled,
        update,
        cum_s,
        step_s,
        factor_s,
        ec_s,
        total_s,
        sems,
    ) = refs
    inner, conv, heads, state_dim = sizes
    width = inner // heads
    span = tokens_ref.shape[0]
    stretch = min(STRETCH, span)
    copies = piece_copies(places_ref, lengths, pieces, weight, sems)
    kept = pltpu.make_async_copy(weight, weight_ref, sems.at[n_pieces])

    @pl.when(pl.program_id(0) == 0)
    def _():
        for copy in copies:
            copy.start()
        state[...] = jnp.zeros_like(state)
        extended[:, span:, :] = jnp.zeros((conv // LANES, 8, LANES), F32)

    u = tokens_ref[...].astype(F32)
    normed = u * lax.rsqrt(jnp.mean(u * u, axis=1, keepdims=True) + EPSILON) * gain_ref[...]
    normed = normed.astype(BF16)
    normed_ref[...] = normed

    @pl.when(pl.program_id(0) == 0)
    def _():
        for copy in copies:
            copy.wait()
        steps = raw_weight_ref.shape[0]
        weight[inner + conv : inner + conv + steps, :] = raw_weight_ref[...]
        weight[inner + conv + steps :, :] = jnp.zeros((SPARE - steps, weight.shape[1]), BF16)
        kept.start()

    @pl.loop(0, inner // TILE, unroll=6)
    def _(i):
        rows = pl.ds(pl.multiple_of(i * TILE, TILE), TILE)
        gate_ref[rows, :] = mul_nt(weight[rows, :], normed)

    @pl.loop(0, conv // TILE, unroll=TILES_ABREAST)
    def _(i):
        first = pl.multiple_of(i * TILE, TILE)
        wide = mul_nt(normed, weight[pl.ds(pl.multiple_of(inner + first, TILE), TILE), :])
        for k in range(TILE // LANES):
            index = i * (TILE // LANES) + k
            block = wide[:, k * LANES : (k + 1) * LANES]
            extended[index, :8, :] = extended[index, span:, :]
            extended[index, 8:, :] = block
            taps = taps_ref[index]
            summed = taps[4:5] + block * taps[3:4]
            for shift in range(1, 4):
                summed = summed + extended[index, 8 - shift : 8 - shift + span, :] * taps[3 - shift : 4 - shift]
            lanes = pl.ds(pl.multiple_of(first + k * LANES, LANES), LANES)
            mixed_ref[:, lanes] = block.astype(BF16)
            active_ref[lanes, :] = (summed * sigmoid(summed)).T.astype(BF16)

    raw = mul_nt(raw_weight_ref[...], normed)[:heads] + heads_ref[:, 0:1]
    raw_ref[...] = raw
    step_all = softplus(raw)
    rate2 = -jnp.exp(heads_ref[:, 1:2]) * LOG2E
    causal = triangle(stretch, lambda r, c: r <= c)
    for part in range(span // stretch):
        lanes = slice(part * stretch, (part + 1) * stretch)
        step = step_all[:, lanes]
        cum, factor, ec, total = decays(step, rate2)
        cum_s[...] = cum
        step_s[...] = step
        factor_s[...] = factor * step
        ec_s[...] = ec
        total_s[...] = jnp.broadcast_to(total, (heads, LANES))
        b_in = active_ref[inner : inner + state_dim, lanes]
        c_in = active_ref[inner + state_dim : inner + 2 * state_dim, lanes]
        scores = jnp.where(causal, mul_tn(b_in, c_in), 0.0)
        low_state = state[...].astype(BF16)
        states_ref[part] = low_state
        carried[...] = mul_nn(low_state, c_in)

        @pl.loop(0, heads // GROUP, unroll=HEADS_ABREAST)
        def _(group):
            eight = pl.ds(pl.multiple_of(group * GROUP, GROUP), GROUP)
            cum_g, step_g, factor_g, ec_g = cum_s[eight, :], step_s[eight, :], factor_s[eight, :], ec_s[eight, :]
            cum_c = as_columns(cum_g)
            for j in range(GROUP):
                rows = pl.ds(pl.multiple_of((group * GROUP + j) * width, width), width)
                row = slice(j, j + 1)
                values = active_ref[rows, lanes].astype(F32)
                stepped = (values * step_g[row]).astype(BF16)
                decay = jnp.exp2(jnp.minimum(cum_g[row] - cum_c[:, row], 0.0))
                weights = (scores * decay).astype(BF16)
                scanned_ref[rows, lanes] = mul_nn(stepped, weights) + ec_g[row] * carried[rows, :]
                scaled[rows, :] = (values * factor_g[row]).astype(BF16)

        update[...] = mul_nt(scaled[...], b_in)

        @pl.loop(0, heads // GROUP, unroll=HEADS_ABREAST)
        def _(group):
            eight = pl.ds(pl.multiple_of(group * GROUP, GROUP), GROUP)
            total_g = total_s[eight, :]
            for j in range(GROUP):
                rows = pl.ds(pl.multiple_of((group * GROUP + j) * width, width), width)
                state[rows, :] = total_g[j : j + 1] * state[rows, :] + update[rows, :]

    @pl.when(pl.program_id(0) == pl.num_programs(0) - 1)
    def _():
        kept.wait()


def gated_body(sizes, lengths, places_ref, skip_ref, alive_ref, cotangent_ref, inner_gain_ref, *refs):
    n_pieces = len(lengths)
    gate, scanned, values_ref = refs[:3]
    pieces, refs = refs[3 : 3 + n_pieces], refs[3 + n_pieces :]
    (
        low_mixed_ref,
        d_gate_ref,
        d_scan_ref,
        row_part_ref,
        skip_part_ref,
        gain_part_ref,
        out_weight_ref,
        out_weight,
        gated,
        d_normed,
        sems,
    ) = refs
    inner, conv, heads, state_dim = sizes
    width = inner // heads
    span = cotangent_ref.shape[0]
    copies = piece_copies(places_ref, lengths, pieces, out_weight, sems)
    kept = pltpu.make_async_copy(out_weight, out_weight_ref, sems.at[n_pieces])

    @pl.when(pl.program_id(0) == 0)
    def _():
        for copy in copies:
            copy.start()
        gain_part_ref[...] = jnp.zeros_like(gain_part_ref)

    def gated_head(h, squares):
        rows = pl.ds(pl.multiple_of(h * width, width), width)
        z = gate[rows, :]
        y = scanned[rows, :] + skip_ref[h] * values_ref[rows, :].astype(F32)
        v = y * (z * sigmoid(z))
        gated[rows, :] = v
        return squares + eighths(v * v)

    squares = lax.fori_loop(0, heads, gated_head, jnp.zeros((8, span), F32), unroll=4)
    scale = lax.rsqrt(jnp.sum(squares, axis=0, keepdims=True) / inner + EPSILON)

    @pl.when(pl.program_id(0) == 0)
    def _():
        for copy in copies:
            copy.wait()
        kept.start()

    incoming = (cotangent_ref[...].astype(F32) * alive_ref[0]).astype(BF16)

    def norm_tile(i, dots):
        rows = pl.ds(pl.multiple_of(i * TILE, TILE), TILE)
        gain = inner_gain_ref[rows, :]
        unit = gated[rows, :] * scale
        low_mixed_ref[rows, :] = (unit * gain).astype(BF16)
        d_mixed = mul_nt(out_weight[rows, :], incoming)
        gain_part_ref[rows, :] += fold(d_mixed * unit)
        d_unit = d_mixed * gain
        d_normed[rows, :] = d_unit
        return dots + eighths(d_unit * unit)

    dots = lax.fori_loop(0, inner // TILE, norm_tile, jnp.zeros((8, span), F32), unroll=3)
    mean_dot = jnp.sum(dots, axis=0, keepdims=True) / inner

    @pl.loop(0, heads // GROUP, unroll=HEADS_ABREAST)
    def _(group):
        eight = pl.ds(pl.multiple_of(group * GROUP, GROUP), GROUP)
        row_parts, skip_parts, d_gates = [], [], []
        for j in range(GROUP):
            h = group * GROUP + j
            rows = pl.ds(pl.multiple_of(h * width, width), width)
            z = gate[rows, :]
            sig = sigmoid(z)
            values = values_ref[rows, :].astype(F32)
            pure = scanned[rows, :]
            y = pure + skip_ref[h] * values
            d_gated = scale * (d_normed[rows, :] - gated[rows, :] * (scale * mean_dot))
            d_scan = (d_gated * (z * sig)).astype(BF16)
            d_scan_ref[rows, :] = d_scan
            d_gates.append(d_gated * y * (sig * (1.0 + z * (1.0 - sig))))
            if len(d_gates) * width == LANES:
                lanes = pl.ds(pl.multiple_of((h + 1) * width - LANES, LANES), LANES)
                d_gate_ref[:, lanes] = jnp.concatenate(d_gates, axis=0).T.astype(BF16)
                d_gates = []
            d_scan = d_scan.astype(F32)
            row_parts.append(jnp.sum(d_scan * pure, axis=0, keepdims=True))
            skip_parts.append(jnp.sum(d_scan * values, axis=0, keepdims=True))
        row_part_ref[eight, :] = jnp.concatenate(row_parts, axis=0)
        skip_part_ref[eight, :] = jnp.concatenate(skip_parts, axis=0)

    @pl.when(pl.program_id(0) == pl.num_programs(0) - 1)
    def _():
        kept.wait()


def backward_body(sizes, first_head, last, *refs):
    refs = list(refs)
    take = lambda n: [refs.pop(0) for _ in range(n)]
    skip_ref, active_ref, low_bc_ref = take(3)
    mixed_refs = take(2 if last else 1)
    before_refs = take(2 if last else 1)
    d_scan_ref, raw_ref, row_part_ref, states_ref, taps_ref, heads_ref = take(6)
    bc_part_ref, d_raw_before_ref, _ = take(3) if last else (None, None, None)
    d_rest_ref = take(1)[0]
    d_raw_ref, rate_part_ref, conv_part_ref = take(3)
    bc_out_ref = None if last else take(1)[0]
    (
        d_state,
        extended,
        d_extended,
        d_active,
        sums,
        from_state,
        scaled,
        d_scaled,
        d_scores,
        state_dots,
        cum_s,
        step_s,
        factor_s,
        ec_s,
        total_s,
        pair_s,
        direct_s,
        ending_s,
    ) = refs
    all_inner, conv, all_heads, state_dim = sizes
    inner, span = active_ref.shape
    width = all_inner // all_heads
    heads = inner // width
    tiles = [(ref, before, t) for ref, before in zip(mixed_refs, before_refs) for t in range(ref.shape[1] // LANES)]
    first_tiles = [first_head * width // LANES, all_inner // LANES]
    stretch = min(STRETCH, span)
    first_block = pl.program_id(0) == pl.num_programs(0) - 1

    @pl.when(pl.program_id(0) == 0)
    def _():
        d_state[...] = jnp.zeros_like(d_state)
        d_extended[:, :8, :] = jnp.zeros((len(tiles), 8, LANES), F32)
        sums[...] = jnp.zeros_like(sums)

    raw = raw_ref[...]
    step_all = softplus(raw)
    slope = sigmoid(raw)
    rate = -jnp.exp(heads_ref[first_head : first_head + heads, 1:2])
    rate2 = rate * LOG2E
    causal = triangle(stretch, lambda r, c: r <= c)
    ending = triangle(stretch, lambda r, c: r >= c).astype(BF16)
    before_it = triangle(stretch, lambda r, c: r < c).astype(BF16)
    for part in reversed(range(span // stretch)):
        lanes = slice(part * stretch, (part + 1) * stretch)
        step = step_all[:, lanes]
        cum, factor, ec, total = decays(step, rate2)
        cum_s[...] = cum
        step_s[...] = step
        factor_s[...] = factor
        ec_s[...] = ec
        total_s[...] = jnp.broadcast_to(total, (heads, LANES))
        b_in = low_bc_ref[:state_dim, lanes]
        c_in = low_bc_ref[state_dim:, lanes]
        scores = jnp.where(causal, mul_tn(b_in, c_in), 0.0)
        low_d_state = d_state[...].astype(BF16)
        from_state[...] = mul_nn(low_d_state, b_in)
        d_scores[...] = jnp.zeros_like(d_scores)

        @pl.loop(0, heads // GROUP, unroll=HEADS_ABREAST)
        def _(group):
            eight = pl.ds(pl.multiple_of(group * GROUP, GROUP), GROUP)
            cum_g, step_g, factor_g, ec_g = cum_s[eight, :], step_s[eight, :], factor_s[eight, :], ec_s[eight, :]
            cum_c = as_columns(cum_g)
            pairs, directs, endings, dots = [], [], [], []
            d_scores_g = d_scores[...]
            for j in range(GROUP):
                h = group * GROUP + j
                rows = pl.ds(pl.multiple_of(h * width, width), width)
                row = slice(j, j + 1)
                values = active_ref[rows, lanes].astype(F32)
                stepped = (values * step_g[row]).astype(BF16)
                low_d = d_scan_ref[rows, lanes]
                d_scan = low_d.astype(F32)
                decay = jnp.exp2(jnp.minimum(cum_g[row] - cum_c[:, row], 0.0))
                weights = (scores * decay).astype(BF16)
                inside = mul_nt(low_d, weights)
                d_scores_g = d_scores_g + mul_tn(stepped, low_d) * decay
                across = from_state[rows, :] * factor_g[row]
                both = inside + across
                d_active[rows, lanes] = step_g[row] * both + skip_ref[first_head + h] * d_scan
                pairs.append(jnp.sum(stepped.astype(F32) * inside, axis=0, keepdims=True))
                directs.append(jnp.sum(values * both, axis=0, keepdims=True))
                endings.append(jnp.sum(values * across, axis=0, keepdims=True))
                scaled[rows, :] = (values * (step_g[row] * factor_g[row])).astype(BF16)
                d_scaled[rows, :] = (d_scan * ec_g[row]).astype(BF16)
                dots.append(jnp.sum(d_state[rows, :] * states_ref[part, rows, :].astype(F32), axis=0, keepdims=True))
            d_scores[...] = d_scores_g
            pair_s[eight, :] = jnp.concatenate(pairs, axis=0)
            direct_s[eight, :] = jnp.concatenate(directs, axis=0)
            ending_s[eight, :] = jnp.concatenate(endings, axis=0)
            state_dots[eight, :] = jnp.concatenate(dots, axis=0)

        low_d_scores = jnp.where(causal, d_scores[...], 0.0).astype(BF16)
        low_state = states_ref[part]
        d_b = mul_tn(low_d_state, scaled[...]) + mul_nt(c_in, low_d_scores)
        d_c = mul_tn(low_state, d_scaled[...]) + mul_nn(b_in, low_d_scores)
        if last:
            d_active[inner : inner + state_dim, lanes] = d_b + bc_part_ref[:state_dim, lanes]
            d_active[inner + state_dim :, lanes] = d_c + bc_part_ref[state_dim:, lanes]
        else:
            bc_out_ref[:state_dim, lanes] = d_b
            bc_out_ref[state_dim:, lanes] = d_c
        from_state[...] = mul_nt(d_scaled[...], c_in)

        @pl.loop(0, heads // GROUP, unroll=HEADS_ABREAST)
        def _(group):
            eight = pl.ds(pl.multiple_of(group * GROUP, GROUP), GROUP)
            total_g = total_s[eight, :]
            for j in range(GROUP):
                rows = pl.ds(pl.multiple_of((group * GROUP + j) * width, width), width)
                d_state[rows, :] = total_g[j : j + 1] * d_state[rows, :] + from_state[rows, :]

        d_log = (
            lane_sums(row_part_ref[:, lanes] - pair_s[...], ending)
            + lane_sums(step * ending_s[...], before_it)
            + total * jnp.sum(state_dots[...], axis=1, keepdims=True)
        )
        rate_part_ref[:, lanes] = d_log * step * rate
        d_raw_ref[:, lanes] = (direct_s[...] + d_log * rate) * slope[:, lanes]

    for index, (mixed_ref, before_ref, tile) in enumerate(tiles):
        lanes = slice(tile * LANES, (tile + 1) * LANES)
        active_rows = slice(index * LANES, (index + 1) * LANES)
        before = before_ref[:, lanes].astype(F32)[8:]
        extended[index, :8, :] = jnp.where(first_block, 0.0, before)
        extended[index, 8:, :] = mixed_ref[:, lanes].astype(F32)
        taps = taps_ref[first_tiles[0] + index if mixed_ref is mixed_refs[0] else first_tiles[1] + tile]
        moved = [extended[index, 8 - shift : 8 - shift + span, :] for shift in range(4)]
        summed = taps[4:5] + moved[0] * taps[3:4]
        for shift in range(1, 4):
            summed = summed + moved[shift] * taps[3 - shift : 4 - shift]
        sig = sigmoid(summed)
        d_summed = d_active[active_rows, :].T * (sig * (1.0 + summed * (1.0 - sig)))
        d_extended[index, span:, :] = d_extended[index, :8, :]
        d_extended[index, :span, :] = d_summed
        d_block = d_summed * taps[3:4]
        for shift in range(1, 4):
            d_block = d_block + d_extended[index, shift : shift + span, :] * taps[3 - shift : 4 - shift]
        d_rest_ref[:, active_rows] = d_block.astype(BF16)
        for shift in range(4):
            sums[3 - shift, index] += eighths(d_summed * moved[shift])
        sums[4, index] += eighths(d_summed)

    if last:
        d_raw = jnp.concatenate([d_raw_before_ref[...], d_raw_ref[...]], axis=0)
        done = len(tiles) * LANES
        d_rest_ref[:, done : done + LANES] = as_columns(d_raw).astype(BF16)
        d_rest_ref[:, done + LANES :] = jnp.zeros((span, d_rest_ref.shape[1] - done - LANES), BF16)

    @pl.when(first_block)
    def _():
        for k in range(5):
            conv_part_ref[k] = jnp.sum(sums[k], axis=1)


def whole(shape):
    return pl.BlockSpec(shape, lambda c: (0,) * len(shape), pipeline_mode=pl.Buffered(1))


ANYWHERE = pl.BlockSpec(memory_space=pl.ANY)
SCALARS = pl.BlockSpec(memory_space=pltpu.SMEM)


def kernel_options(microseconds):
    return dict(
        compiler_params=pltpu.CompilerParams(
            dimension_semantics=("arbitrary",), vmem_limit_bytes=VMEM_LIMIT
        ),
        cost_estimate=pl.CostEstimate(
            flops=microseconds * 10**9, bytes_accessed=microseconds * 10**6, transcendentals=0
        ),
    )


def forward(sizes, places, tokens, gain, raw_weight, taps, heads_in, pieces, lengths):
    inner, conv, heads, state_dim = sizes
    length, model = tokens.shape
    span = min(SPAN, length)
    stretch = min(STRETCH, span)
    parts = span // stretch
    along = lambda rows: pl.BlockSpec((rows, span), lambda c: (0, c))
    down = lambda columns: pl.BlockSpec((span, columns), lambda c: (c, 0))
    shape = jax.ShapeDtypeStruct
    return pl.pallas_call(
        functools.partial(forward_body, sizes, tuple(lengths)),
        grid=(length // span,),
        in_specs=[
            SCALARS,
            down(model),
            whole(gain.shape),
            whole(raw_weight.shape),
            whole(taps.shape),
            whole(heads_in.shape),
        ]
        + [ANYWHERE] * len(pieces),
        out_specs=[
            down(model),
            down(conv),
            along(conv),
            along(heads),
            pl.BlockSpec((parts, inner, state_dim), lambda c: (c, 0, 0)),
            along(inner),
            along(inner),
            ANYWHERE,
        ],
        out_shape=[
            shape((length, model), BF16),
            shape((length, conv), BF16),
            shape((conv, length), BF16),
            shape((heads, length), F32),
            shape((length // stretch, inner, state_dim), BF16),
            shape((inner, length), F32),
            shape((inner, length), F32),
            shape((inner + conv + SPARE, model), BF16),
        ],
        scratch_shapes=[
            pltpu.VMEM((inner + conv + SPARE, model), BF16),
            pltpu.VMEM((inner, state_dim), F32),
            pltpu.VMEM((conv // LANES, span + 8, LANES), F32),
            pltpu.VMEM((inner, stretch), F32),
            pltpu.VMEM((inner, stretch), BF16),
            pltpu.VMEM((inner, state_dim), F32),
            pltpu.VMEM((heads, stretch), F32),
            pltpu.VMEM((heads, stretch), F32),
            pltpu.VMEM((heads, stretch), F32),
            pltpu.VMEM((heads, stretch), F32),
            pltpu.VMEM((heads, LANES), F32),
            pltpu.SemaphoreType.DMA((len(pieces) + 1,)),
        ],
        name="block_forward",
        **kernel_options(30),
    )(places, tokens, gain, raw_weight, taps, heads_in, *pieces)


def gated(sizes, places, skip, alive, cotangent, inner_gain, gate, scanned, active, pieces, lengths):
    inner, conv, heads, state_dim = sizes
    length, model = cotangent.shape
    span = min(SPAN, length)
    along = lambda rows: pl.BlockSpec((rows, span), lambda c: (0, c))
    shape = jax.ShapeDtypeStruct
    return pl.pallas_call(
        functools.partial(gated_body, sizes, tuple(lengths)),
        grid=(length // span,),
        in_specs=[
            SCALARS,
            SCALARS,
            SCALARS,
            pl.BlockSpec((span, model), lambda c: (c, 0)),
            whole(inner_gain.shape),
            along(inner),
            along(inner),
            along(inner),
        ]
        + [ANYWHERE] * len(pieces),
        out_specs=[
            along(inner),
            pl.BlockSpec((span, inner), lambda c: (c, 0)),
            along(inner),
            along(heads),
            along(heads),
            pl.BlockSpec((inner, LANES), lambda c: (0, 0)),
            ANYWHERE,
        ],
        out_shape=[
            shape((inner, length), BF16),
            shape((length, inner), BF16),
            shape((inner, length), BF16),
            shape((heads, length), F32),
            shape((heads, length), F32),
            shape((inner, LANES), F32),
            shape((inner, model), BF16),
        ],
        scratch_shapes=[
            pltpu.VMEM((inner, model), BF16),
            pltpu.VMEM((inner, span), F32),
            pltpu.VMEM((inner, span), F32),
            pltpu.SemaphoreType.DMA((len(pieces) + 1,)),
        ],
        name="block_gated",
        **kernel_options(15),
    )(places, skip, alive, cotangent, inner_gain, gate, scanned, active, *pieces)


def input_body(alive_ref, tokens_ref, cotangent_ref, gain_ref, d_gate_ref, d_rest_ref, weight_ref, grad_ref, gain_part_ref):
    @pl.when(pl.program_id(0) == 0)
    def _():
        gain_part_ref[...] = jnp.zeros_like(gain_part_ref)

    inner = d_gate_ref.shape[1]
    d_normed = mul_nn(d_gate_ref[...], weight_ref[:inner, :]) + mul_nn(d_rest_ref[...], weight_ref[inner:, :])
    u = tokens_ref[...].astype(F32)
    scale = lax.rsqrt(jnp.mean(u * u, axis=1, keepdims=True) + EPSILON)
    unit = u * scale
    gain_part_ref[...] += eighths(d_normed * unit)
    d_unit = d_normed * gain_ref[...]
    slope = scale * (d_unit - unit * jnp.mean(d_unit * unit, axis=1, keepdims=True))
    grad_ref[...] = cotangent_ref[...].astype(F32) * alive_ref[0] + slope


def input_backward(alive, tokens, cotangent, gain, d_gate, d_rest, weight):
    length, model = tokens.shape
    span = min(SPAN, length)
    down = lambda columns: pl.BlockSpec((span, columns), lambda c: (c, 0))
    shape = jax.ShapeDtypeStruct
    return pl.pallas_call(
        input_body,
        grid=(length // span,),
        in_specs=[
            SCALARS,
            down(model),
            down(model),
            whole(gain.shape),
            down(d_gate.shape[1]),
            down(d_rest.shape[1]),
            whole(weight.shape),
        ],
        out_specs=[down(model), pl.BlockSpec((8, model), lambda c: (0, 0))],
        out_shape=[shape((length, model), F32), shape((8, model), F32)],
        name="input_backward",
        **kernel_options(8),
    )(alive, tokens, cotangent, gain, d_gate, d_rest, weight)


def backward(sizes, first_head, heads, skip, active, mixed, d_scan, raw, row_part, states, taps, heads_in, earlier):
    all_inner, conv, all_heads, state_dim = sizes
    width = all_inner // all_heads
    inner = heads * width
    last = first_head + heads == all_heads
    length = active.shape[1]
    span = min(SPAN, length)
    stretch = min(STRETCH, span)
    parts = span // stretch
    blocks = length // span
    per = span // 16
    at = first_head // heads
    bc = conv - all_inner
    bc_at = all_inner // bc
    along = lambda rows, index: pl.BlockSpec((rows, span), lambda c: (index, blocks - 1 - c))
    down = lambda columns, index: pl.BlockSpec((span, columns), lambda c: (blocks - 1 - c, index))
    ahead = lambda columns, index: pl.BlockSpec(
        (16, columns), lambda c: (jnp.maximum((blocks - 1 - c) * per - 1, 0), index)
    )
    shape = jax.ShapeDtypeStruct
    tiles = (inner + (bc if last else 0)) // LANES
    share = first_head * width if last else inner
    results = pl.pallas_call(
        functools.partial(backward_body, sizes, first_head, last),
        grid=(blocks,),
        in_specs=[SCALARS, along(inner, at), along(bc, bc_at), down(inner, at)]
        + [down(bc, bc_at)] * last
        + [ahead(inner, at)]
        + [ahead(bc, bc_at)] * last
        + [
            along(inner, at),
            along(heads, at),
            along(heads, at),
            pl.BlockSpec((parts, inner, state_dim), lambda c: (blocks - 1 - c, at, 0)),
            whole(taps.shape),
            whole(heads_in.shape),
        ]
        + [along(bc, 0), along(first_head, 0), ANYWHERE] * last,
        out_specs=[down(share, 1 if last else 0)]
        + [along(heads, 0), along(heads, 0), pl.BlockSpec((5, tiles, LANES), lambda c: (0, 0, 0))]
        + [along(bc, 0)] * (not last),
        out_shape=[shape((length, 2 * share), BF16)]
        + [shape((heads, length), F32), shape((heads, length), F32), shape((5, tiles, LANES), F32)]
        + [shape((bc, length), F32)] * (not last),
        scratch_shapes=[
            pltpu.VMEM((inner, state_dim), F32),
            pltpu.VMEM((tiles, span + 8, LANES), F32),
            pltpu.VMEM((tiles, span + 8, LANES), F32),
            pltpu.VMEM((tiles * LANES, span), F32),
            pltpu.VMEM((5, tiles, 8, LANES), F32),
            pltpu.VMEM((inner, stretch), F32),
            pltpu.VMEM((inner, stretch), BF16),
            pltpu.VMEM((inner, stretch), BF16),
            pltpu.VMEM((stretch, stretch), F32),
            pltpu.VMEM((heads, state_dim), F32),
            pltpu.VMEM((heads, stretch), F32),
            pltpu.VMEM((heads, stretch), F32),
            pltpu.VMEM((heads, stretch), F32),
            pltpu.VMEM((heads, stretch), F32),
            pltpu.VMEM((heads, LANES), F32),
            pltpu.VMEM((heads, stretch), F32),
            pltpu.VMEM((heads, stretch), F32),
            pltpu.VMEM((heads, stretch), F32),
        ],
        input_output_aliases={3 + 2 * 2 + 6 + 2: 0} if last else {},
        name="block_backward",
        **kernel_options(4 + heads),
    )(
        skip,
        active,
        active,
        *[mixed] * (2 + 2 * last),
        d_scan,
        raw,
        row_part,
        states,
        taps,
        heads_in,
        *((earlier[-1], earlier[1], earlier[0]) if last else ()),
    )
    return results


def powers_of_two(size):
    bits, bit = [], 1
    while bit < size:
        bits.append(bit)
        bit *= 2
    return bits if bit == size else None


def swap(block, axis, bit):
    pairs = [(k, k ^ bit) for k in range(lax.axis_size(axis))]
    return lax.ppermute(block, axis, pairs)


def cut(block, index, pieces, axis=0):
    size = block.shape[axis] // pieces
    return lax.dynamic_slice_in_dim(block, index * size, size, axis)


def halve(block, axis, bit):
    side = (lax.axis_index(axis) // bit) % 2
    got = swap(cut(block, 1 - side, 2), axis, bit)
    return (cut(block, side, 2).astype(F32) + got.astype(F32)).astype(block.dtype)


def double(block, axis, bit):
    side = (lax.axis_index(axis) // bit) % 2
    other = swap(block, axis, bit)
    return jnp.where(
        side == 0, jnp.concatenate([block, other], axis=0), jnp.concatenate([other, block], axis=0)
    )


def pair_sum(product, core):
    return added(product(core), swap(product(1 - core).astype(BF16), "dp", 1))


def after(value, *earlier):
    return lax.optimization_barrier((value, *earlier))[0]


def added(keep, got):
    return (keep.astype(F32) + got.astype(F32)).astype(BF16)


def together(*arrays):
    return lax.optimization_barrier(arrays)


def sides(block, axis, bit):
    side = (lax.axis_index(axis) // bit) % 2
    return cut(block, side, 2), cut(block, 1 - side, 2)


def joined(block, other, side, axis=0):
    return jnp.where(
        side == 0, jnp.concatenate([block, other], axis), jnp.concatenate([other, block], axis)
    )


def pair_sum(product, core):
    return added(product(core), swap(product(1 - core).astype(BF16), "dp", 1))


def after(value, *earlier):
    return lax.optimization_barrier((value, *earlier))[0]


def added(keep, got):
    return (keep.astype(F32) + got.astype(F32)).astype(BF16)


class Chain:
    def __init__(self, keep, give, axis, bit):
        self.keep, self.give, self.axis, self.bit = keep, give, axis, bit

    def start(self):
        self.got = swap(self.give, self.axis, self.bit)
        return self.give

    def finish(self, *beside):
        return added(self.keep, after(self.got, *beside) if beside else self.got)


def halving(block, axis, bit):
    side = (lax.axis_index(axis) // bit) % 2
    return Chain(cut(block, side, 2), cut(block, 1 - side, 2), axis, bit)


def spread(block, bits):
    for bit in reversed(bits):
        block = double(block, "dp", bit)
    return block


class Plain:
    def __init__(self):
        self.groups = lax.axis_size("fsdp")
        self.mine = lax.axis_index("fsdp")

    def gather(self, w_in, packed, w_out, main, prepare):
        by_group = lax.all_gather(w_in.T, "fsdp")
        weight = by_group.transpose(1, 0, 2).reshape(by_group.shape[1], -1)
        out_weight = lax.all_gather(w_out, "fsdp", tiled=True)
        here = jnp.zeros((2,), jnp.int32)
        sizes = [main], [out_weight.shape[0]]
        return (
            ([weight], here, sizes[0]),
            weight[main:],
            prepare(lax.all_gather(packed, "fsdp")),
            ([out_weight], here, sizes[1]),
        )

    def late(self, pieces, places, lengths, earlier):
        return pieces, places, lengths

    def own(self, total, axis):
        return cut(total, self.mine, self.groups, axis).astype(F32)

    def sums(self, low_mixed, incoming, d_gate, normed, kernels, columns, fillers):
        everywhere = lambda term, axis: self.own(lax.psum(term.astype(BF16), ("fsdp", "dp")), axis)
        g_out = everywhere(mul_nn(low_mixed, incoming), 0)
        g_rows, results = [everywhere(mul_tn(d_gate, normed), 1)], []
        for kernel in kernels:
            results.append(kernel(results))
        rest = results[-1][0]
        g_rows.append(everywhere(mul_tn(rest[:, :columns], normed), 1))
        block_out = fillers[0](d_gate)
        input_grad, small = fillers[1](results, rest, d_gate)
        total = cut(lax.psum(small, ("fsdp", "dp")), self.mine, self.groups)[0]
        return g_out, g_rows, fillers[2](total), input_grad, block_out


class Paired:
    def __init__(self):
        self.mine = lax.axis_index("fsdp")
        self.core = lax.axis_index("dp") % 2
        self.bits = powers_of_two(lax.axis_size("dp"))

    def gather(self, w_in, packed, w_out, main, prepare):
        mine, core = self.mine, self.core
        rows = w_in.T
        columns = rows.shape[1]
        last = jnp.pad(rows[main:], ((0, 32 - (rows.shape[0] - main)), (0, 0)))
        half = main // 2
        outer = half // 48 * 16
        middle = half - 2 * outer
        near = self.bits[1]
        side = (lax.axis_index("dp") // near) % 2
        first_row = core * half
        row = lambda where: first_row + jnp.where(side == where, 0, outer + middle)
        part = lambda start, count: lax.dynamic_slice_in_dim(rows, start, count, 0)
        other_packed = swap(packed, "fsdp", 1)
        mine_outer = swap(jnp.concatenate([part(row(0), outer), last], axis=0), "fsdp", 1)
        mine_middle = swap(after(part(first_row + outer, middle), mine_outer), "fsdp", 1)
        near_outer = swap(mine_outer, "dp", near)
        in_order = lambda a, b, axis: jnp.where(
            mine == 0, jnp.concatenate([a, b], axis), jnp.concatenate([b, a], axis)
        )
        raw_weight = in_order(last, mine_outer[outer:], 1)
        prepared = prepare(in_order(packed[None], other_packed[None], 0))
        raw_weight, *prepared = together(raw_weight, *prepared, mine_middle)[:-1]
        core_outer = swap(after(mine_outer, near_outer, mine_middle, raw_weight, *prepared), "dp", 1)
        core_middle = swap(mine_middle, "dp", 1)
        core_near = swap(near_outer, "dp", 1)
        there = (1 - mine) * columns
        across = half - 2 * first_row
        places = [0, mine * columns]
        for start in (row(0), first_row + outer, row(1)):
            places += [start, there, start + across, there]
        places = jnp.stack(places).astype(jnp.int32)
        pieces = [rows, mine_outer, core_outer, mine_middle, core_middle, near_outer, core_near]
        lengths = [main, outer, outer, middle, middle, outer, outer]
        relayed = core_near

        each = w_out.shape[0]
        direct_out = swap(after(cut(w_out, core, 2), relayed), "fsdp", 1)
        other = (1 - mine) * each
        places_out = jnp.stack(
            [mine * each, 0, other + core * (each // 2), 0, other + (1 - core) * (each // 2), 0]
        ).astype(jnp.int32)
        return (
            (pieces, places, lengths),
            raw_weight,
            prepared,
            ([w_out, direct_out], places_out, [each, each // 2, each // 2]),
        )

    def late(self, pieces, places, lengths, earlier):
        own, direct = pieces
        direct = after(direct, earlier)
        return [own, direct, swap(direct, "dp", 1)], places, lengths

    def sums(self, low_mixed, incoming, d_gate, normed, kernels, columns, fillers):
        mine, core, (near, *far) = self.mine, self.core, self.bits[1:]
        near_side = (lax.axis_index("dp") // near) % 2
        owned = lambda block: (cut(block, mine, 2, 1), cut(block, 1 - mine, 2, 1))
        across = lambda give: swap(give, "fsdp", 1)
        over = lambda give, bit: swap(give, "dp", bit)

        def by_cores(term, axis):
            return cut(term, core, 2, axis), swap(cut(term, 1 - core, 2, axis), "dp", 1)

        out_keep, out_got = by_cores(mul_nn(low_mixed, incoming).astype(BF16), 1)
        gate_term = mul_tn(d_gate, normed).astype(BF16)
        out_got, gate_term = together(out_got, gate_term)
        out_block = added(out_keep, out_got)
        out_give = cut(out_block, 1 - mine, 2)
        got_out = across(out_give)
        gate_keep, gate_got = by_cores(after(gate_term, out_give), 0)
        gate_keep, gate_give = owned(added(gate_keep, gate_got))
        got_gate = across(gate_give)
        first = kernels[0]([], gate_give)
        got_out, got_gate, _ = together(got_out, got_gate, first[-1])
        keep_a = jnp.concatenate([cut(out_block, mine, 2), gate_keep], axis=0)
        got_a = jnp.concatenate([got_out, got_gate], axis=0)
        keep_a, give_a = sides(added(keep_a, got_a), "dp", near)
        got_a = over(give_a, near)
        second = kernels[1]([first], give_a)
        got_a, rest = together(got_a, second[0])
        keep_b, got_b = by_cores(mul_tn(rest[:, :columns], normed).astype(BF16), 0)
        block_b = added(keep_b, got_b)
        keep_b, give_b = owned(block_b)
        got_b = across(give_b)
        side = lambda bit: (lax.axis_index("dp") // bit) % 2
        results = [first, second]
        turn, wide = far[0], far[1:]

        keep_a, give_a = sides(added(keep_a, after(got_a, give_b)), "dp", turn)
        got_a = over(give_a, turn)
        block_out = fillers[0](after(give_b, give_a))
        got_a, block_out = together(got_a, block_out)
        block_a = added(keep_a, got_a)
        sent_a = [over(block_a, bit) for bit in wide[:1]]
        input_grad, small = fillers[1](results, rest, block_a)
        for bit in wide[1:]:
            block_a = added(block_a, sent_a.pop())
            sent_a = [over(block_a, bit)]
        *sent_a, got_b, small = together(*sent_a, got_b, small)
        if sent_a:
            block_a = added(block_a, sent_a[0])
        block_b = added(keep_b, got_b)

        keep_b, give_b = sides(block_b, "dp", near)
        got_b, got_a, got_s = together(over(give_b, near), over(block_a, turn), over(small, 1))
        block_a, small = joined(block_a, got_a, side(turn)), small + got_s
        spread_a = over(block_a, near)
        keep_b, give_b = sides(added(keep_b, got_b), "dp", turn)
        got_b, got_s = together(over(give_b, turn), over(small, near))
        block_b, small = added(keep_b, got_b), small + got_s
        for bit in wide:
            got_b, got_s = together(over(block_b, bit), over(small, bit))
            block_b, small = added(block_b, got_b), small + got_s
        got_b, got_s, spread_a = together(over(block_b, turn), over(small, turn), spread_a)
        block_b, small = joined(block_b, got_b, side(turn)), small + got_s
        block_a = joined(block_a, spread_a, side(near))
        got_b, got_s = together(over(block_b, near), across(cut(small, 1 - mine, 2)[0]))
        block_b, total = joined(block_b, got_b, side(near)), cut(small, mine, 2)[0] + got_s
        size = out_block.shape[0] // 2
        swapped_a, swapped_b, *g_small = together(swap(block_a, "dp", 1), swap(block_b, "dp", 1), *fillers[2](total))
        g_out = joined(block_a[:size], swapped_a[:size], core, 1).astype(F32)
        g_rows = [joined(block_a[size:], swapped_a[size:], core), joined(block_b, swapped_b, core)]
        return g_out, [rows.astype(F32) for rows in g_rows], g_small, input_grad, block_out


def shards(
    tokens,
    live,
    norm_gain,
    w_in,
    conv_weight,
    conv_bias,
    dt_bias,
    a_log,
    d_skip,
    inner_gain,
    w_out,
    cotangent,
):
    groups, copies = lax.axis_size("fsdp"), lax.axis_size("dp")
    taps = conv_weight.shape[1]
    heads = dt_bias.shape[0] * groups
    inner, conv = inner_gain.shape[0] * groups, conv_bias.shape[0] * groups
    model = tokens.shape[-1]
    proj = w_in.shape[1]
    main = inner + conv
    sizes = (inner, conv, heads, (conv - inner) // 2)
    paired = groups == 2 and powers_of_two(copies) and copies > 2 and main % 32 == 0
    links = Paired() if paired else Plain()

    rest = jnp.concatenate([norm_gain, dt_bias, a_log, d_skip])
    line = max(conv_bias.shape[0], inner_gain.shape[0], rest.shape[0])
    lined = lambda table: jnp.pad(table, ((0, 0), (0, line - table.shape[1])))
    packed = jnp.concatenate([lined(conv_weight.T), lined(conv_bias[None]), lined(inner_gain[None]), lined(rest[None])])

    def prepare(packed):
        packed = packed.astype(F32)
        pick = lambda row, first, each: packed[:, row, first : first + each].reshape(-1)
        model_each, heads_each = norm_gain.shape[0], dt_bias.shape[0]
        table = packed[:, : taps + 1, : conv // groups].transpose(1, 0, 2).reshape(taps + 1, conv)
        table = jnp.concatenate([table, jnp.zeros((7 - taps, conv), F32)], axis=0)
        taps_in = table.reshape(8, conv // LANES, LANES).transpose(1, 0, 2)
        inner_all = pick(taps + 1, 0, inner // groups)[:, None]
        gain_all = pick(taps + 2, 0, model_each)[None]
        by_head = [pick(taps + 2, model_each + k * heads_each, heads_each) for k in range(3)]
        return [taps_in, inner_all, gain_all, jnp.stack(by_head[:2], axis=1), by_head[2]]

    in_pieces, raw_weight, prepared, out_pieces = links.gather(w_in, packed, w_out, main, prepare)
    raw_weight = jnp.pad(raw_weight, ((0, 32 - raw_weight.shape[0]), (0, 0)))
    taps_in, inner_all, gain_all, heads_in, skip = prepared

    alive = live.astype(F32).reshape(1)
    low_tokens, low_cotangent = tokens[0, 0], cotangent[0, 0]
    normed, mixed, active, raw, states, gate, scanned, weight = forward(
        sizes, in_pieces[1], low_tokens, gain_all, raw_weight, taps_in, heads_in, in_pieces[0], in_pieces[2]
    )
    out_pieces = links.late(*out_pieces, normed)
    low_mixed, d_gate, d_scan, row_part, skip_part, gain_part, out_weight = gated(
        sizes, out_pieces[1], skip, alive, low_cotangent, inner_all, gate, scanned, active, out_pieces[0], out_pieces[2]
    )
    u = low_tokens.astype(F32)
    incoming = low_cotangent.astype(F32) * alive[0]

    def backward_step(first, count):
        def step(earlier, *sent):
            scan = after(d_scan, *sent) if sent else d_scan
            return backward(
                sizes,
                first,
                count,
                skip,
                active,
                mixed,
                scan,
                raw,
                row_part,
                states,
                taps_in,
                heads_in,
                earlier[-1] if earlier else None,
            )

        return step

    kernels = [backward_step(first, count) for first, count in HEAD_RANGES]

    step = 64
    rest_columns = -(-(proj - inner) // step) * step

    def input_part(results, rest, tie):
        d_raw, rate_part = [jnp.concatenate([result[k] for result in results], axis=0) for k in (1, 2)]
        conv_part = jnp.concatenate([result[3] for result in results], axis=1).reshape(taps + 1, conv)
        input_grad, gain_part_in = input_backward(
            alive, low_tokens, low_cotangent, gain_all, d_gate, after(rest, tie), weight
        )
        terms = [
            conv_part,
            jnp.sum(gain_part, axis=1)[None],
            jnp.sum(gain_part_in, axis=0)[None],
            jnp.sum(d_raw, axis=1)[None],
            jnp.sum(rate_part, axis=1)[None],
            jnp.sum(skip_part, axis=1)[None],
        ]
        by_owner = [
            jnp.moveaxis(term.reshape(term.shape[0], groups, -1), 1, 0).reshape(groups, -1) for term in terms
        ]
        count = sum(term.shape[1] for term in by_owner)
        by_owner.append(jnp.zeros((groups, -count % (8 * LANES)), F32))
        return input_grad, jnp.concatenate(by_owner, axis=1).reshape(groups, -1, LANES)

    def out_part(tie):
        branch = mul_tn(after(low_mixed, tie), out_weight)
        return (alive[0] * (u + branch)).astype(BF16)

    def small_grads(total):
        total = total.reshape(-1)
        shapes = [(taps + 1, conv), (1, inner), (1, model), (1, heads), (1, heads), (1, heads)]
        first, parts = 0, []
        for lines, line in shapes:
            size = lines * line // groups
            parts.append(total[first : first + size].reshape(lines, -1))
            first += size
        g_conv, g_inner, g_gain, g_bias, g_rate, g_skip = parts
        return [g_gain[0], g_conv[:taps].T, g_conv[taps], g_bias[0], g_rate[0], g_skip[0], g_inner[0]]

    g_out, g_rows, g_small, input_grad, block_out = links.sums(
        low_mixed,
        incoming.astype(BF16),
        d_gate,
        normed,
        kernels,
        rest_columns,
        [out_part, input_part, small_grads],
    )
    g_proj = jnp.concatenate([g_rows[0], g_rows[1][: proj - inner]], axis=0).T
    return (
        block_out.reshape(tokens.shape),
        input_grad.reshape(cotangent.shape),
        g_small[0],
        g_proj,
        *g_small[1:],
        g_out,
    )


def solution(mesh):
    by_device = P("fsdp", "dp", None, None)
    lines, tables = P("fsdp"), P("fsdp", None)
    return jax.shard_map(
        shards,
        mesh=mesh,
        in_specs=(
            by_device,
            P("fsdp", "dp"),
            lines,
            tables,
            tables,
            lines,
            lines,
            lines,
            lines,
            lines,
            tables,
            by_device,
        ),
        out_specs=(by_device, by_device, lines, tables, tables, lines, lines, lines, lines, lines, tables),
        check_vma=False,
    )
```

```python
import functools
import math

import jax
import jax.numpy as jnp
from jax import lax
from jax.experimental import pallas as pl
from jax.experimental.pallas import tpu as pltpu
from jax.sharding import PartitionSpec as P

EPSILON = 1e-05
LOG2E = math.log2(math.e)
SPAN = 256
STRETCH = 256
GROUP = 8
TILE = 256
LANES = 128
SPARE = 256
TILES_ABREAST = 7
HEADS_ABREAST = 2
HEAD_RANGES = ((0, 16), (16, 8))
VMEM_LIMIT = 60 * 1024 * 1024

F32 = jnp.float32
BF16 = jnp.bfloat16


def mul_nn(a, b):
    return lax.dot_general(a, b, (((1,), (0,)), ((), ())), preferred_element_type=F32)


def mul_nt(a, b):
    return lax.dot_general(a, b, (((1,), (1,)), ((), ())), preferred_element_type=F32)


def mul_tn(a, b):
    return lax.dot_general(a, b, (((0,), (0,)), ((), ())), preferred_element_type=F32)


def triangle(size, keep):
    rows = lax.broadcasted_iota(jnp.int32, (size, size), 0)
    cols = lax.broadcasted_iota(jnp.int32, (size, size), 1)
    return keep(rows, cols)


def lane_sums(values, matrix):
    high = values.astype(BF16)
    rest = values - high.astype(F32)
    middle = rest.astype(BF16)
    low = (rest - middle.astype(F32)).astype(BF16)
    return mul_nn(high, matrix) + mul_nn(middle, matrix) + mul_nn(low, matrix)


def as_columns(rows):
    heads, span = rows.shape
    return jnp.concatenate([rows, jnp.zeros((LANES - heads, span), F32)], axis=0).T


def fold(block):
    total = block[:, :LANES]
    for first in range(LANES, block.shape[1], LANES):
        total = total + block[:, first : first + LANES]
    return total


def eighths(block):
    return block.reshape(block.shape[0] // 8, 8, block.shape[1]).sum(axis=0)


def softplus(v):
    return jnp.maximum(v, 0.0) + jnp.log1p(jnp.exp(-jnp.abs(v)))


def sigmoid(v):
    return 0.5 * jnp.tanh(0.5 * v) + 0.5


def decay_between(later, earlier):
    return jnp.exp2(jnp.minimum(later - earlier, 0.0))


def decays(step, rate2):
    span = step.shape[1]
    upper = triangle(span, lambda r, c: r <= c).astype(BF16)
    cum = lane_sums(step * rate2, upper)
    total = cum[:, span - 1 : span]
    return cum, jnp.exp2(total - cum), jnp.exp2(cum), jnp.exp2(total)


def piece_copies(places_ref, lengths, pieces, whole_ref, sems):
    copies = []
    for k, piece in enumerate(pieces):
        rows, columns = lengths[k], piece.shape[1]
        target = whole_ref.at[
            pl.ds(pl.multiple_of(places_ref[2 * k], 16), rows),
            pl.ds(pl.multiple_of(places_ref[2 * k + 1], LANES), columns),
        ]
        copies.append(pltpu.make_async_copy(piece.at[pl.ds(0, rows), :], target, sems.at[k]))
    return copies


def forward_body(sizes, lengths, places_ref, tokens_ref, gain_ref, raw_weight_ref, taps_ref, heads_ref, *refs):
    n_pieces = len(lengths)
    pieces, refs = refs[:n_pieces], refs[n_pieces:]
    (
        normed_ref,
        mixed_ref,
        active_ref,
        raw_ref,
        states_ref,
        gate_ref,
        scanned_ref,
        weight_ref,
        weight,
        state,
        extended,
        carried,
        scaled,
        update,
        cum_s,
        step_s,
        factor_s,
        ec_s,
        total_s,
        sems,
    ) = refs
    inner, conv, heads, state_dim = sizes
    width = inner // heads
    span = tokens_ref.shape[0]
    stretch = min(STRETCH, span)
    half = stretch // 2
    copies = piece_copies(places_ref, lengths, pieces, weight, sems)
    kept = pltpu.make_async_copy(weight, weight_ref, sems.at[n_pieces])

    @pl.when(pl.program_id(0) == 0)
    def _():
        for copy in copies:
            copy.start()
        state[...] = jnp.zeros_like(state)
        extended[:, span:, :] = jnp.zeros((conv // LANES, 8, LANES), F32)

    u = tokens_ref[...].astype(F32)
    normed = u * lax.rsqrt(jnp.mean(u * u, axis=1, keepdims=True) + EPSILON) * gain_ref[...]
    normed = normed.astype(BF16)
    normed_ref[...] = normed

    @pl.when(pl.program_id(0) == 0)
    def _():
        for copy in copies:
            copy.wait()
        steps = raw_weight_ref.shape[0]
        weight[inner + conv : inner + conv + steps, :] = raw_weight_ref[...]
        weight[inner + conv + steps :, :] = jnp.zeros((SPARE - steps, weight.shape[1]), BF16)
        kept.start()

    @pl.loop(0, inner // TILE, unroll=6)
    def _(i):
        rows = pl.ds(pl.multiple_of(i * TILE, TILE), TILE)
        gate_ref[rows, :] = mul_nt(weight[rows, :], normed)

    @pl.loop(0, conv // TILE, unroll=TILES_ABREAST)
    def _(i):
        first = pl.multiple_of(i * TILE, TILE)
        wide = mul_nt(normed, weight[pl.ds(pl.multiple_of(inner + first, TILE), TILE), :])
        for k in range(TILE // LANES):
            index = i * (TILE // LANES) + k
            block = wide[:, k * LANES : (k + 1) * LANES]
            extended[index, :8, :] = extended[index, span:, :]
            extended[index, 8:, :] = block
            taps = taps_ref[index]
            summed = taps[4:5] + block * taps[3:4]
            for shift in range(1, 4):
                summed = summed + extended[index, 8 - shift : 8 - shift + span, :] * taps[3 - shift : 4 - shift]
            lanes = pl.ds(pl.multiple_of(first + k * LANES, LANES), LANES)
            mixed_ref[:, lanes] = block.astype(BF16)
            active_ref[lanes, :] = (summed * sigmoid(summed)).T.astype(BF16)

    raw = mul_nt(raw_weight_ref[...], normed)[:heads] + heads_ref[:, 0:1]
    raw_ref[...] = raw
    step_all = softplus(raw)
    rate2 = -jnp.exp(heads_ref[:, 1:2]) * LOG2E
    causal = triangle(stretch, lambda r, c: r <= c)
    for part in range(span // stretch):
        lanes = slice(part * stretch, (part + 1) * stretch)
        step = step_all[:, lanes]
        cum, factor, ec, total = decays(step, rate2)
        cum_s[...] = cum
        step_s[...] = step
        factor_s[...] = factor * step
        ec_s[...] = ec
        total_s[...] = jnp.broadcast_to(total, (heads, LANES))
        b_in = active_ref[inner : inner + state_dim, lanes]
        c_in = active_ref[inner + state_dim : inner + 2 * state_dim, lanes]
        scores = jnp.where(causal, mul_tn(b_in, c_in), 0.0)
        low_state = state[...].astype(BF16)
        states_ref[part] = low_state
        carried[...] = mul_nn(low_state, c_in)

        @pl.loop(0, heads // GROUP, unroll=HEADS_ABREAST)
        def _(group):
            eight = pl.ds(pl.multiple_of(group * GROUP, GROUP), GROUP)
            cum_g, step_g, factor_g, ec_g = cum_s[eight, :], step_s[eight, :], factor_s[eight, :], ec_s[eight, :]
            cum_c = as_columns(cum_g)
            for j in range(GROUP):
                rows = pl.ds(pl.multiple_of((group * GROUP + j) * width, width), width)
                row = slice(j, j + 1)
                values = active_ref[rows, lanes].astype(F32)
                stepped = (values * step_g[row]).astype(BF16)
                early = (scores[:half] * decay_between(cum_g[row], cum_c[:half, row])).astype(BF16)
                late = (scores[half:, half:] * decay_between(cum_g[row, half:], cum_c[half:, row])).astype(BF16)
                inside = mul_nn(stepped[:, :half], early)
                inside = jnp.concatenate(
                    [inside[:, :half], inside[:, half:] + mul_nn(stepped[:, half:], late)], axis=1
                )
                scanned_ref[rows, lanes] = inside + ec_g[row] * carried[rows, :]
                scaled[rows, :] = (values * factor_g[row]).astype(BF16)

        update[...] = mul_nt(scaled[...], b_in)

        @pl.loop(0, heads // GROUP, unroll=HEADS_ABREAST)
        def _(group):
            eight = pl.ds(pl.multiple_of(group * GROUP, GROUP), GROUP)
            total_g = total_s[eight, :]
            for j in range(GROUP):
                rows = pl.ds(pl.multiple_of((group * GROUP + j) * width, width), width)
                state[rows, :] = total_g[j : j + 1] * state[rows, :] + update[rows, :]

    @pl.when(pl.program_id(0) == pl.num_programs(0) - 1)
    def _():
        kept.wait()


def gated_body(sizes, lengths, places_ref, skip_ref, alive_ref, cotangent_ref, inner_gain_ref, *refs):
    n_pieces = len(lengths)
    gate, scanned, values_ref = refs[:3]
    pieces, refs = refs[3 : 3 + n_pieces], refs[3 + n_pieces :]
    (
        low_mixed_ref,
        d_gate_ref,
        d_scan_ref,
        row_part_ref,
        skip_part_ref,
        gain_part_ref,
        out_weight_ref,
        out_weight,
        gated,
        d_normed,
        sems,
    ) = refs
    inner, conv, heads, state_dim = sizes
    width = inner // heads
    span = cotangent_ref.shape[0]
    copies = piece_copies(places_ref, lengths, pieces, out_weight, sems)
    kept = pltpu.make_async_copy(out_weight, out_weight_ref, sems.at[n_pieces])

    @pl.when(pl.program_id(0) == 0)
    def _():
        for copy in copies:
            copy.start()
        gain_part_ref[...] = jnp.zeros_like(gain_part_ref)

    def gated_head(h, squares):
        rows = pl.ds(pl.multiple_of(h * width, width), width)
        z = gate[rows, :]
        y = scanned[rows, :] + skip_ref[h] * values_ref[rows, :].astype(F32)
        v = y * (z * sigmoid(z))
        gated[rows, :] = v
        return squares + eighths(v * v)

    squares = lax.fori_loop(0, heads, gated_head, jnp.zeros((8, span), F32), unroll=4)
    scale = lax.rsqrt(jnp.sum(squares, axis=0, keepdims=True) / inner + EPSILON)

    @pl.when(pl.program_id(0) == 0)
    def _():
        for copy in copies:
            copy.wait()
        kept.start()

    incoming = (cotangent_ref[...].astype(F32) * alive_ref[0]).astype(BF16)

    def norm_tile(i, dots):
        rows = pl.ds(pl.multiple_of(i * TILE, TILE), TILE)
        gain = inner_gain_ref[rows, :]
        unit = gated[rows, :] * scale
        low_mixed_ref[rows, :] = (unit * gain).astype(BF16)
        d_mixed = mul_nt(out_weight[rows, :], incoming)
        gain_part_ref[rows, :] += fold(d_mixed * unit)
        d_unit = d_mixed * gain
        d_normed[rows, :] = d_unit
        return dots + eighths(d_unit * unit)

    dots = lax.fori_loop(0, inner // TILE, norm_tile, jnp.zeros((8, span), F32), unroll=3)
    mean_dot = jnp.sum(dots, axis=0, keepdims=True) / inner

    @pl.loop(0, heads // GROUP, unroll=HEADS_ABREAST)
    def _(group):
        eight = pl.ds(pl.multiple_of(group * GROUP, GROUP), GROUP)
        row_parts, skip_parts, d_gates = [], [], []
        for j in range(GROUP):
            h = group * GROUP + j
            rows = pl.ds(pl.multiple_of(h * width, width), width)
            z = gate[rows, :]
            sig = sigmoid(z)
            values = values_ref[rows, :].astype(F32)
            pure = scanned[rows, :]
            y = pure + skip_ref[h] * values
            d_gated = scale * (d_normed[rows, :] - gated[rows, :] * (scale * mean_dot))
            d_scan = (d_gated * (z * sig)).astype(BF16)
            d_scan_ref[rows, :] = d_scan
            d_gates.append(d_gated * y * (sig * (1.0 + z * (1.0 - sig))))
            if len(d_gates) * width == LANES:
                lanes = pl.ds(pl.multiple_of((h + 1) * width - LANES, LANES), LANES)
                d_gate_ref[:, lanes] = jnp.concatenate(d_gates, axis=0).T.astype(BF16)
                d_gates = []
            d_scan = d_scan.astype(F32)
            row_parts.append(jnp.sum(d_scan * pure, axis=0, keepdims=True))
            skip_parts.append(jnp.sum(d_scan * values, axis=0, keepdims=True))
        row_part_ref[eight, :] = jnp.concatenate(row_parts, axis=0)
        skip_part_ref[eight, :] = jnp.concatenate(skip_parts, axis=0)

    @pl.when(pl.program_id(0) == pl.num_programs(0) - 1)
    def _():
        kept.wait()


def backward_body(sizes, first_head, last, *refs):
    refs = list(refs)
    take = lambda n: [refs.pop(0) for _ in range(n)]
    skip_ref, active_ref, low_bc_ref = take(3)
    mixed_refs = take(2 if last else 1)
    before_refs = take(2 if last else 1)
    d_scan_ref, raw_ref, row_part_ref, states_ref, taps_ref, heads_ref = take(6)
    bc_part_ref, d_raw_before_ref, _ = take(3) if last else (None, None, None)
    d_rest_ref = take(1)[0]
    d_raw_ref, rate_part_ref, conv_part_ref = take(3)
    bc_out_ref = None if last else take(1)[0]
    (
        d_state,
        extended,
        d_extended,
        d_active,
        sums,
        from_state,
        push,
        scaled,
        d_scaled,
        d_scores,
        state_dots,
        cum_s,
        step_s,
        factor_s,
        ec_s,
        total_s,
        pair_s,
        direct_s,
        ending_s,
    ) = refs
    all_inner, conv, all_heads, state_dim = sizes
    inner, span = active_ref.shape
    width = all_inner // all_heads
    heads = inner // width
    tiles = [(ref, before, t) for ref, before in zip(mixed_refs, before_refs) for t in range(ref.shape[1] // LANES)]
    first_tiles = [first_head * width // LANES, all_inner // LANES]
    stretch = min(STRETCH, span)
    half = stretch // 2
    first_block = pl.program_id(0) == pl.num_programs(0) - 1

    @pl.when(pl.program_id(0) == 0)
    def _():
        d_state[...] = jnp.zeros_like(d_state)
        d_extended[:, :8, :] = jnp.zeros((len(tiles), 8, LANES), F32)
        sums[...] = jnp.zeros_like(sums)

    raw = raw_ref[...]
    step_all = softplus(raw)
    slope = sigmoid(raw)
    rate = -jnp.exp(heads_ref[first_head : first_head + heads, 1:2])
    rate2 = rate * LOG2E
    causal = triangle(stretch, lambda r, c: r <= c)
    ending = triangle(stretch, lambda r, c: r >= c).astype(BF16)
    before_it = triangle(stretch, lambda r, c: r < c).astype(BF16)
    for part in reversed(range(span // stretch)):
        lanes = slice(part * stretch, (part + 1) * stretch)
        step = step_all[:, lanes]
        cum, factor, ec, total = decays(step, rate2)
        cum_s[...] = cum
        step_s[...] = step
        factor_s[...] = factor
        ec_s[...] = ec
        total_s[...] = jnp.broadcast_to(total, (heads, LANES))
        b_in = low_bc_ref[:state_dim, lanes]
        c_in = low_bc_ref[state_dim:, lanes]
        scores = jnp.where(causal, mul_tn(b_in, c_in), 0.0)
        low_d_state = d_state[...].astype(BF16)
        from_state[...] = mul_nn(low_d_state, b_in)
        d_scores[...] = jnp.zeros_like(d_scores)

        @pl.loop(0, heads // GROUP, unroll=HEADS_ABREAST)
        def _(group):
            eight = pl.ds(pl.multiple_of(group * GROUP, GROUP), GROUP)
            cum_g, step_g, factor_g, ec_g = cum_s[eight, :], step_s[eight, :], factor_s[eight, :], ec_s[eight, :]
            cum_c = as_columns(cum_g)
            pairs, directs, endings, dots = [], [], [], []
            d_early, d_late = d_scores[:half, :], d_scores[half:, half:]
            for j in range(GROUP):
                h = group * GROUP + j
                rows = pl.ds(pl.multiple_of(h * width, width), width)
                row = slice(j, j + 1)
                values = active_ref[rows, lanes].astype(F32)
                stepped = (values * step_g[row]).astype(BF16)
                low_d = d_scan_ref[rows, lanes]
                d_scan = low_d.astype(F32)
                early = decay_between(cum_g[row], cum_c[:half, row])
                late = decay_between(cum_g[row, half:], cum_c[half:, row])
                inside = jnp.concatenate(
                    [
                        mul_nt(low_d, (scores[:half] * early).astype(BF16)),
                        mul_nt(low_d[:, half:], (scores[half:, half:] * late).astype(BF16)),
                    ],
                    axis=1,
                )
                d_early = d_early + mul_tn(stepped[:, :half], low_d) * early
                d_late = d_late + mul_tn(stepped[:, half:], low_d[:, half:]) * late
                across = from_state[rows, :] * factor_g[row]
                both = inside + across
                d_active[rows, lanes] = step_g[row] * both + skip_ref[first_head + h] * d_scan
                pairs.append(jnp.sum(stepped.astype(F32) * inside, axis=0, keepdims=True))
                directs.append(jnp.sum(values * both, axis=0, keepdims=True))
                endings.append(jnp.sum(values * across, axis=0, keepdims=True))
                scaled[rows, :] = (values * (step_g[row] * factor_g[row])).astype(BF16)
                d_scaled[rows, :] = (d_scan * ec_g[row]).astype(BF16)
                dots.append(jnp.sum(d_state[rows, :] * states_ref[part, rows, :].astype(F32), axis=0, keepdims=True))
            d_scores[:half, :] = d_early
            d_scores[half:, half:] = d_late
            pair_s[eight, :] = jnp.concatenate(pairs, axis=0)
            direct_s[eight, :] = jnp.concatenate(directs, axis=0)
            ending_s[eight, :] = jnp.concatenate(endings, axis=0)
            state_dots[eight, :] = jnp.concatenate(dots, axis=0)

        low_d_scores = jnp.where(causal, d_scores[...], 0.0).astype(BF16)
        low_state = states_ref[part]
        d_b = mul_tn(low_d_state, scaled[...]) + mul_nt(c_in, low_d_scores)
        d_c = mul_tn(low_state, d_scaled[...]) + mul_nn(b_in, low_d_scores)
        if last:
            d_active[inner : inner + state_dim, lanes] = d_b + bc_part_ref[:state_dim, lanes]
            d_active[inner + state_dim :, lanes] = d_c + bc_part_ref[state_dim:, lanes]
        else:
            bc_out_ref[:state_dim, lanes] = d_b
            bc_out_ref[state_dim:, lanes] = d_c
        push[...] = mul_nt(d_scaled[...], c_in)

        @pl.loop(0, heads // GROUP, unroll=HEADS_ABREAST)
        def _(group):
            eight = pl.ds(pl.multiple_of(group * GROUP, GROUP), GROUP)
            total_g = total_s[eight, :]
            for j in range(GROUP):
                rows = pl.ds(pl.multiple_of((group * GROUP + j) * width, width), width)
                d_state[rows, :] = total_g[j : j + 1] * d_state[rows, :] + push[rows, :]

        d_log = (
            lane_sums(row_part_ref[:, lanes] - pair_s[...], ending)
            + lane_sums(step * ending_s[...], before_it)
            + total * jnp.sum(state_dots[...], axis=1, keepdims=True)
        )
        rate_part_ref[:, lanes] = d_log * step * rate
        d_raw_ref[:, lanes] = (direct_s[...] + d_log * rate) * slope[:, lanes]

    for index, (mixed_ref, before_ref, tile) in enumerate(tiles):
        lanes = slice(tile * LANES, (tile + 1) * LANES)
        active_rows = slice(index * LANES, (index + 1) * LANES)
        before = before_ref[:, lanes].astype(F32)[8:]
        extended[index, :8, :] = jnp.where(first_block, 0.0, before)
        extended[index, 8:, :] = mixed_ref[:, lanes].astype(F32)
        taps = taps_ref[first_tiles[0] + index if mixed_ref is mixed_refs[0] else first_tiles[1] + tile]
        moved = [extended[index, 8 - shift : 8 - shift + span, :] for shift in range(4)]
        summed = taps[4:5] + moved[0] * taps[3:4]
        for shift in range(1, 4):
            summed = summed + moved[shift] * taps[3 - shift : 4 - shift]
        sig = sigmoid(summed)
        d_summed = d_active[active_rows, :].T * (sig * (1.0 + summed * (1.0 - sig)))
        d_extended[index, span:, :] = d_extended[index, :8, :]
        d_extended[index, :span, :] = d_summed
        d_block = d_summed * taps[3:4]
        for shift in range(1, 4):
            d_block = d_block + d_extended[index, shift : shift + span, :] * taps[3 - shift : 4 - shift]
        d_rest_ref[:, active_rows] = d_block.astype(BF16)
        for shift in range(4):
            sums[3 - shift, index] += eighths(d_summed * moved[shift])
        sums[4, index] += eighths(d_summed)

    if last:
        d_raw = jnp.concatenate([d_raw_before_ref[...], d_raw_ref[...]], axis=0)
        done = len(tiles) * LANES
        d_rest_ref[:, done : done + LANES] = as_columns(d_raw).astype(BF16)
        d_rest_ref[:, done + LANES :] = jnp.zeros((span, d_rest_ref.shape[1] - done - LANES), BF16)

    @pl.when(first_block)
    def _():
        for k in range(5):
            conv_part_ref[k] = jnp.sum(sums[k], axis=1)


def whole(shape):
    return pl.BlockSpec(shape, lambda c: (0,) * len(shape), pipeline_mode=pl.Buffered(1))


ANYWHERE = pl.BlockSpec(memory_space=pl.ANY)
SCALARS = pl.BlockSpec(memory_space=pltpu.SMEM)


def kernel_options(microseconds):
    return dict(
        compiler_params=pltpu.CompilerParams(
            dimension_semantics=("arbitrary",), vmem_limit_bytes=VMEM_LIMIT
        ),
        cost_estimate=pl.CostEstimate(
            flops=microseconds * 10**9, bytes_accessed=microseconds * 10**6, transcendentals=0
        ),
    )


def forward(sizes, places, tokens, gain, raw_weight, taps, heads_in, pieces, lengths):
    inner, conv, heads, state_dim = sizes
    length, model = tokens.shape
    span = min(SPAN, length)
    stretch = min(STRETCH, span)
    parts = span // stretch
    along = lambda rows: pl.BlockSpec((rows, span), lambda c: (0, c))
    down = lambda columns: pl.BlockSpec((span, columns), lambda c: (c, 0))
    shape = jax.ShapeDtypeStruct
    return pl.pallas_call(
        functools.partial(forward_body, sizes, tuple(lengths)),
        grid=(length // span,),
        in_specs=[
            SCALARS,
            down(model),
            whole(gain.shape),
            whole(raw_weight.shape),
            whole(taps.shape),
            whole(heads_in.shape),
        ]
        + [ANYWHERE] * len(pieces),
        out_specs=[
            down(model),
            down(conv),
            along(conv),
            along(heads),
            pl.BlockSpec((parts, inner, state_dim), lambda c: (c, 0, 0)),
            along(inner),
            along(inner),
            ANYWHERE,
        ],
        out_shape=[
            shape((length, model), BF16),
            shape((length, conv), BF16),
            shape((conv, length), BF16),
            shape((heads, length), F32),
            shape((length // stretch, inner, state_dim), BF16),
            shape((inner, length), F32),
            shape((inner, length), F32),
            shape((inner + conv + SPARE, model), BF16),
        ],
        scratch_shapes=[
            pltpu.VMEM((inner + conv + SPARE, model), BF16),
            pltpu.VMEM((inner, state_dim), F32),
            pltpu.VMEM((conv // LANES, span + 8, LANES), F32),
            pltpu.VMEM((inner, stretch), F32),
            pltpu.VMEM((inner, stretch), BF16),
            pltpu.VMEM((inner, state_dim), F32),
            pltpu.VMEM((heads, stretch), F32),
            pltpu.VMEM((heads, stretch), F32),
            pltpu.VMEM((heads, stretch), F32),
            pltpu.VMEM((heads, stretch), F32),
            pltpu.VMEM((heads, LANES), F32),
            pltpu.SemaphoreType.DMA((len(pieces) + 1,)),
        ],
        name="block_forward",
        **kernel_options(30),
    )(places, tokens, gain, raw_weight, taps, heads_in, *pieces)


def gated(sizes, places, skip, alive, cotangent, inner_gain, gate, scanned, active, pieces, lengths):
    inner, conv, heads, state_dim = sizes
    length, model = cotangent.shape
    span = min(SPAN, length)
    along = lambda rows: pl.BlockSpec((rows, span), lambda c: (0, c))
    shape = jax.ShapeDtypeStruct
    return pl.pallas_call(
        functools.partial(gated_body, sizes, tuple(lengths)),
        grid=(length // span,),
        in_specs=[
            SCALARS,
            SCALARS,
            SCALARS,
            pl.BlockSpec((span, model), lambda c: (c, 0)),
            whole(inner_gain.shape),
            along(inner),
            along(inner),
            along(inner),
        ]
        + [ANYWHERE] * len(pieces),
        out_specs=[
            along(inner),
            pl.BlockSpec((span, inner), lambda c: (c, 0)),
            along(inner),
            along(heads),
            along(heads),
            pl.BlockSpec((inner, LANES), lambda c: (0, 0)),
            ANYWHERE,
        ],
        out_shape=[
            shape((inner, length), BF16),
            shape((length, inner), BF16),
            shape((inner, length), BF16),
            shape((heads, length), F32),
            shape((heads, length), F32),
            shape((inner, LANES), F32),
            shape((inner, model), BF16),
        ],
        scratch_shapes=[
            pltpu.VMEM((inner, model), BF16),
            pltpu.VMEM((inner, span), F32),
            pltpu.VMEM((inner, span), F32),
            pltpu.SemaphoreType.DMA((len(pieces) + 1,)),
        ],
        name="block_gated",
        **kernel_options(15),
    )(places, skip, alive, cotangent, inner_gain, gate, scanned, active, *pieces)


def input_body(alive_ref, tokens_ref, cotangent_ref, gain_ref, d_gate_ref, d_rest_ref, weight_ref, grad_ref, gain_part_ref):
    @pl.when(pl.program_id(0) == 0)
    def _():
        gain_part_ref[...] = jnp.zeros_like(gain_part_ref)

    inner = d_gate_ref.shape[1]
    d_normed = mul_nn(d_gate_ref[...], weight_ref[:inner, :]) + mul_nn(d_rest_ref[...], weight_ref[inner:, :])
    u = tokens_ref[...].astype(F32)
    scale = lax.rsqrt(jnp.mean(u * u, axis=1, keepdims=True) + EPSILON)
    unit = u * scale
    gain_part_ref[...] += eighths(d_normed * unit)
    d_unit = d_normed * gain_ref[...]
    slope = scale * (d_unit - unit * jnp.mean(d_unit * unit, axis=1, keepdims=True))
    grad_ref[...] = cotangent_ref[...].astype(F32) * alive_ref[0] + slope


def input_backward(alive, tokens, cotangent, gain, d_gate, d_rest, weight):
    length, model = tokens.shape
    span = min(SPAN, length)
    down = lambda columns: pl.BlockSpec((span, columns), lambda c: (c, 0))
    shape = jax.ShapeDtypeStruct
    return pl.pallas_call(
        input_body,
        grid=(length // span,),
        in_specs=[
            SCALARS,
            down(model),
            down(model),
            whole(gain.shape),
            down(d_gate.shape[1]),
            down(d_rest.shape[1]),
            whole(weight.shape),
        ],
        out_specs=[down(model), pl.BlockSpec((8, model), lambda c: (0, 0))],
        out_shape=[shape((length, model), F32), shape((8, model), F32)],
        name="input_backward",
        **kernel_options(8),
    )(alive, tokens, cotangent, gain, d_gate, d_rest, weight)


def backward(sizes, first_head, heads, skip, active, mixed, d_scan, raw, row_part, states, taps, heads_in, earlier):
    all_inner, conv, all_heads, state_dim = sizes
    width = all_inner // all_heads
    inner = heads * width
    last = first_head + heads == all_heads
    length = active.shape[1]
    span = min(SPAN, length)
    stretch = min(STRETCH, span)
    parts = span // stretch
    blocks = length // span
    per = span // 16
    at = first_head // heads
    bc = conv - all_inner
    bc_at = all_inner // bc
    along = lambda rows, index: pl.BlockSpec((rows, span), lambda c: (index, blocks - 1 - c))
    down = lambda columns, index: pl.BlockSpec((span, columns), lambda c: (blocks - 1 - c, index))
    ahead = lambda columns, index: pl.BlockSpec(
        (16, columns), lambda c: (jnp.maximum((blocks - 1 - c) * per - 1, 0), index)
    )
    shape = jax.ShapeDtypeStruct
    tiles = (inner + (bc if last else 0)) // LANES
    share = first_head * width if last else inner
    results = pl.pallas_call(
        functools.partial(backward_body, sizes, first_head, last),
        grid=(blocks,),
        in_specs=[SCALARS, along(inner, at), along(bc, bc_at), down(inner, at)]
        + [down(bc, bc_at)] * last
        + [ahead(inner, at)]
        + [ahead(bc, bc_at)] * last
        + [
            along(inner, at),
            along(heads, at),
            along(heads, at),
            pl.BlockSpec((parts, inner, state_dim), lambda c: (blocks - 1 - c, at, 0)),
            whole(taps.shape),
            whole(heads_in.shape),
        ]
        + [along(bc, 0), along(first_head, 0), ANYWHERE] * last,
        out_specs=[down(share, 1 if last else 0)]
        + [along(heads, 0), along(heads, 0), pl.BlockSpec((5, tiles, LANES), lambda c: (0, 0, 0))]
        + [along(bc, 0)] * (not last),
        out_shape=[shape((length, 2 * share), BF16)]
        + [shape((heads, length), F32), shape((heads, length), F32), shape((5, tiles, LANES), F32)]
        + [shape((bc, length), F32)] * (not last),
        scratch_shapes=[
            pltpu.VMEM((inner, state_dim), F32),
            pltpu.VMEM((tiles, span + 8, LANES), F32),
            pltpu.VMEM((tiles, span + 8, LANES), F32),
            pltpu.VMEM((tiles * LANES, span), F32),
            pltpu.VMEM((5, tiles, 8, LANES), F32),
            pltpu.VMEM((inner, stretch), F32),
            pltpu.VMEM((inner, state_dim), F32),
            pltpu.VMEM((inner, stretch), BF16),
            pltpu.VMEM((inner, stretch), BF16),
            pltpu.VMEM((stretch, stretch), F32),
            pltpu.VMEM((heads, state_dim), F32),
            pltpu.VMEM((heads, stretch), F32),
            pltpu.VMEM((heads, stretch), F32),
            pltpu.VMEM((heads, stretch), F32),
            pltpu.VMEM((heads, stretch), F32),
            pltpu.VMEM((heads, LANES), F32),
            pltpu.VMEM((heads, stretch), F32),
            pltpu.VMEM((heads, stretch), F32),
            pltpu.VMEM((heads, stretch), F32),
        ],
        input_output_aliases={3 + 2 * 2 + 6 + 2: 0} if last else {},
        name="block_backward",
        **kernel_options(4 + heads),
    )(
        skip,
        active,
        active,
        *[mixed] * (2 + 2 * last),
        d_scan,
        raw,
        row_part,
        states,
        taps,
        heads_in,
        *((earlier[-1], earlier[1], earlier[0]) if last else ()),
    )
    return results


def powers_of_two(size):
    bits, bit = [], 1
    while bit < size:
        bits.append(bit)
        bit *= 2
    return bits if bit == size else None


def swap(block, axis, bit):
    pairs = [(k, k ^ bit) for k in range(lax.axis_size(axis))]
    return lax.ppermute(block, axis, pairs)


def cut(block, index, pieces, axis=0):
    size = block.shape[axis] // pieces
    return lax.dynamic_slice_in_dim(block, index * size, size, axis)


def halve(block, axis, bit):
    side = (lax.axis_index(axis) // bit) % 2
    got = swap(cut(block, 1 - side, 2), axis, bit)
    return (cut(block, side, 2).astype(F32) + got.astype(F32)).astype(block.dtype)


def double(block, axis, bit):
    side = (lax.axis_index(axis) // bit) % 2
    other = swap(block, axis, bit)
    return jnp.where(
        side == 0, jnp.concatenate([block, other], axis=0), jnp.concatenate([other, block], axis=0)
    )


def pair_sum(product, core):
    return added(product(core), swap(product(1 - core).astype(BF16), "dp", 1))


def after(value, *earlier):
    return lax.optimization_barrier((value, *earlier))[0]


def added(keep, got):
    return (keep.astype(F32) + got.astype(F32)).astype(BF16)


def together(*arrays):
    return lax.optimization_barrier(arrays)


def sides(block, axis, bit):
    side = (lax.axis_index(axis) // bit) % 2
    return cut(block, side, 2), cut(block, 1 - side, 2)


def joined(block, other, side, axis=0):
    return jnp.where(
        side == 0, jnp.concatenate([block, other], axis), jnp.concatenate([other, block], axis)
    )


def pair_sum(product, core):
    return added(product(core), swap(product(1 - core).astype(BF16), "dp", 1))


def after(value, *earlier):
    return lax.optimization_barrier((value, *earlier))[0]


def added(keep, got):
    return (keep.astype(F32) + got.astype(F32)).astype(BF16)


class Chain:
    def __init__(self, keep, give, axis, bit):
        self.keep, self.give, self.axis, self.bit = keep, give, axis, bit

    def start(self):
        self.got = swap(self.give, self.axis, self.bit)
        return self.give

    def finish(self, *beside):
        return added(self.keep, after(self.got, *beside) if beside else self.got)


def halving(block, axis, bit):
    side = (lax.axis_index(axis) // bit) % 2
    return Chain(cut(block, side, 2), cut(block, 1 - side, 2), axis, bit)


def spread(block, bits):
    for bit in reversed(bits):
        block = double(block, "dp", bit)
    return block


class Plain:
    def __init__(self):
        self.groups = lax.axis_size("fsdp")
        self.mine = lax.axis_index("fsdp")

    def gather(self, w_in, packed, w_out, main, prepare):
        by_group = lax.all_gather(w_in.T, "fsdp")
        weight = by_group.transpose(1, 0, 2).reshape(by_group.shape[1], -1)
        out_weight = lax.all_gather(w_out, "fsdp", tiled=True)
        here = jnp.zeros((2,), jnp.int32)
        sizes = [main], [out_weight.shape[0]]
        return (
            ([weight], here, sizes[0]),
            weight[main:],
            prepare(lax.all_gather(packed, "fsdp")),
            ([out_weight], here, sizes[1]),
        )

    def late(self, pieces, places, lengths, earlier):
        return pieces, places, lengths

    def own(self, total, axis):
        return cut(total, self.mine, self.groups, axis).astype(F32)

    def sums(self, low_mixed, incoming, d_gate, normed, kernels, columns, fillers):
        everywhere = lambda term, axis: self.own(lax.psum(term.astype(BF16), ("fsdp", "dp")), axis)
        g_out = everywhere(mul_nn(low_mixed, incoming), 0)
        g_rows, results = [everywhere(mul_tn(d_gate, normed), 1)], []
        for kernel in kernels:
            results.append(kernel(results))
        rest = results[-1][0]
        g_rows.append(everywhere(mul_tn(rest[:, :columns], normed), 1))
        block_out = fillers[0](d_gate)
        input_grad, small = fillers[1](results, rest, d_gate)
        total = cut(lax.psum(small, ("fsdp", "dp")), self.mine, self.groups)[0]
        return g_out, g_rows, fillers[2](total), input_grad, block_out


class Paired:
    def __init__(self):
        self.mine = lax.axis_index("fsdp")
        self.core = lax.axis_index("dp") % 2
        self.bits = powers_of_two(lax.axis_size("dp"))

    def gather(self, w_in, packed, w_out, main, prepare):
        mine, core = self.mine, self.core
        rows = w_in.T
        columns = rows.shape[1]
        last = jnp.pad(rows[main:], ((0, 32 - (rows.shape[0] - main)), (0, 0)))
        half = main // 2
        outer = half // 48 * 16
        middle = half - 2 * outer
        near = self.bits[1]
        side = (lax.axis_index("dp") // near) % 2
        first_row = core * half
        row = lambda where: first_row + jnp.where(side == where, 0, outer + middle)
        part = lambda start, count: lax.dynamic_slice_in_dim(rows, start, count, 0)
        other_packed = swap(packed, "fsdp", 1)
        mine_outer = swap(jnp.concatenate([part(row(0), outer), last], axis=0), "fsdp", 1)
        mine_middle = swap(after(part(first_row + outer, middle), mine_outer), "fsdp", 1)
        near_outer = swap(mine_outer, "dp", near)
        in_order = lambda a, b, axis: jnp.where(
            mine == 0, jnp.concatenate([a, b], axis), jnp.concatenate([b, a], axis)
        )
        raw_weight = in_order(last, mine_outer[outer:], 1)
        prepared = prepare(in_order(packed[None], other_packed[None], 0))
        raw_weight, *prepared = together(raw_weight, *prepared, mine_middle)[:-1]
        core_outer = swap(after(mine_outer, near_outer, mine_middle, raw_weight, *prepared), "dp", 1)
        core_middle = swap(mine_middle, "dp", 1)
        core_near = swap(near_outer, "dp", 1)
        there = (1 - mine) * columns
        across = half - 2 * first_row
        places = [0, mine * columns]
        for start in (row(0), first_row + outer, row(1)):
            places += [start, there, start + across, there]
        places = jnp.stack(places).astype(jnp.int32)
        pieces = [rows, mine_outer, core_outer, mine_middle, core_middle, near_outer, core_near]
        lengths = [main, outer, outer, middle, middle, outer, outer]
        relayed = core_near

        each = w_out.shape[0]
        direct_out = swap(after(cut(w_out, core, 2), relayed), "fsdp", 1)
        other = (1 - mine) * each
        places_out = jnp.stack(
            [mine * each, 0, other + core * (each // 2), 0, other + (1 - core) * (each // 2), 0]
        ).astype(jnp.int32)
        return (
            (pieces, places, lengths),
            raw_weight,
            prepared,
            ([w_out, direct_out], places_out, [each, each // 2, each // 2]),
        )

    def late(self, pieces, places, lengths, earlier):
        own, direct = pieces
        direct = after(direct, earlier)
        return [own, direct, swap(direct, "dp", 1)], places, lengths

    def sums(self, low_mixed, incoming, d_gate, normed, kernels, columns, fillers):
        mine, core, (near, *far) = self.mine, self.core, self.bits[1:]
        near_side = (lax.axis_index("dp") // near) % 2
        owned = lambda block: (cut(block, mine, 2, 1), cut(block, 1 - mine, 2, 1))
        across = lambda give: swap(give, "fsdp", 1)
        over = lambda give, bit: swap(give, "dp", bit)

        def by_cores(term, axis):
            return cut(term, core, 2, axis), swap(cut(term, 1 - core, 2, axis), "dp", 1)

        out_keep, out_got = by_cores(mul_nn(low_mixed, incoming).astype(BF16), 1)
        gate_term = mul_tn(d_gate, normed).astype(BF16)
        out_got, gate_term = together(out_got, gate_term)
        out_block = added(out_keep, out_got)
        out_give = cut(out_block, 1 - mine, 2)
        got_out = across(out_give)
        gate_keep, gate_got = by_cores(after(gate_term, out_give), 0)
        gate_keep, gate_give = owned(added(gate_keep, gate_got))
        got_gate = across(gate_give)
        first = kernels[0]([], gate_give)
        got_out, got_gate, _ = together(got_out, got_gate, first[-1])
        keep_a = jnp.concatenate([cut(out_block, mine, 2), gate_keep], axis=0)
        got_a = jnp.concatenate([got_out, got_gate], axis=0)
        keep_a, give_a = sides(added(keep_a, got_a), "dp", near)
        got_a = over(give_a, near)
        second = kernels[1]([first], give_a)
        got_a, rest = together(got_a, second[0])
        keep_b, got_b = by_cores(mul_tn(rest[:, :columns], normed).astype(BF16), 0)
        block_b = added(keep_b, got_b)
        keep_b, give_b = owned(block_b)
        got_b = across(give_b)
        side = lambda bit: (lax.axis_index("dp") // bit) % 2
        results = [first, second]
        turn, wide = far[0], far[1:]

        keep_a, give_a = sides(added(keep_a, after(got_a, give_b)), "dp", turn)
        got_a = over(give_a, turn)
        block_out = fillers[0](after(give_b, give_a))
        got_a, block_out = together(got_a, block_out)
        block_a = added(keep_a, got_a)
        sent_a = [over(block_a, bit) for bit in wide[:1]]
        input_grad, small = fillers[1](results, rest, block_a)
        for bit in wide[1:]:
            block_a = added(block_a, sent_a.pop())
            sent_a = [over(block_a, bit)]
        *sent_a, got_b, small = together(*sent_a, got_b, small)
        if sent_a:
            block_a = added(block_a, sent_a[0])
        block_b = added(keep_b, got_b)

        keep_b, give_b = sides(block_b, "dp", near)
        got_b, got_a, got_s = together(over(give_b, near), over(block_a, turn), over(small, 1))
        block_a, small = joined(block_a, got_a, side(turn)), small + got_s
        spread_a = over(block_a, near)
        keep_b, give_b = sides(added(keep_b, got_b), "dp", turn)
        got_b, got_s = together(over(give_b, turn), over(small, near))
        block_b, small = added(keep_b, got_b), small + got_s
        for bit in wide:
            got_b, got_s = together(over(block_b, bit), over(small, bit))
            block_b, small = added(block_b, got_b), small + got_s
        got_b, got_s, spread_a = together(over(block_b, turn), over(small, turn), spread_a)
        block_b, small = joined(block_b, got_b, side(turn)), small + got_s
        block_a = joined(block_a, spread_a, side(near))
        got_b, got_s = together(over(block_b, near), across(cut(small, 1 - mine, 2)[0]))
        block_b, total = joined(block_b, got_b, side(near)), cut(small, mine, 2)[0] + got_s
        size = out_block.shape[0] // 2
        swapped_a, swapped_b, *g_small = together(swap(block_a, "dp", 1), swap(block_b, "dp", 1), *fillers[2](total))
        g_out = joined(block_a[:size], swapped_a[:size], core, 1).astype(F32)
        g_rows = [joined(block_a[size:], swapped_a[size:], core), joined(block_b, swapped_b, core)]
        return g_out, [rows.astype(F32) for rows in g_rows], g_small, input_grad, block_out


def shards(
    tokens,
    live,
    norm_gain,
    w_in,
    conv_weight,
    conv_bias,
    dt_bias,
    a_log,
    d_skip,
    inner_gain,
    w_out,
    cotangent,
):
    groups, copies = lax.axis_size("fsdp"), lax.axis_size("dp")
    taps = conv_weight.shape[1]
    heads = dt_bias.shape[0] * groups
    inner, conv = inner_gain.shape[0] * groups, conv_bias.shape[0] * groups
    model = tokens.shape[-1]
    proj = w_in.shape[1]
    main = inner + conv
    sizes = (inner, conv, heads, (conv - inner) // 2)
    paired = groups == 2 and powers_of_two(copies) and copies > 2 and main % 32 == 0
    links = Paired() if paired else Plain()

    rest = jnp.concatenate([norm_gain, dt_bias, a_log, d_skip])
    line = max(conv_bias.shape[0], inner_gain.shape[0], rest.shape[0])
    lined = lambda table: jnp.pad(table, ((0, 0), (0, line - table.shape[1])))
    packed = jnp.concatenate([lined(conv_weight.T), lined(conv_bias[None]), lined(inner_gain[None]), lined(rest[None])])

    def prepare(packed):
        packed = packed.astype(F32)
        pick = lambda row, first, each: packed[:, row, first : first + each].reshape(-1)
        model_each, heads_each = norm_gain.shape[0], dt_bias.shape[0]
        table = packed[:, : taps + 1, : conv // groups].transpose(1, 0, 2).reshape(taps + 1, conv)
        table = jnp.concatenate([table, jnp.zeros((7 - taps, conv), F32)], axis=0)
        taps_in = table.reshape(8, conv // LANES, LANES).transpose(1, 0, 2)
        inner_all = pick(taps + 1, 0, inner // groups)[:, None]
        gain_all = pick(taps + 2, 0, model_each)[None]
        by_head = [pick(taps + 2, model_each + k * heads_each, heads_each) for k in range(3)]
        return [taps_in, inner_all, gain_all, jnp.stack(by_head[:2], axis=1), by_head[2]]

    in_pieces, raw_weight, prepared, out_pieces = links.gather(w_in, packed, w_out, main, prepare)
    raw_weight = jnp.pad(raw_weight, ((0, 32 - raw_weight.shape[0]), (0, 0)))
    taps_in, inner_all, gain_all, heads_in, skip = prepared

    alive = live.astype(F32).reshape(1)
    low_tokens, low_cotangent = tokens[0, 0], cotangent[0, 0]
    normed, mixed, active, raw, states, gate, scanned, weight = forward(
        sizes, in_pieces[1], low_tokens, gain_all, raw_weight, taps_in, heads_in, in_pieces[0], in_pieces[2]
    )
    out_pieces = links.late(*out_pieces, normed)
    low_mixed, d_gate, d_scan, row_part, skip_part, gain_part, out_weight = gated(
        sizes, out_pieces[1], skip, alive, low_cotangent, inner_all, gate, scanned, active, out_pieces[0], out_pieces[2]
    )
    u = low_tokens.astype(F32)
    incoming = low_cotangent.astype(F32) * alive[0]

    def backward_step(first, count):
        def step(earlier, *sent):
            scan = after(d_scan, *sent) if sent else d_scan
            return backward(
                sizes,
                first,
                count,
                skip,
                active,
                mixed,
                scan,
                raw,
                row_part,
                states,
                taps_in,
                heads_in,
                earlier[-1] if earlier else None,
            )

        return step

    kernels = [backward_step(first, count) for first, count in HEAD_RANGES]

    step = 64
    rest_columns = -(-(proj - inner) // step) * step

    def input_part(results, rest, tie):
        d_raw, rate_part = [jnp.concatenate([result[k] for result in results], axis=0) for k in (1, 2)]
        conv_part = jnp.concatenate([result[3] for result in results], axis=1).reshape(taps + 1, conv)
        input_grad, gain_part_in = input_backward(
            alive, low_tokens, low_cotangent, gain_all, d_gate, after(rest, tie), weight
        )
        terms = [
            conv_part,
            jnp.sum(gain_part, axis=1)[None],
            jnp.sum(gain_part_in, axis=0)[None],
            jnp.sum(d_raw, axis=1)[None],
            jnp.sum(rate_part, axis=1)[None],
            jnp.sum(skip_part, axis=1)[None],
        ]
        by_owner = [
            jnp.moveaxis(term.reshape(term.shape[0], groups, -1), 1, 0).reshape(groups, -1) for term in terms
        ]
        count = sum(term.shape[1] for term in by_owner)
        by_owner.append(jnp.zeros((groups, -count % (8 * LANES)), F32))
        return input_grad, jnp.concatenate(by_owner, axis=1).reshape(groups, -1, LANES)

    def out_part(tie):
        branch = mul_tn(after(low_mixed, tie), out_weight)
        return (alive[0] * (u + branch)).astype(BF16)

    def small_grads(total):
        total = total.reshape(-1)
        shapes = [(taps + 1, conv), (1, inner), (1, model), (1, heads), (1, heads), (1, heads)]
        first, parts = 0, []
        for lines, line in shapes:
            size = lines * line // groups
            parts.append(total[first : first + size].reshape(lines, -1))
            first += size
        g_conv, g_inner, g_gain, g_bias, g_rate, g_skip = parts
        return [g_gain[0], g_conv[:taps].T, g_conv[taps], g_bias[0], g_rate[0], g_skip[0], g_inner[0]]

    g_out, g_rows, g_small, input_grad, block_out = links.sums(
        low_mixed,
        incoming.astype(BF16),
        d_gate,
        normed,
        kernels,
        rest_columns,
        [out_part, input_part, small_grads],
    )
    g_proj = jnp.concatenate([g_rows[0], g_rows[1][: proj - inner]], axis=0).T
    return (
        block_out.reshape(tokens.shape),
        input_grad.reshape(cotangent.shape),
        g_small[0],
        g_proj,
        *g_small[1:],
        g_out,
    )


def solution(mesh):
    by_device = P("fsdp", "dp", None, None)
    lines, tables = P("fsdp"), P("fsdp", None)
    return jax.shard_map(
        shards,
        mesh=mesh,
        in_specs=(
            by_device,
            P("fsdp", "dp"),
            lines,
            tables,
            tables,
            lines,
            lines,
            lines,
            lines,
            lines,
            tables,
            by_device,
        ),
        out_specs=(by_device, by_device, lines, tables, tables, lines, lines, lines, lines, lines, tables),
        check_vma=False,
    )
```

```python
import functools
import math

import jax
import jax.numpy as jnp
from jax import lax
from jax.experimental import pallas as pl
from jax.experimental.pallas import tpu as pltpu
from jax.sharding import PartitionSpec as P

EPSILON = 1e-05
LOG2E = math.log2(math.e)
SPAN = 256
STRETCH = 256
GROUP = 8
TILE = 256
LANES = 128
SPARE = 256
TILES_ABREAST = 7
HEADS_ABREAST = 2
HEAD_RANGES = ((0, 16), (16, 8))
VMEM_LIMIT = 60 * 1024 * 1024

F32 = jnp.float32
BF16 = jnp.bfloat16


def mul_nn(a, b):
    return lax.dot_general(a, b, (((1,), (0,)), ((), ())), preferred_element_type=F32)


def mul_nt(a, b):
    return lax.dot_general(a, b, (((1,), (1,)), ((), ())), preferred_element_type=F32)


def mul_tn(a, b):
    return lax.dot_general(a, b, (((0,), (0,)), ((), ())), preferred_element_type=F32)


def triangle(size, keep):
    rows = lax.broadcasted_iota(jnp.int32, (size, size), 0)
    cols = lax.broadcasted_iota(jnp.int32, (size, size), 1)
    return keep(rows, cols)


def lane_sums(values, matrix):
    high = values.astype(BF16)
    rest = values - high.astype(F32)
    middle = rest.astype(BF16)
    low = (rest - middle.astype(F32)).astype(BF16)
    return mul_nn(high, matrix) + mul_nn(middle, matrix) + mul_nn(low, matrix)


def as_columns(rows):
    heads, span = rows.shape
    return jnp.concatenate([rows, jnp.zeros((LANES - heads, span), F32)], axis=0).T


def fold(block):
    total = block[:, :LANES]
    for first in range(LANES, block.shape[1], LANES):
        total = total + block[:, first : first + LANES]
    return total


def eighths(block):
    return block.reshape(block.shape[0] // 8, 8, block.shape[1]).sum(axis=0)


def softplus(v):
    return jnp.maximum(v, 0.0) + jnp.log1p(jnp.exp(-jnp.abs(v)))


def sigmoid(v):
    return 0.5 * jnp.tanh(0.5 * v) + 0.5


def decay_between(later, earlier):
    return jnp.exp2(jnp.minimum(later - earlier, 0.0))


def decays(step, rate2):
    span = step.shape[1]
    upper = triangle(span, lambda r, c: r <= c).astype(BF16)
    cum = lane_sums(step * rate2, upper)
    total = cum[:, span - 1 : span]
    return cum, jnp.exp2(total - cum), jnp.exp2(cum), jnp.exp2(total)


def piece_copies(places_ref, lengths, pieces, whole_ref, sems):
    copies = []
    for k, piece in enumerate(pieces):
        rows, columns = lengths[k], piece.shape[1]
        target = whole_ref.at[
            pl.ds(pl.multiple_of(places_ref[2 * k], 16), rows),
            pl.ds(pl.multiple_of(places_ref[2 * k + 1], LANES), columns),
        ]
        copies.append(pltpu.make_async_copy(piece.at[pl.ds(0, rows), :], target, sems.at[k]))
    return copies


def forward_body(sizes, lengths, places_ref, tokens_ref, gain_ref, raw_weight_ref, taps_ref, heads_ref, *refs):
    n_pieces = len(lengths)
    pieces, refs = refs[:n_pieces], refs[n_pieces:]
    (
        normed_ref,
        mixed_ref,
        active_ref,
        raw_ref,
        states_ref,
        gate_ref,
        scanned_ref,
        weight_ref,
        weight,
        state,
        extended,
        carried,
        scaled,
        update,
        cum_s,
        step_s,
        factor_s,
        ec_s,
        total_s,
        sems,
    ) = refs
    inner, conv, heads, state_dim = sizes
    width = inner // heads
    span = tokens_ref.shape[0]
    stretch = min(STRETCH, span)
    half = stretch // 2
    copies = piece_copies(places_ref, lengths, pieces, weight, sems)
    kept = pltpu.make_async_copy(weight, weight_ref, sems.at[n_pieces])

    @pl.when(pl.program_id(0) == 0)
    def _():
        for copy in copies:
            copy.start()
        state[...] = jnp.zeros_like(state)
        extended[:, span:, :] = jnp.zeros((conv // LANES, 8, LANES), F32)

    u = tokens_ref[...].astype(F32)
    normed = u * lax.rsqrt(jnp.mean(u * u, axis=1, keepdims=True) + EPSILON) * gain_ref[...]
    normed = normed.astype(BF16)
    normed_ref[...] = normed

    @pl.when(pl.program_id(0) == 0)
    def _():
        for copy in copies:
            copy.wait()
        steps = raw_weight_ref.shape[0]
        weight[inner + conv : inner + conv + steps, :] = raw_weight_ref[...]
        weight[inner + conv + steps :, :] = jnp.zeros((SPARE - steps, weight.shape[1]), BF16)
        kept.start()

    @pl.loop(0, inner // TILE, unroll=6)
    def _(i):
        rows = pl.ds(pl.multiple_of(i * TILE, TILE), TILE)
        gate_ref[rows, :] = mul_nt(weight[rows, :], normed)

    @pl.loop(0, conv // TILE, unroll=TILES_ABREAST)
    def _(i):
        first = pl.multiple_of(i * TILE, TILE)
        wide = mul_nt(normed, weight[pl.ds(pl.multiple_of(inner + first, TILE), TILE), :])
        for k in range(TILE // LANES):
            index = i * (TILE // LANES) + k
            block = wide[:, k * LANES : (k + 1) * LANES]
            extended[index, :8, :] = extended[index, span:, :]
            extended[index, 8:, :] = block
            taps = taps_ref[index]
            summed = taps[4:5] + block * taps[3:4]
            for shift in range(1, 4):
                summed = summed + extended[index, 8 - shift : 8 - shift + span, :] * taps[3 - shift : 4 - shift]
            lanes = pl.ds(pl.multiple_of(first + k * LANES, LANES), LANES)
            mixed_ref[:, lanes] = block.astype(BF16)
            active_ref[lanes, :] = (summed * sigmoid(summed)).T.astype(BF16)

    raw = mul_nt(raw_weight_ref[...], normed)[:heads] + heads_ref[:, 0:1]
    raw_ref[...] = raw
    step_all = softplus(raw)
    rate2 = -jnp.exp(heads_ref[:, 1:2]) * LOG2E
    causal = triangle(stretch, lambda r, c: r <= c)
    for part in range(span // stretch):
        lanes = slice(part * stretch, (part + 1) * stretch)
        step = step_all[:, lanes]
        cum, factor, ec, total = decays(step, rate2)
        cum_s[...] = cum
        step_s[...] = step
        factor_s[...] = factor * step
        ec_s[...] = ec
        total_s[...] = jnp.broadcast_to(total, (heads, LANES))
        b_in = active_ref[inner : inner + state_dim, lanes]
        c_in = active_ref[inner + state_dim : inner + 2 * state_dim, lanes]
        scores = jnp.where(causal, mul_tn(b_in, c_in), 0.0)
        low_state = state[...].astype(BF16)
        states_ref[part] = low_state
        carried[...] = mul_nn(low_state, c_in)

        @pl.loop(0, heads // GROUP, unroll=HEADS_ABREAST)
        def _(group):
            eight = pl.ds(pl.multiple_of(group * GROUP, GROUP), GROUP)
            cum_g, step_g, factor_g, ec_g = cum_s[eight, :], step_s[eight, :], factor_s[eight, :], ec_s[eight, :]
            cum_c = as_columns(cum_g)
            for j in range(GROUP):
                rows = pl.ds(pl.multiple_of((group * GROUP + j) * width, width), width)
                row = slice(j, j + 1)
                values = active_ref[rows, lanes].astype(F32)
                stepped = (values * step_g[row]).astype(BF16)
                early = (scores[:half] * decay_between(cum_g[row], cum_c[:half, row])).astype(BF16)
                late = (scores[half:, half:] * decay_between(cum_g[row, half:], cum_c[half:, row])).astype(BF16)
                inside = mul_nn(stepped[:, :half], early)
                inside = jnp.concatenate(
                    [inside[:, :half], inside[:, half:] + mul_nn(stepped[:, half:], late)], axis=1
                )
                scanned_ref[rows, lanes] = inside + ec_g[row] * carried[rows, :]
                scaled[rows, :] = (values * factor_g[row]).astype(BF16)

        update[...] = mul_nt(scaled[...], b_in)

        @pl.loop(0, heads // GROUP, unroll=HEADS_ABREAST)
        def _(group):
            eight = pl.ds(pl.multiple_of(group * GROUP, GROUP), GROUP)
            total_g = total_s[eight, :]
            for j in range(GROUP):
                rows = pl.ds(pl.multiple_of((group * GROUP + j) * width, width), width)
                state[rows, :] = total_g[j : j + 1] * state[rows, :] + update[rows, :]

    @pl.when(pl.program_id(0) == pl.num_programs(0) - 1)
    def _():
        kept.wait()


def gated_body(sizes, lengths, places_ref, skip_ref, alive_ref, cotangent_ref, inner_gain_ref, *refs):
    n_pieces = len(lengths)
    gate, scanned, values_ref = refs[:3]
    pieces, refs = refs[3 : 3 + n_pieces], refs[3 + n_pieces :]
    (
        low_mixed_ref,
        d_gate_ref,
        d_scan_ref,
        row_part_ref,
        skip_part_ref,
        gain_part_ref,
        out_weight_ref,
        out_weight,
        gated,
        d_normed,
        sems,
    ) = refs
    inner, conv, heads, state_dim = sizes
    width = inner // heads
    span = cotangent_ref.shape[0]
    copies = piece_copies(places_ref, lengths, pieces, out_weight, sems)
    kept = pltpu.make_async_copy(out_weight, out_weight_ref, sems.at[n_pieces])

    @pl.when(pl.program_id(0) == 0)
    def _():
        for copy in copies:
            copy.start()
        gain_part_ref[...] = jnp.zeros_like(gain_part_ref)

    def gated_head(h, squares):
        rows = pl.ds(pl.multiple_of(h * width, width), width)
        z = gate[rows, :]
        y = scanned[rows, :] + skip_ref[h] * values_ref[rows, :].astype(F32)
        v = y * (z * sigmoid(z))
        gated[rows, :] = v
        return squares + eighths(v * v)

    squares = lax.fori_loop(0, heads, gated_head, jnp.zeros((8, span), F32), unroll=4)
    scale = lax.rsqrt(jnp.sum(squares, axis=0, keepdims=True) / inner + EPSILON)

    @pl.when(pl.program_id(0) == 0)
    def _():
        for copy in copies:
            copy.wait()
        kept.start()

    incoming = (cotangent_ref[...].astype(F32) * alive_ref[0]).astype(BF16)

    def norm_tile(i, dots):
        rows = pl.ds(pl.multiple_of(i * TILE, TILE), TILE)
        gain = inner_gain_ref[rows, :]
        unit = gated[rows, :] * scale
        low_mixed_ref[rows, :] = (unit * gain).astype(BF16)
        d_mixed = mul_nt(out_weight[rows, :], incoming)
        gain_part_ref[rows, :] += fold(d_mixed * unit)
        d_unit = d_mixed * gain
        d_normed[rows, :] = d_unit
        return dots + eighths(d_unit * unit)

    dots = lax.fori_loop(0, inner // TILE, norm_tile, jnp.zeros((8, span), F32), unroll=3)
    mean_dot = jnp.sum(dots, axis=0, keepdims=True) / inner

    @pl.loop(0, heads // GROUP, unroll=HEADS_ABREAST)
    def _(group):
        eight = pl.ds(pl.multiple_of(group * GROUP, GROUP), GROUP)
        row_parts, skip_parts, d_gates = [], [], []
        for j in range(GROUP):
            h = group * GROUP + j
            rows = pl.ds(pl.multiple_of(h * width, width), width)
            z = gate[rows, :]
            sig = sigmoid(z)
            values = values_ref[rows, :].astype(F32)
            pure = scanned[rows, :]
            y = pure + skip_ref[h] * values
            d_gated = scale * (d_normed[rows, :] - gated[rows, :] * (scale * mean_dot))
            d_scan = (d_gated * (z * sig)).astype(BF16)
            d_scan_ref[rows, :] = d_scan
            d_gates.append(d_gated * y * (sig * (1.0 + z * (1.0 - sig))))
            if len(d_gates) * width == LANES:
                lanes = pl.ds(pl.multiple_of((h + 1) * width - LANES, LANES), LANES)
                d_gate_ref[:, lanes] = jnp.concatenate(d_gates, axis=0).T.astype(BF16)
                d_gates = []
            d_scan = d_scan.astype(F32)
            row_parts.append(jnp.sum(d_scan * pure, axis=0, keepdims=True))
            skip_parts.append(jnp.sum(d_scan * values, axis=0, keepdims=True))
        row_part_ref[eight, :] = jnp.concatenate(row_parts, axis=0)
        skip_part_ref[eight, :] = jnp.concatenate(skip_parts, axis=0)

    @pl.when(pl.program_id(0) == pl.num_programs(0) - 1)
    def _():
        kept.wait()


def backward_body(sizes, first_head, last, *refs):
    refs = list(refs)
    take = lambda n: [refs.pop(0) for _ in range(n)]
    skip_ref, active_ref, low_bc_ref = take(3)
    mixed_refs = take(2 if last else 1)
    before_refs = take(2 if last else 1)
    d_scan_ref, raw_ref, row_part_ref, states_ref, taps_ref, heads_ref = take(6)
    bc_part_ref, d_raw_before_ref, _ = take(3) if last else (None, None, None)
    d_rest_ref = take(1)[0]
    d_raw_ref, rate_part_ref, conv_part_ref = take(3)
    bc_out_ref = None if last else take(1)[0]
    (
        d_state,
        extended,
        d_extended,
        d_active,
        sums,
        from_state,
        push,
        scaled,
        d_scaled,
        d_scores,
        state_dots,
        cum_s,
        step_s,
        factor_s,
        ec_s,
        total_s,
        pair_s,
        direct_s,
        ending_s,
    ) = refs
    all_inner, conv, all_heads, state_dim = sizes
    inner, span = active_ref.shape
    width = all_inner // all_heads
    heads = inner // width
    tiles = [(ref, before, t) for ref, before in zip(mixed_refs, before_refs) for t in range(ref.shape[1] // LANES)]
    first_tiles = [first_head * width // LANES, all_inner // LANES]
    stretch = min(STRETCH, span)
    half = stretch // 2
    first_block = pl.program_id(0) == pl.num_programs(0) - 1

    @pl.when(pl.program_id(0) == 0)
    def _():
        d_state[...] = jnp.zeros_like(d_state)
        d_extended[:, :8, :] = jnp.zeros((len(tiles), 8, LANES), F32)
        sums[...] = jnp.zeros_like(sums)

    raw = raw_ref[...]
    step_all = softplus(raw)
    slope = sigmoid(raw)
    rate = -jnp.exp(heads_ref[first_head : first_head + heads, 1:2])
    rate2 = rate * LOG2E
    causal = triangle(stretch, lambda r, c: r <= c)
    ending = triangle(stretch, lambda r, c: r >= c).astype(BF16)
    before_it = triangle(stretch, lambda r, c: r < c).astype(BF16)
    for part in reversed(range(span // stretch)):
        lanes = slice(part * stretch, (part + 1) * stretch)
        step = step_all[:, lanes]
        cum, factor, ec, total = decays(step, rate2)
        cum_s[...] = cum
        step_s[...] = step
        factor_s[...] = factor
        ec_s[...] = ec
        total_s[...] = jnp.broadcast_to(total, (heads, LANES))
        b_in = low_bc_ref[:state_dim, lanes]
        c_in = low_bc_ref[state_dim:, lanes]
        scores = jnp.where(causal, mul_tn(b_in, c_in), 0.0)
        low_d_state = d_state[...].astype(BF16)
        from_state[...] = mul_nn(low_d_state, b_in)
        d_scores[...] = jnp.zeros_like(d_scores)

        @pl.loop(0, heads // GROUP, unroll=HEADS_ABREAST)
        def _(group):
            eight = pl.ds(pl.multiple_of(group * GROUP, GROUP), GROUP)
            cum_g, step_g, factor_g, ec_g = cum_s[eight, :], step_s[eight, :], factor_s[eight, :], ec_s[eight, :]
            cum_c = as_columns(cum_g)
            pairs, directs, endings, dots = [], [], [], []
            d_early, d_late = d_scores[:half, :], d_scores[half:, half:]
            for j in range(GROUP):
                h = group * GROUP + j
                rows = pl.ds(pl.multiple_of(h * width, width), width)
                row = slice(j, j + 1)
                values = active_ref[rows, lanes].astype(F32)
                stepped = (values * step_g[row]).astype(BF16)
                low_d = d_scan_ref[rows, lanes]
                d_scan = low_d.astype(F32)
                early = decay_between(cum_g[row], cum_c[:half, row])
                late = decay_between(cum_g[row, half:], cum_c[half:, row])
                inside = jnp.concatenate(
                    [
                        mul_nt(low_d, (scores[:half] * early).astype(BF16)),
                        mul_nt(low_d[:, half:], (scores[half:, half:] * late).astype(BF16)),
                    ],
                    axis=1,
                )
                d_early = d_early + mul_tn(stepped[:, :half], low_d) * early
                d_late = d_late + mul_tn(stepped[:, half:], low_d[:, half:]) * late
                across = from_state[rows, :] * factor_g[row]
                both = inside + across
                d_active[rows, lanes] = step_g[row] * both + skip_ref[first_head + h] * d_scan
                pairs.append(jnp.sum(stepped.astype(F32) * inside, axis=0, keepdims=True))
                directs.append(jnp.sum(values * both, axis=0, keepdims=True))
                endings.append(jnp.sum(values * across, axis=0, keepdims=True))
                scaled[rows, :] = (values * (step_g[row] * factor_g[row])).astype(BF16)
                d_scaled[rows, :] = (d_scan * ec_g[row]).astype(BF16)
                dots.append(jnp.sum(d_state[rows, :] * states_ref[part, rows, :].astype(F32), axis=0, keepdims=True))
            d_scores[:half, :] = d_early
            d_scores[half:, half:] = d_late
            pair_s[eight, :] = jnp.concatenate(pairs, axis=0)
            direct_s[eight, :] = jnp.concatenate(directs, axis=0)
            ending_s[eight, :] = jnp.concatenate(endings, axis=0)
            state_dots[eight, :] = jnp.concatenate(dots, axis=0)

        low_d_scores = jnp.where(causal, d_scores[...], 0.0).astype(BF16)
        low_state = states_ref[part]
        d_b = mul_tn(low_d_state, scaled[...]) + mul_nt(c_in, low_d_scores)
        d_c = mul_tn(low_state, d_scaled[...]) + mul_nn(b_in, low_d_scores)
        if last:
            d_active[inner : inner + state_dim, lanes] = d_b + bc_part_ref[:state_dim, lanes]
            d_active[inner + state_dim :, lanes] = d_c + bc_part_ref[state_dim:, lanes]
        else:
            bc_out_ref[:state_dim, lanes] = d_b
            bc_out_ref[state_dim:, lanes] = d_c
        push[...] = mul_nt(d_scaled[...], c_in)

        @pl.loop(0, heads // GROUP, unroll=HEADS_ABREAST)
        def _(group):
            eight = pl.ds(pl.multiple_of(group * GROUP, GROUP), GROUP)
            total_g = total_s[eight, :]
            for j in range(GROUP):
                rows = pl.ds(pl.multiple_of((group * GROUP + j) * width, width), width)
                d_state[rows, :] = total_g[j : j + 1] * d_state[rows, :] + push[rows, :]

        d_log = (
            lane_sums(row_part_ref[:, lanes] - pair_s[...], ending)
            + lane_sums(step * ending_s[...], before_it)
            + total * jnp.sum(state_dots[...], axis=1, keepdims=True)
        )
        rate_part_ref[:, lanes] = d_log * step * rate
        d_raw_ref[:, lanes] = (direct_s[...] + d_log * rate) * slope[:, lanes]

    for index, (mixed_ref, before_ref, tile) in enumerate(tiles):
        lanes = slice(tile * LANES, (tile + 1) * LANES)
        active_rows = slice(index * LANES, (index + 1) * LANES)
        before = before_ref[:, lanes].astype(F32)[8:]
        extended[index, :8, :] = jnp.where(first_block, 0.0, before)
        extended[index, 8:, :] = mixed_ref[:, lanes].astype(F32)
        taps = taps_ref[first_tiles[0] + index if mixed_ref is mixed_refs[0] else first_tiles[1] + tile]
        moved = [extended[index, 8 - shift : 8 - shift + span, :] for shift in range(4)]
        summed = taps[4:5] + moved[0] * taps[3:4]
        for shift in range(1, 4):
            summed = summed + moved[shift] * taps[3 - shift : 4 - shift]
        sig = sigmoid(summed)
        d_summed = d_active[active_rows, :].T * (sig * (1.0 + summed * (1.0 - sig)))
        d_extended[index, span:, :] = d_extended[index, :8, :]
        d_extended[index, :span, :] = d_summed
        d_block = d_summed * taps[3:4]
        for shift in range(1, 4):
            d_block = d_block + d_extended[index, shift : shift + span, :] * taps[3 - shift : 4 - shift]
        d_rest_ref[:, active_rows] = d_block.astype(BF16)
        for shift in range(4):
            sums[3 - shift, index] += eighths(d_summed * moved[shift])
        sums[4, index] += eighths(d_summed)

    if last:
        d_raw = jnp.concatenate([d_raw_before_ref[...], d_raw_ref[...]], axis=0)
        done = len(tiles) * LANES
        d_rest_ref[:, done : done + LANES] = as_columns(d_raw).astype(BF16)
        d_rest_ref[:, done + LANES :] = jnp.zeros((span, d_rest_ref.shape[1] - done - LANES), BF16)

    @pl.when(first_block)
    def _():
        for k in range(5):
            conv_part_ref[k] = jnp.sum(sums[k], axis=1)


def whole(shape):
    return pl.BlockSpec(shape, lambda c: (0,) * len(shape), pipeline_mode=pl.Buffered(1))


ANYWHERE = pl.BlockSpec(memory_space=pl.ANY)
SCALARS = pl.BlockSpec(memory_space=pltpu.SMEM)


def kernel_options(microseconds):
    return dict(
        compiler_params=pltpu.CompilerParams(
            dimension_semantics=("arbitrary",), vmem_limit_bytes=VMEM_LIMIT
        ),
        cost_estimate=pl.CostEstimate(
            flops=microseconds * 10**9, bytes_accessed=microseconds * 10**6, transcendentals=0
        ),
    )


def forward(sizes, places, tokens, gain, raw_weight, taps, heads_in, pieces, lengths):
    inner, conv, heads, state_dim = sizes
    length, model = tokens.shape
    span = min(SPAN, length)
    stretch = min(STRETCH, span)
    parts = span // stretch
    along = lambda rows: pl.BlockSpec((rows, span), lambda c: (0, c))
    down = lambda columns: pl.BlockSpec((span, columns), lambda c: (c, 0))
    shape = jax.ShapeDtypeStruct
    return pl.pallas_call(
        functools.partial(forward_body, sizes, tuple(lengths)),
        grid=(length // span,),
        in_specs=[
            SCALARS,
            down(model),
            whole(gain.shape),
            whole(raw_weight.shape),
            whole(taps.shape),
            whole(heads_in.shape),
        ]
        + [ANYWHERE] * len(pieces),
        out_specs=[
            down(model),
            down(conv),
            along(conv),
            along(heads),
            pl.BlockSpec((parts, inner, state_dim), lambda c: (c, 0, 0)),
            along(inner),
            along(inner),
            ANYWHERE,
        ],
        out_shape=[
            shape((length, model), BF16),
            shape((length, conv), BF16),
            shape((conv, length), BF16),
            shape((heads, length), F32),
            shape((length // stretch, inner, state_dim), BF16),
            shape((inner, length), F32),
            shape((inner, length), F32),
            shape((inner + conv + SPARE, model), BF16),
        ],
        scratch_shapes=[
            pltpu.VMEM((inner + conv + SPARE, model), BF16),
            pltpu.VMEM((inner, state_dim), F32),
            pltpu.VMEM((conv // LANES, span + 8, LANES), F32),
            pltpu.VMEM((inner, stretch), F32),
            pltpu.VMEM((inner, stretch), BF16),
            pltpu.VMEM((inner, state_dim), F32),
            pltpu.VMEM((heads, stretch), F32),
            pltpu.VMEM((heads, stretch), F32),
            pltpu.VMEM((heads, stretch), F32),
            pltpu.VMEM((heads, stretch), F32),
            pltpu.VMEM((heads, LANES), F32),
            pltpu.SemaphoreType.DMA((len(pieces) + 1,)),
        ],
        name="block_forward",
        **kernel_options(30),
    )(places, tokens, gain, raw_weight, taps, heads_in, *pieces)


def gated(sizes, places, skip, alive, cotangent, inner_gain, gate, scanned, active, pieces, lengths):
    inner, conv, heads, state_dim = sizes
    length, model = cotangent.shape
    span = min(SPAN, length)
    along = lambda rows: pl.BlockSpec((rows, span), lambda c: (0, c))
    shape = jax.ShapeDtypeStruct
    return pl.pallas_call(
        functools.partial(gated_body, sizes, tuple(lengths)),
        grid=(length // span,),
        in_specs=[
            SCALARS,
            SCALARS,
            SCALARS,
            pl.BlockSpec((span, model), lambda c: (c, 0)),
            whole(inner_gain.shape),
            along(inner),
            along(inner),
            along(inner),
        ]
        + [ANYWHERE] * len(pieces),
        out_specs=[
            along(inner),
            pl.BlockSpec((span, inner), lambda c: (c, 0)),
            along(inner),
            along(heads),
            along(heads),
            pl.BlockSpec((inner, LANES), lambda c: (0, 0)),
            ANYWHERE,
        ],
        out_shape=[
            shape((inner, length), BF16),
            shape((length, inner), BF16),
            shape((inner, length), BF16),
            shape((heads, length), F32),
            shape((heads, length), F32),
            shape((inner, LANES), F32),
            shape((inner, model), BF16),
        ],
        scratch_shapes=[
            pltpu.VMEM((inner, model), BF16),
            pltpu.VMEM((inner, span), F32),
            pltpu.VMEM((inner, span), F32),
            pltpu.SemaphoreType.DMA((len(pieces) + 1,)),
        ],
        name="block_gated",
        **kernel_options(15),
    )(places, skip, alive, cotangent, inner_gain, gate, scanned, active, *pieces)


def input_body(alive_ref, tokens_ref, cotangent_ref, gain_ref, d_gate_ref, d_rest_ref, weight_ref, grad_ref, gain_part_ref):
    @pl.when(pl.program_id(0) == 0)
    def _():
        gain_part_ref[...] = jnp.zeros_like(gain_part_ref)

    inner = d_gate_ref.shape[1]
    d_normed = mul_nn(d_gate_ref[...], weight_ref[:inner, :]) + mul_nn(d_rest_ref[...], weight_ref[inner:, :])
    u = tokens_ref[...].astype(F32)
    scale = lax.rsqrt(jnp.mean(u * u, axis=1, keepdims=True) + EPSILON)
    unit = u * scale
    gain_part_ref[...] += eighths(d_normed * unit)
    d_unit = d_normed * gain_ref[...]
    slope = scale * (d_unit - unit * jnp.mean(d_unit * unit, axis=1, keepdims=True))
    grad_ref[...] = cotangent_ref[...].astype(F32) * alive_ref[0] + slope


def input_backward(alive, tokens, cotangent, gain, d_gate, d_rest, weight):
    length, model = tokens.shape
    span = min(SPAN, length)
    down = lambda columns: pl.BlockSpec((span, columns), lambda c: (c, 0))
    shape = jax.ShapeDtypeStruct
    return pl.pallas_call(
        input_body,
        grid=(length // span,),
        in_specs=[
            SCALARS,
            down(model),
            down(model),
            whole(gain.shape),
            down(d_gate.shape[1]),
            down(d_rest.shape[1]),
            whole(weight.shape),
        ],
        out_specs=[down(model), pl.BlockSpec((8, model), lambda c: (0, 0))],
        out_shape=[shape((length, model), F32), shape((8, model), F32)],
        name="input_backward",
        **kernel_options(8),
    )(alive, tokens, cotangent, gain, d_gate, d_rest, weight)


def backward(sizes, first_head, heads, skip, active, mixed, d_scan, raw, row_part, states, taps, heads_in, earlier):
    all_inner, conv, all_heads, state_dim = sizes
    width = all_inner // all_heads
    inner = heads * width
    last = first_head + heads == all_heads
    length = active.shape[1]
    span = min(SPAN, length)
    stretch = min(STRETCH, span)
    parts = span // stretch
    blocks = length // span
    per = span // 16
    at = first_head // heads
    bc = conv - all_inner
    bc_at = all_inner // bc
    along = lambda rows, index: pl.BlockSpec((rows, span), lambda c: (index, blocks - 1 - c))
    down = lambda columns, index: pl.BlockSpec((span, columns), lambda c: (blocks - 1 - c, index))
    ahead = lambda columns, index: pl.BlockSpec(
        (16, columns), lambda c: (jnp.maximum((blocks - 1 - c) * per - 1, 0), index)
    )
    shape = jax.ShapeDtypeStruct
    tiles = (inner + (bc if last else 0)) // LANES
    share = first_head * width if last else inner
    results = pl.pallas_call(
        functools.partial(backward_body, sizes, first_head, last),
        grid=(blocks,),
        in_specs=[SCALARS, along(inner, at), along(bc, bc_at), down(inner, at)]
        + [down(bc, bc_at)] * last
        + [ahead(inner, at)]
        + [ahead(bc, bc_at)] * last
        + [
            along(inner, at),
            along(heads, at),
            along(heads, at),
            pl.BlockSpec((parts, inner, state_dim), lambda c: (blocks - 1 - c, at, 0)),
            whole(taps.shape),
            whole(heads_in.shape),
        ]
        + [along(bc, 0), along(first_head, 0), ANYWHERE] * last,
        out_specs=[down(share, 1 if last else 0)]
        + [along(heads, 0), along(heads, 0), pl.BlockSpec((5, tiles, LANES), lambda c: (0, 0, 0))]
        + [along(bc, 0)] * (not last),
        out_shape=[shape((length, 2 * share), BF16)]
        + [shape((heads, length), F32), shape((heads, length), F32), shape((5, tiles, LANES), F32)]
        + [shape((bc, length), F32)] * (not last),
        scratch_shapes=[
            pltpu.VMEM((inner, state_dim), F32),
            pltpu.VMEM((tiles, span + 8, LANES), F32),
            pltpu.VMEM((tiles, span + 8, LANES), F32),
            pltpu.VMEM((tiles * LANES, span), F32),
            pltpu.VMEM((5, tiles, 8, LANES), F32),
            pltpu.VMEM((inner, stretch), F32),
            pltpu.VMEM((inner, state_dim), F32),
            pltpu.VMEM((inner, stretch), BF16),
            pltpu.VMEM((inner, stretch), BF16),
            pltpu.VMEM((stretch, stretch), F32),
            pltpu.VMEM((heads, state_dim), F32),
            pltpu.VMEM((heads, stretch), F32),
            pltpu.VMEM((heads, stretch), F32),
            pltpu.VMEM((heads, stretch), F32),
            pltpu.VMEM((heads, stretch), F32),
            pltpu.VMEM((heads, LANES), F32),
            pltpu.VMEM((heads, stretch), F32),
            pltpu.VMEM((heads, stretch), F32),
            pltpu.VMEM((heads, stretch), F32),
        ],
        input_output_aliases={3 + 2 * 2 + 6 + 2: 0} if last else {},
        name="block_backward",
        **kernel_options(4 + heads),
    )(
        skip,
        active,
        active,
        *[mixed] * (2 + 2 * last),
        d_scan,
        raw,
        row_part,
        states,
        taps,
        heads_in,
        *((earlier[-1], earlier[1], earlier[0]) if last else ()),
    )
    return results


def powers_of_two(size):
    bits, bit = [], 1
    while bit < size:
        bits.append(bit)
        bit *= 2
    return bits if bit == size else None


def swap(block, axis, bit):
    pairs = [(k, k ^ bit) for k in range(lax.axis_size(axis))]
    return lax.ppermute(block, axis, pairs)


def cut(block, index, pieces, axis=0):
    size = block.shape[axis] // pieces
    return lax.dynamic_slice_in_dim(block, index * size, size, axis)


def halve(block, axis, bit):
    side = (lax.axis_index(axis) // bit) % 2
    got = swap(cut(block, 1 - side, 2), axis, bit)
    return (cut(block, side, 2).astype(F32) + got.astype(F32)).astype(block.dtype)


def double(block, axis, bit):
    side = (lax.axis_index(axis) // bit) % 2
    other = swap(block, axis, bit)
    return jnp.where(
        side == 0, jnp.concatenate([block, other], axis=0), jnp.concatenate([other, block], axis=0)
    )


def pair_sum(product, core):
    return added(product(core), swap(product(1 - core).astype(BF16), "dp", 1))


def after(value, *earlier):
    return lax.optimization_barrier((value, *earlier))[0]


def added(keep, got):
    return (keep.astype(F32) + got.astype(F32)).astype(BF16)


def together(*arrays):
    return lax.optimization_barrier(arrays)


def sides(block, axis, bit):
    side = (lax.axis_index(axis) // bit) % 2
    return cut(block, side, 2), cut(block, 1 - side, 2)


def joined(block, other, side, axis=0):
    return jnp.where(
        side == 0, jnp.concatenate([block, other], axis), jnp.concatenate([other, block], axis)
    )


def pair_sum(product, core):
    return added(product(core), swap(product(1 - core).astype(BF16), "dp", 1))


def after(value, *earlier):
    return lax.optimization_barrier((value, *earlier))[0]


def added(keep, got):
    return (keep.astype(F32) + got.astype(F32)).astype(BF16)


class Chain:
    def __init__(self, keep, give, axis, bit):
        self.keep, self.give, self.axis, self.bit = keep, give, axis, bit

    def start(self):
        self.got = swap(self.give, self.axis, self.bit)
        return self.give

    def finish(self, *beside):
        return added(self.keep, after(self.got, *beside) if beside else self.got)


def halving(block, axis, bit):
    side = (lax.axis_index(axis) // bit) % 2
    return Chain(cut(block, side, 2), cut(block, 1 - side, 2), axis, bit)


def spread(block, bits):
    for bit in reversed(bits):
        block = double(block, "dp", bit)
    return block


class Plain:
    def __init__(self):
        self.groups = lax.axis_size("fsdp")
        self.mine = lax.axis_index("fsdp")

    def gather(self, w_in, packed, w_out, main, prepare):
        by_group = lax.all_gather(w_in.T, "fsdp")
        weight = by_group.transpose(1, 0, 2).reshape(by_group.shape[1], -1)
        out_weight = lax.all_gather(w_out, "fsdp", tiled=True)
        here = jnp.zeros((2,), jnp.int32)
        sizes = [main], [out_weight.shape[0]]
        return (
            ([weight], here, sizes[0]),
            weight[main:],
            prepare(lax.all_gather(packed, "fsdp")),
            ([out_weight], here, sizes[1]),
        )

    def late(self, pieces, places, lengths, earlier):
        return pieces, places, lengths

    def own(self, total, axis):
        return cut(total, self.mine, self.groups, axis).astype(F32)

    def sums(self, low_mixed, incoming, d_gate, normed, kernels, columns, fillers):
        everywhere = lambda term, axis: self.own(lax.psum(term.astype(BF16), ("fsdp", "dp")), axis)
        g_out = everywhere(mul_nn(low_mixed, incoming), 0)
        g_rows, results = [everywhere(mul_tn(d_gate, normed), 1)], []
        for kernel in kernels:
            results.append(kernel(results))
        rest = results[-1][0]
        g_rows.append(everywhere(mul_tn(rest[:, :columns], normed), 1))
        block_out = fillers[0](d_gate)
        input_grad, small = fillers[1](results, rest, d_gate)
        total = cut(lax.psum(small, ("fsdp", "dp")), self.mine, self.groups)[0]
        return g_out, g_rows, fillers[2](total), input_grad, block_out


class Paired:
    def __init__(self):
        self.mine = lax.axis_index("fsdp")
        self.core = lax.axis_index("dp") % 2
        self.bits = powers_of_two(lax.axis_size("dp"))

    def gather(self, w_in, packed, w_out, main, prepare):
        mine, core = self.mine, self.core
        rows = w_in.T
        columns = rows.shape[1]
        last = jnp.pad(rows[main:], ((0, 32 - (rows.shape[0] - main)), (0, 0)))
        half = main // 2
        outer = half // 48 * 16
        middle = half - 2 * outer
        near = self.bits[1]
        side = (lax.axis_index("dp") // near) % 2
        first_row = core * half
        row = lambda where: first_row + jnp.where(side == where, 0, outer + middle)
        part = lambda start, count: lax.dynamic_slice_in_dim(rows, start, count, 0)
        other_packed = swap(packed, "fsdp", 1)
        mine_outer = swap(jnp.concatenate([part(row(0), outer), last], axis=0), "fsdp", 1)
        mine_middle = swap(after(part(first_row + outer, middle), mine_outer), "fsdp", 1)
        near_outer = swap(mine_outer, "dp", near)
        in_order = lambda a, b, axis: jnp.where(
            mine == 0, jnp.concatenate([a, b], axis), jnp.concatenate([b, a], axis)
        )
        raw_weight = in_order(last, mine_outer[outer:], 1)
        prepared = prepare(in_order(packed[None], other_packed[None], 0))
        raw_weight, *prepared = together(raw_weight, *prepared, mine_middle)[:-1]
        core_outer = swap(after(mine_outer, near_outer, mine_middle, raw_weight, *prepared), "dp", 1)
        core_middle = swap(mine_middle, "dp", 1)
        core_near = swap(near_outer, "dp", 1)
        there = (1 - mine) * columns
        across = half - 2 * first_row
        places = [0, mine * columns]
        for start in (row(0), first_row + outer, row(1)):
            places += [start, there, start + across, there]
        places = jnp.stack(places).astype(jnp.int32)
        pieces = [rows, mine_outer, core_outer, mine_middle, core_middle, near_outer, core_near]
        lengths = [main, outer, outer, middle, middle, outer, outer]
        relayed = core_near

        each = w_out.shape[0]
        direct_out = swap(after(cut(w_out, core, 2), relayed), "fsdp", 1)
        other = (1 - mine) * each
        places_out = jnp.stack(
            [mine * each, 0, other + core * (each // 2), 0, other + (1 - core) * (each // 2), 0]
        ).astype(jnp.int32)
        return (
            (pieces, places, lengths),
            raw_weight,
            prepared,
            ([w_out, direct_out], places_out, [each, each // 2, each // 2]),
        )

    def late(self, pieces, places, lengths, earlier):
        own, direct = pieces
        direct = after(direct, earlier)
        return [own, direct, swap(direct, "dp", 1)], places, lengths

    def sums(self, low_mixed, incoming, d_gate, normed, kernels, columns, fillers):
        mine, core, (near, *far) = self.mine, self.core, self.bits[1:]
        near_side = (lax.axis_index("dp") // near) % 2
        owned = lambda block: (cut(block, mine, 2, 1), cut(block, 1 - mine, 2, 1))
        across = lambda give: swap(give, "fsdp", 1)
        over = lambda give, bit: swap(give, "dp", bit)

        def by_cores(term, axis):
            return cut(term, core, 2, axis), swap(cut(term, 1 - core, 2, axis), "dp", 1)

        out_keep, out_got = by_cores(mul_nn(low_mixed, incoming).astype(BF16), 1)
        gate_part = lambda c, left: mul_tn(cut(left, c, 2, 1), normed)
        gate_sent = gate_part(1 - core, d_gate).astype(BF16)
        out_got, gate_sent = together(out_got, gate_sent)
        out_block = added(out_keep, out_got)
        out_give = cut(out_block, 1 - mine, 2)
        got_out = across(out_give)
        gate_got = swap(gate_sent, "dp", 1)
        gate_block = added(gate_part(core, after(d_gate, gate_sent, out_give)), gate_got)
        gate_keep, gate_give = owned(gate_block)
        got_gate = across(gate_give)
        first = kernels[0]([], gate_give)
        got_out, got_gate, _ = together(got_out, got_gate, first[-1])
        keep_a = jnp.concatenate([cut(out_block, mine, 2), gate_keep], axis=0)
        got_a = jnp.concatenate([got_out, got_gate], axis=0)
        keep_a, give_a = sides(added(keep_a, got_a), "dp", near)
        got_a = over(give_a, near)
        second = kernels[1]([first], give_a)
        got_a, rest = together(got_a, second[0])
        keep_b, got_b = by_cores(mul_tn(rest[:, :columns], normed).astype(BF16), 0)
        block_b = added(keep_b, got_b)
        keep_b, give_b = owned(block_b)
        got_b = across(give_b)
        side = lambda bit: (lax.axis_index("dp") // bit) % 2
        results = [first, second]
        turn, wide = far[0], far[1:]

        keep_a, give_a = sides(added(keep_a, after(got_a, give_b)), "dp", turn)
        got_a = over(give_a, turn)
        block_out = fillers[0](after(give_b, give_a))
        got_a, block_out = together(got_a, block_out)
        block_a = added(keep_a, got_a)
        sent_a = [over(block_a, bit) for bit in wide[:1]]
        input_grad, small = fillers[1](results, rest, block_a)
        for bit in wide[1:]:
            block_a = added(block_a, sent_a.pop())
            sent_a = [over(block_a, bit)]
        *sent_a, got_b, small = together(*sent_a, got_b, small)
        if sent_a:
            block_a = added(block_a, sent_a[0])
        block_b = added(keep_b, got_b)

        keep_b, give_b = sides(block_b, "dp", near)
        got_b, got_a, got_s = together(over(give_b, near), over(block_a, turn), over(small, 1))
        block_a, small = joined(block_a, got_a, side(turn)), small + got_s
        spread_a = over(block_a, near)
        keep_b, give_b = sides(added(keep_b, got_b), "dp", turn)
        got_b, got_s = together(over(give_b, turn), over(small, near))
        block_b, small = added(keep_b, got_b), small + got_s
        for bit in wide:
            got_b, got_s = together(over(block_b, bit), over(small, bit))
            block_b, small = added(block_b, got_b), small + got_s
        got_b, got_s, spread_a = together(over(block_b, turn), over(small, turn), spread_a)
        block_b, small = joined(block_b, got_b, side(turn)), small + got_s
        block_a = joined(block_a, spread_a, side(near))
        got_b, got_s = together(over(block_b, near), across(cut(small, 1 - mine, 2)[0]))
        block_b, total = joined(block_b, got_b, side(near)), cut(small, mine, 2)[0] + got_s
        size = out_block.shape[0] // 2
        swapped_a, swapped_b, *g_small = together(swap(block_a, "dp", 1), swap(block_b, "dp", 1), *fillers[2](total))
        g_out = joined(block_a[:size], swapped_a[:size], core, 1).astype(F32)
        g_rows = [joined(block_a[size:], swapped_a[size:], core), joined(block_b, swapped_b, core)]
        return g_out, [rows.astype(F32) for rows in g_rows], g_small, input_grad, block_out


def shards(
    tokens,
    live,
    norm_gain,
    w_in,
    conv_weight,
    conv_bias,
    dt_bias,
    a_log,
    d_skip,
    inner_gain,
    w_out,
    cotangent,
):
    groups, copies = lax.axis_size("fsdp"), lax.axis_size("dp")
    taps = conv_weight.shape[1]
    heads = dt_bias.shape[0] * groups
    inner, conv = inner_gain.shape[0] * groups, conv_bias.shape[0] * groups
    model = tokens.shape[-1]
    proj = w_in.shape[1]
    main = inner + conv
    sizes = (inner, conv, heads, (conv - inner) // 2)
    paired = groups == 2 and powers_of_two(copies) and copies > 2 and main % 32 == 0
    links = Paired() if paired else Plain()

    rest = jnp.concatenate([norm_gain, dt_bias, a_log, d_skip])
    line = max(conv_bias.shape[0], inner_gain.shape[0], rest.shape[0])
    lined = lambda table: jnp.pad(table, ((0, 0), (0, line - table.shape[1])))
    packed = jnp.concatenate([lined(conv_weight.T), lined(conv_bias[None]), lined(inner_gain[None]), lined(rest[None])])

    def prepare(packed):
        packed = packed.astype(F32)
        pick = lambda row, first, each: packed[:, row, first : first + each].reshape(-1)
        model_each, heads_each = norm_gain.shape[0], dt_bias.shape[0]
        table = packed[:, : taps + 1, : conv // groups].transpose(1, 0, 2).reshape(taps + 1, conv)
        table = jnp.concatenate([table, jnp.zeros((7 - taps, conv), F32)], axis=0)
        taps_in = table.reshape(8, conv // LANES, LANES).transpose(1, 0, 2)
        inner_all = pick(taps + 1, 0, inner // groups)[:, None]
        gain_all = pick(taps + 2, 0, model_each)[None]
        by_head = [pick(taps + 2, model_each + k * heads_each, heads_each) for k in range(3)]
        return [taps_in, inner_all, gain_all, jnp.stack(by_head[:2], axis=1), by_head[2]]

    in_pieces, raw_weight, prepared, out_pieces = links.gather(w_in, packed, w_out, main, prepare)
    raw_weight = jnp.pad(raw_weight, ((0, 32 - raw_weight.shape[0]), (0, 0)))
    taps_in, inner_all, gain_all, heads_in, skip = prepared

    alive = live.astype(F32).reshape(1)
    low_tokens, low_cotangent = tokens[0, 0], cotangent[0, 0]
    normed, mixed, active, raw, states, gate, scanned, weight = forward(
        sizes, in_pieces[1], low_tokens, gain_all, raw_weight, taps_in, heads_in, in_pieces[0], in_pieces[2]
    )
    out_pieces = links.late(*out_pieces, normed)
    low_mixed, d_gate, d_scan, row_part, skip_part, gain_part, out_weight = gated(
        sizes, out_pieces[1], skip, alive, low_cotangent, inner_all, gate, scanned, active, out_pieces[0], out_pieces[2]
    )
    u = low_tokens.astype(F32)
    incoming = low_cotangent.astype(F32) * alive[0]

    def backward_step(first, count):
        def step(earlier, *sent):
            scan = after(d_scan, *sent) if sent else d_scan
            return backward(
                sizes,
                first,
                count,
                skip,
                active,
                mixed,
                scan,
                raw,
                row_part,
                states,
                taps_in,
                heads_in,
                earlier[-1] if earlier else None,
            )

        return step

    kernels = [backward_step(first, count) for first, count in HEAD_RANGES]

    step = 64
    rest_columns = -(-(proj - inner) // step) * step

    def input_part(results, rest, tie):
        d_raw, rate_part = [jnp.concatenate([result[k] for result in results], axis=0) for k in (1, 2)]
        conv_part = jnp.concatenate([result[3] for result in results], axis=1).reshape(taps + 1, conv)
        input_grad, gain_part_in = input_backward(
            alive, low_tokens, low_cotangent, gain_all, d_gate, after(rest, tie), weight
        )
        terms = [
            conv_part,
            jnp.sum(gain_part, axis=1)[None],
            jnp.sum(gain_part_in, axis=0)[None],
            jnp.sum(d_raw, axis=1)[None],
            jnp.sum(rate_part, axis=1)[None],
            jnp.sum(skip_part, axis=1)[None],
        ]
        by_owner = [
            jnp.moveaxis(term.reshape(term.shape[0], groups, -1), 1, 0).reshape(groups, -1) for term in terms
        ]
        count = sum(term.shape[1] for term in by_owner)
        by_owner.append(jnp.zeros((groups, -count % (8 * LANES)), F32))
        return input_grad, jnp.concatenate(by_owner, axis=1).reshape(groups, -1, LANES)

    def out_part(tie):
        branch = mul_tn(after(low_mixed, tie), out_weight)
        return (alive[0] * (u + branch)).astype(BF16)

    def small_grads(total):
        total = total.reshape(-1)
        shapes = [(taps + 1, conv), (1, inner), (1, model), (1, heads), (1, heads), (1, heads)]
        first, parts = 0, []
        for lines, line in shapes:
            size = lines * line // groups
            parts.append(total[first : first + size].reshape(lines, -1))
            first += size
        g_conv, g_inner, g_gain, g_bias, g_rate, g_skip = parts
        return [g_gain[0], g_conv[:taps].T, g_conv[taps], g_bias[0], g_rate[0], g_skip[0], g_inner[0]]

    g_out, g_rows, g_small, input_grad, block_out = links.sums(
        low_mixed,
        incoming.astype(BF16),
        d_gate,
        normed,
        kernels,
        rest_columns,
        [out_part, input_part, small_grads],
    )
    g_proj = jnp.concatenate([g_rows[0], g_rows[1][: proj - inner]], axis=0).T
    return (
        block_out.reshape(tokens.shape),
        input_grad.reshape(cotangent.shape),
        g_small[0],
        g_proj,
        *g_small[1:],
        g_out,
    )


def solution(mesh):
    by_device = P("fsdp", "dp", None, None)
    lines, tables = P("fsdp"), P("fsdp", None)
    return jax.shard_map(
        shards,
        mesh=mesh,
        in_specs=(
            by_device,
            P("fsdp", "dp"),
            lines,
            tables,
            tables,
            lines,
            lines,
            lines,
            lines,
            lines,
            tables,
            by_device,
        ),
        out_specs=(by_device, by_device, lines, tables, tables, lines, lines, lines, lines, lines, tables),
        check_vma=False,
    )
```

```python
import functools
import math

import jax
import jax.numpy as jnp
from jax import lax
from jax.experimental import pallas as pl
from jax.experimental.pallas import tpu as pltpu
from jax.sharding import PartitionSpec as P

EPSILON = 1e-05
LOG2E = math.log2(math.e)
SPAN = 256
STRETCH = 256
GROUP = 8
TILE = 256
LANES = 128
SPARE = 256
TILES_ABREAST = 7
HEADS_ABREAST = 2
HEAD_RANGES = ((0, 16), (16, 8))
VMEM_LIMIT = 60 * 1024 * 1024

F32 = jnp.float32
BF16 = jnp.bfloat16


def mul_nn(a, b):
    return lax.dot_general(a, b, (((1,), (0,)), ((), ())), preferred_element_type=F32)


def mul_nt(a, b):
    return lax.dot_general(a, b, (((1,), (1,)), ((), ())), preferred_element_type=F32)


def mul_tn(a, b):
    return lax.dot_general(a, b, (((0,), (0,)), ((), ())), preferred_element_type=F32)


def triangle(size, keep):
    rows = lax.broadcasted_iota(jnp.int32, (size, size), 0)
    cols = lax.broadcasted_iota(jnp.int32, (size, size), 1)
    return keep(rows, cols)


def lane_sums(values, matrix):
    high = values.astype(BF16)
    rest = values - high.astype(F32)
    middle = rest.astype(BF16)
    low = (rest - middle.astype(F32)).astype(BF16)
    return mul_nn(high, matrix) + mul_nn(middle, matrix) + mul_nn(low, matrix)


def as_columns(rows):
    heads, span = rows.shape
    return jnp.concatenate([rows, jnp.zeros((LANES - heads, span), F32)], axis=0).T


def fold(block):
    total = block[:, :LANES]
    for first in range(LANES, block.shape[1], LANES):
        total = total + block[:, first : first + LANES]
    return total


def eighths(block):
    return block.reshape(block.shape[0] // 8, 8, block.shape[1]).sum(axis=0)


def softplus(v):
    return jnp.maximum(v, 0.0) + jnp.log1p(jnp.exp(-jnp.abs(v)))


def sigmoid(v):
    return 0.5 * jnp.tanh(0.5 * v) + 0.5


def decay_between(later, earlier):
    return jnp.exp2(jnp.minimum(later - earlier, 0.0))


def decays(step, rate2):
    span = step.shape[1]
    upper = triangle(span, lambda r, c: r <= c).astype(BF16)
    cum = lane_sums(step * rate2, upper)
    total = cum[:, span - 1 : span]
    return cum, jnp.exp2(total - cum), jnp.exp2(cum), jnp.exp2(total)


def piece_copies(places_ref, lengths, pieces, whole_ref, sems):
    copies = []
    for k, piece in enumerate(pieces):
        rows, columns = lengths[k], piece.shape[1]
        target = whole_ref.at[
            pl.ds(pl.multiple_of(places_ref[2 * k], 16), rows),
            pl.ds(pl.multiple_of(places_ref[2 * k + 1], LANES), columns),
        ]
        copies.append(pltpu.make_async_copy(piece.at[pl.ds(0, rows), :], target, sems.at[k]))
    return copies


def forward_body(sizes, lengths, places_ref, tokens_ref, gain_ref, raw_weight_ref, taps_ref, heads_ref, *refs):
    n_pieces = len(lengths)
    pieces, refs = refs[:n_pieces], refs[n_pieces:]
    (
        normed_ref,
        mixed_ref,
        active_ref,
        raw_ref,
        states_ref,
        gate_ref,
        scanned_ref,
        weight_ref,
        weight,
        state,
        extended,
        carried,
        scaled,
        update,
        cum_s,
        step_s,
        factor_s,
        ec_s,
        total_s,
        sems,
    ) = refs
    inner, conv, heads, state_dim = sizes
    width = inner // heads
    span = tokens_ref.shape[0]
    stretch = min(STRETCH, span)
    half = stretch // 2
    copies = piece_copies(places_ref, lengths, pieces, weight, sems)
    kept = pltpu.make_async_copy(weight, weight_ref, sems.at[n_pieces])

    @pl.when(pl.program_id(0) == 0)
    def _():
        for copy in copies:
            copy.start()
        state[...] = jnp.zeros_like(state)
        extended[:, span:, :] = jnp.zeros((conv // LANES, 8, LANES), F32)

    u = tokens_ref[...].astype(F32)
    normed = u * lax.rsqrt(jnp.mean(u * u, axis=1, keepdims=True) + EPSILON) * gain_ref[...]
    normed = normed.astype(BF16)
    normed_ref[...] = normed

    @pl.when(pl.program_id(0) == 0)
    def _():
        for copy in copies:
            copy.wait()
        steps = raw_weight_ref.shape[0]
        weight[inner + conv : inner + conv + steps, :] = raw_weight_ref[...]
        weight[inner + conv + steps :, :] = jnp.zeros((SPARE - steps, weight.shape[1]), BF16)
        kept.start()

    @pl.loop(0, inner // TILE, unroll=6)
    def _(i):
        rows = pl.ds(pl.multiple_of(i * TILE, TILE), TILE)
        gate_ref[rows, :] = mul_nt(weight[rows, :], normed)

    @pl.loop(0, conv // TILE, unroll=TILES_ABREAST)
    def _(i):
        first = pl.multiple_of(i * TILE, TILE)
        wide = mul_nt(normed, weight[pl.ds(pl.multiple_of(inner + first, TILE), TILE), :])
        for k in range(TILE // LANES):
            index = i * (TILE // LANES) + k
            block = wide[:, k * LANES : (k + 1) * LANES]
            extended[index, :8, :] = extended[index, span:, :]
            extended[index, 8:, :] = block
            taps = taps_ref[index]
            summed = taps[4:5] + block * taps[3:4]
            for shift in range(1, 4):
                summed = summed + extended[index, 8 - shift : 8 - shift + span, :] * taps[3 - shift : 4 - shift]
            lanes = pl.ds(pl.multiple_of(first + k * LANES, LANES), LANES)
            mixed_ref[:, lanes] = block.astype(BF16)
            active_ref[lanes, :] = (summed * sigmoid(summed)).T.astype(BF16)

    raw = mul_nt(raw_weight_ref[...], normed)[:heads] + heads_ref[:, 0:1]
    raw_ref[...] = raw
    step_all = softplus(raw)
    rate2 = -jnp.exp(heads_ref[:, 1:2]) * LOG2E
    causal = triangle(stretch, lambda r, c: r <= c)
    for part in range(span // stretch):
        lanes = slice(part * stretch, (part + 1) * stretch)
        step = step_all[:, lanes]
        cum, factor, ec, total = decays(step, rate2)
        cum_s[...] = cum
        step_s[...] = step
        factor_s[...] = factor * step
        ec_s[...] = ec
        total_s[...] = jnp.broadcast_to(total, (heads, LANES))
        b_in = active_ref[inner : inner + state_dim, lanes]
        c_in = active_ref[inner + state_dim : inner + 2 * state_dim, lanes]
        scores = jnp.where(causal, mul_tn(b_in, c_in), 0.0)
        low_state = state[...].astype(BF16)
        states_ref[part] = low_state
        carried[...] = mul_nn(low_state, c_in)

        @pl.loop(0, heads // GROUP, unroll=HEADS_ABREAST)
        def _(group):
            eight = pl.ds(pl.multiple_of(group * GROUP, GROUP), GROUP)
            cum_g, step_g, factor_g, ec_g = cum_s[eight, :], step_s[eight, :], factor_s[eight, :], ec_s[eight, :]
            cum_c = as_columns(cum_g)
            for j in range(GROUP):
                rows = pl.ds(pl.multiple_of((group * GROUP + j) * width, width), width)
                row = slice(j, j + 1)
                values = active_ref[rows, lanes].astype(F32)
                stepped = (values * step_g[row]).astype(BF16)
                early = (scores[:half] * decay_between(cum_g[row], cum_c[:half, row])).astype(BF16)
                late = (scores[half:, half:] * decay_between(cum_g[row, half:], cum_c[half:, row])).astype(BF16)
                inside = mul_nn(stepped[:, :half], early)
                inside = jnp.concatenate(
                    [inside[:, :half], inside[:, half:] + mul_nn(stepped[:, half:], late)], axis=1
                )
                scanned_ref[rows, lanes] = inside + ec_g[row] * carried[rows, :]
                scaled[rows, :] = (values * factor_g[row]).astype(BF16)

        update[...] = mul_nt(scaled[...], b_in)

        @pl.loop(0, heads // GROUP, unroll=HEADS_ABREAST)
        def _(group):
            eight = pl.ds(pl.multiple_of(group * GROUP, GROUP), GROUP)
            total_g = total_s[eight, :]
            for j in range(GROUP):
                rows = pl.ds(pl.multiple_of((group * GROUP + j) * width, width), width)
                state[rows, :] = total_g[j : j + 1] * state[rows, :] + update[rows, :]

    @pl.when(pl.program_id(0) == pl.num_programs(0) - 1)
    def _():
        kept.wait()


def gated_body(sizes, lengths, places_ref, skip_ref, alive_ref, cotangent_ref, inner_gain_ref, *refs):
    n_pieces = len(lengths)
    gate, scanned, values_ref = refs[:3]
    pieces, refs = refs[3 : 3 + n_pieces], refs[3 + n_pieces :]
    (
        low_mixed_ref,
        d_gate_ref,
        d_scan_ref,
        row_part_ref,
        skip_part_ref,
        gain_part_ref,
        out_weight_ref,
        out_weight,
        gated,
        d_normed,
        sems,
    ) = refs
    inner, conv, heads, state_dim = sizes
    width = inner // heads
    span = cotangent_ref.shape[0]
    copies = piece_copies(places_ref, lengths, pieces, out_weight, sems)
    kept = pltpu.make_async_copy(out_weight, out_weight_ref, sems.at[n_pieces])

    @pl.when(pl.program_id(0) == 0)
    def _():
        for copy in copies:
            copy.start()
        gain_part_ref[...] = jnp.zeros_like(gain_part_ref)

    def gated_head(h, squares):
        rows = pl.ds(pl.multiple_of(h * width, width), width)
        z = gate[rows, :]
        y = scanned[rows, :] + skip_ref[h] * values_ref[rows, :].astype(F32)
        v = y * (z * sigmoid(z))
        gated[rows, :] = v
        return squares + eighths(v * v)

    squares = lax.fori_loop(0, heads, gated_head, jnp.zeros((8, span), F32), unroll=4)
    scale = lax.rsqrt(jnp.sum(squares, axis=0, keepdims=True) / inner + EPSILON)

    @pl.when(pl.program_id(0) == 0)
    def _():
        for copy in copies:
            copy.wait()
        kept.start()

    incoming = (cotangent_ref[...].astype(F32) * alive_ref[0]).astype(BF16)

    def norm_tile(i, dots):
        rows = pl.ds(pl.multiple_of(i * TILE, TILE), TILE)
        gain = inner_gain_ref[rows, :]
        unit = gated[rows, :] * scale
        low_mixed_ref[rows, :] = (unit * gain).astype(BF16)
        d_mixed = mul_nt(out_weight[rows, :], incoming)
        gain_part_ref[rows, :] += fold(d_mixed * unit)
        d_unit = d_mixed * gain
        d_normed[rows, :] = d_unit
        return dots + eighths(d_unit * unit)

    dots = lax.fori_loop(0, inner // TILE, norm_tile, jnp.zeros((8, span), F32), unroll=3)
    mean_dot = jnp.sum(dots, axis=0, keepdims=True) / inner

    @pl.loop(0, heads // GROUP, unroll=HEADS_ABREAST)
    def _(group):
        eight = pl.ds(pl.multiple_of(group * GROUP, GROUP), GROUP)
        row_parts, skip_parts, d_gates = [], [], []
        for j in range(GROUP):
            h = group * GROUP + j
            rows = pl.ds(pl.multiple_of(h * width, width), width)
            z = gate[rows, :]
            sig = sigmoid(z)
            values = values_ref[rows, :].astype(F32)
            pure = scanned[rows, :]
            y = pure + skip_ref[h] * values
            d_gated = scale * (d_normed[rows, :] - gated[rows, :] * (scale * mean_dot))
            d_scan = (d_gated * (z * sig)).astype(BF16)
            d_scan_ref[rows, :] = d_scan
            d_gates.append(d_gated * y * (sig * (1.0 + z * (1.0 - sig))))
            if len(d_gates) * width == LANES:
                lanes = pl.ds(pl.multiple_of((h + 1) * width - LANES, LANES), LANES)
                d_gate_ref[:, lanes] = jnp.concatenate(d_gates, axis=0).T.astype(BF16)
                d_gates = []
            d_scan = d_scan.astype(F32)
            row_parts.append(jnp.sum(d_scan * pure, axis=0, keepdims=True))
            skip_parts.append(jnp.sum(d_scan * values, axis=0, keepdims=True))
        row_part_ref[eight, :] = jnp.concatenate(row_parts, axis=0)
        skip_part_ref[eight, :] = jnp.concatenate(skip_parts, axis=0)

    @pl.when(pl.program_id(0) == pl.num_programs(0) - 1)
    def _():
        kept.wait()


def backward_body(sizes, first_head, last, *refs):
    refs = list(refs)
    take = lambda n: [refs.pop(0) for _ in range(n)]
    skip_ref, active_ref, low_bc_ref = take(3)
    mixed_refs = take(2 if last else 1)
    before_refs = take(2 if last else 1)
    d_scan_ref, raw_ref, row_part_ref, states_ref, taps_ref, heads_ref = take(6)
    bc_part_ref, d_raw_before_ref, _ = take(3) if last else (None, None, None)
    d_rest_ref = take(1)[0]
    d_raw_ref, rate_part_ref, conv_part_ref = take(3)
    bc_out_ref = None if last else take(1)[0]
    (
        d_state,
        extended,
        d_extended,
        d_active,
        sums,
        from_state,
        push,
        scaled,
        d_scaled,
        d_scores,
        state_dots,
        cum_s,
        step_s,
        factor_s,
        ec_s,
        total_s,
        pair_s,
        direct_s,
        ending_s,
    ) = refs
    all_inner, conv, all_heads, state_dim = sizes
    inner, span = active_ref.shape
    width = all_inner // all_heads
    heads = inner // width
    tiles = [(ref, before, t) for ref, before in zip(mixed_refs, before_refs) for t in range(ref.shape[1] // LANES)]
    first_tiles = [first_head * width // LANES, all_inner // LANES]
    stretch = min(STRETCH, span)
    half = stretch // 2
    first_block = pl.program_id(0) == pl.num_programs(0) - 1

    @pl.when(pl.program_id(0) == 0)
    def _():
        d_state[...] = jnp.zeros_like(d_state)
        d_extended[:, :8, :] = jnp.zeros((len(tiles), 8, LANES), F32)
        sums[...] = jnp.zeros_like(sums)

    raw = raw_ref[...]
    step_all = softplus(raw)
    slope = sigmoid(raw)
    rate = -jnp.exp(heads_ref[first_head : first_head + heads, 1:2])
    rate2 = rate * LOG2E
    causal = triangle(stretch, lambda r, c: r <= c)
    ending = triangle(stretch, lambda r, c: r >= c).astype(BF16)
    before_it = triangle(stretch, lambda r, c: r < c).astype(BF16)
    for part in reversed(range(span // stretch)):
        lanes = slice(part * stretch, (part + 1) * stretch)
        step = step_all[:, lanes]
        cum, factor, ec, total = decays(step, rate2)
        cum_s[...] = cum
        step_s[...] = step
        factor_s[...] = factor
        ec_s[...] = ec
        total_s[...] = jnp.broadcast_to(total, (heads, LANES))
        b_in = low_bc_ref[:state_dim, lanes]
        c_in = low_bc_ref[state_dim:, lanes]
        scores = jnp.where(causal, mul_tn(b_in, c_in), 0.0)
        low_d_state = d_state[...].astype(BF16)
        from_state[...] = mul_nn(low_d_state, b_in)
        d_scores[...] = jnp.zeros_like(d_scores)

        @pl.loop(0, heads // GROUP, unroll=HEADS_ABREAST)
        def _(group):
            eight = pl.ds(pl.multiple_of(group * GROUP, GROUP), GROUP)
            cum_g, step_g, factor_g, ec_g = cum_s[eight, :], step_s[eight, :], factor_s[eight, :], ec_s[eight, :]
            cum_c = as_columns(cum_g)
            pairs, directs, endings, dots = [], [], [], []
            d_early, d_late = d_scores[:half, :], d_scores[half:, half:]
            for j in range(GROUP):
                h = group * GROUP + j
                rows = pl.ds(pl.multiple_of(h * width, width), width)
                row = slice(j, j + 1)
                values = active_ref[rows, lanes].astype(F32)
                stepped = (values * step_g[row]).astype(BF16)
                low_d = d_scan_ref[rows, lanes]
                d_scan = low_d.astype(F32)
                early = decay_between(cum_g[row], cum_c[:half, row])
                late = decay_between(cum_g[row, half:], cum_c[half:, row])
                inside = jnp.concatenate(
                    [
                        mul_nt(low_d, (scores[:half] * early).astype(BF16)),
                        mul_nt(low_d[:, half:], (scores[half:, half:] * late).astype(BF16)),
                    ],
                    axis=1,
                )
                d_early = d_early + mul_tn(stepped[:, :half], low_d) * early
                d_late = d_late + mul_tn(stepped[:, half:], low_d[:, half:]) * late
                across = from_state[rows, :] * factor_g[row]
                both = inside + across
                d_active[rows, lanes] = step_g[row] * both + skip_ref[first_head + h] * d_scan
                pairs.append(jnp.sum(stepped.astype(F32) * inside, axis=0, keepdims=True))
                directs.append(jnp.sum(values * both, axis=0, keepdims=True))
                endings.append(jnp.sum(values * across, axis=0, keepdims=True))
                scaled[rows, :] = (values * (step_g[row] * factor_g[row])).astype(BF16)
                d_scaled[rows, :] = (d_scan * ec_g[row]).astype(BF16)
                dots.append(jnp.sum(d_state[rows, :] * states_ref[part, rows, :].astype(F32), axis=0, keepdims=True))
            d_scores[:half, :] = d_early
            d_scores[half:, half:] = d_late
            pair_s[eight, :] = jnp.concatenate(pairs, axis=0)
            direct_s[eight, :] = jnp.concatenate(directs, axis=0)
            ending_s[eight, :] = jnp.concatenate(endings, axis=0)
            state_dots[eight, :] = jnp.concatenate(dots, axis=0)

        low_d_scores = jnp.where(causal, d_scores[...], 0.0).astype(BF16)
        low_state = states_ref[part]
        d_b = mul_tn(low_d_state, scaled[...]) + mul_nt(c_in, low_d_scores)
        d_c = mul_tn(low_state, d_scaled[...]) + mul_nn(b_in, low_d_scores)
        if last:
            d_active[inner : inner + state_dim, lanes] = d_b + bc_part_ref[:state_dim, lanes]
            d_active[inner + state_dim :, lanes] = d_c + bc_part_ref[state_dim:, lanes]
        else:
            bc_out_ref[:state_dim, lanes] = d_b
            bc_out_ref[state_dim:, lanes] = d_c
        push[...] = mul_nt(d_scaled[...], c_in)

        @pl.loop(0, heads // GROUP, unroll=HEADS_ABREAST)
        def _(group):
            eight = pl.ds(pl.multiple_of(group * GROUP, GROUP), GROUP)
            total_g = total_s[eight, :]
            for j in range(GROUP):
                rows = pl.ds(pl.multiple_of((group * GROUP + j) * width, width), width)
                d_state[rows, :] = total_g[j : j + 1] * d_state[rows, :] + push[rows, :]

        d_log = (
            lane_sums(row_part_ref[:, lanes] - pair_s[...], ending)
            + lane_sums(step * ending_s[...], before_it)
            + total * jnp.sum(state_dots[...], axis=1, keepdims=True)
        )
        rate_part_ref[:, lanes] = d_log * step * rate
        d_raw_ref[:, lanes] = (direct_s[...] + d_log * rate) * slope[:, lanes]

    for index, (mixed_ref, before_ref, tile) in enumerate(tiles):
        lanes = slice(tile * LANES, (tile + 1) * LANES)
        active_rows = slice(index * LANES, (index + 1) * LANES)
        before = before_ref[:, lanes].astype(F32)[8:]
        extended[index, :8, :] = jnp.where(first_block, 0.0, before)
        extended[index, 8:, :] = mixed_ref[:, lanes].astype(F32)
        taps = taps_ref[first_tiles[0] + index if mixed_ref is mixed_refs[0] else first_tiles[1] + tile]
        moved = [extended[index, 8 - shift : 8 - shift + span, :] for shift in range(4)]
        summed = taps[4:5] + moved[0] * taps[3:4]
        for shift in range(1, 4):
            summed = summed + moved[shift] * taps[3 - shift : 4 - shift]
        sig = sigmoid(summed)
        d_summed = d_active[active_rows, :].T * (sig * (1.0 + summed * (1.0 - sig)))
        d_extended[index, span:, :] = d_extended[index, :8, :]
        d_extended[index, :span, :] = d_summed
        d_block = d_summed * taps[3:4]
        for shift in range(1, 4):
            d_block = d_block + d_extended[index, shift : shift + span, :] * taps[3 - shift : 4 - shift]
        d_rest_ref[:, active_rows] = d_block.astype(BF16)
        for shift in range(4):
            sums[3 - shift, index] += eighths(d_summed * moved[shift])
        sums[4, index] += eighths(d_summed)

    if last:
        d_raw = jnp.concatenate([d_raw_before_ref[...], d_raw_ref[...]], axis=0)
        done = len(tiles) * LANES
        d_rest_ref[:, done : done + LANES] = as_columns(d_raw).astype(BF16)
        d_rest_ref[:, done + LANES :] = jnp.zeros((span, d_rest_ref.shape[1] - done - LANES), BF16)

    @pl.when(first_block)
    def _():
        for k in range(5):
            conv_part_ref[k] = jnp.sum(sums[k], axis=1)


def whole(shape):
    return pl.BlockSpec(shape, lambda c: (0,) * len(shape), pipeline_mode=pl.Buffered(1))


ANYWHERE = pl.BlockSpec(memory_space=pl.ANY)
SCALARS = pl.BlockSpec(memory_space=pltpu.SMEM)


def kernel_options(microseconds):
    return dict(
        compiler_params=pltpu.CompilerParams(
            dimension_semantics=("arbitrary",), vmem_limit_bytes=VMEM_LIMIT
        ),
        cost_estimate=pl.CostEstimate(
            flops=microseconds * 10**9, bytes_accessed=microseconds * 10**6, transcendentals=0
        ),
    )


def forward(sizes, places, tokens, gain, raw_weight, taps, heads_in, pieces, lengths):
    inner, conv, heads, state_dim = sizes
    length, model = tokens.shape
    span = min(SPAN, length)
    stretch = min(STRETCH, span)
    parts = span // stretch
    along = lambda rows: pl.BlockSpec((rows, span), lambda c: (0, c))
    down = lambda columns: pl.BlockSpec((span, columns), lambda c: (c, 0))
    shape = jax.ShapeDtypeStruct
    return pl.pallas_call(
        functools.partial(forward_body, sizes, tuple(lengths)),
        grid=(length // span,),
        in_specs=[
            SCALARS,
            down(model),
            whole(gain.shape),
            whole(raw_weight.shape),
            whole(taps.shape),
            whole(heads_in.shape),
        ]
        + [ANYWHERE] * len(pieces),
        out_specs=[
            down(model),
            down(conv),
            along(conv),
            along(heads),
            pl.BlockSpec((parts, inner, state_dim), lambda c: (c, 0, 0)),
            along(inner),
            along(inner),
            ANYWHERE,
        ],
        out_shape=[
            shape((length, model), BF16),
            shape((length, conv), BF16),
            shape((conv, length), BF16),
            shape((heads, length), F32),
            shape((length // stretch, inner, state_dim), BF16),
            shape((inner, length), F32),
            shape((inner, length), F32),
            shape((inner + conv + SPARE, model), BF16),
        ],
        scratch_shapes=[
            pltpu.VMEM((inner + conv + SPARE, model), BF16),
            pltpu.VMEM((inner, state_dim), F32),
            pltpu.VMEM((conv // LANES, span + 8, LANES), F32),
            pltpu.VMEM((inner, stretch), F32),
            pltpu.VMEM((inner, stretch), BF16),
            pltpu.VMEM((inner, state_dim), F32),
            pltpu.VMEM((heads, stretch), F32),
            pltpu.VMEM((heads, stretch), F32),
            pltpu.VMEM((heads, stretch), F32),
            pltpu.VMEM((heads, stretch), F32),
            pltpu.VMEM((heads, LANES), F32),
            pltpu.SemaphoreType.DMA((len(pieces) + 1,)),
        ],
        name="block_forward",
        **kernel_options(30),
    )(places, tokens, gain, raw_weight, taps, heads_in, *pieces)


def gated(sizes, places, skip, alive, cotangent, inner_gain, gate, scanned, active, pieces, lengths):
    inner, conv, heads, state_dim = sizes
    length, model = cotangent.shape
    span = min(SPAN, length)
    along = lambda rows: pl.BlockSpec((rows, span), lambda c: (0, c))
    shape = jax.ShapeDtypeStruct
    return pl.pallas_call(
        functools.partial(gated_body, sizes, tuple(lengths)),
        grid=(length // span,),
        in_specs=[
            SCALARS,
            SCALARS,
            SCALARS,
            pl.BlockSpec((span, model), lambda c: (c, 0)),
            whole(inner_gain.shape),
            along(inner),
            along(inner),
            along(inner),
        ]
        + [ANYWHERE] * len(pieces),
        out_specs=[
            along(inner),
            pl.BlockSpec((span, inner), lambda c: (c, 0)),
            along(inner),
            along(heads),
            along(heads),
            pl.BlockSpec((inner, LANES), lambda c: (0, 0)),
            ANYWHERE,
        ],
        out_shape=[
            shape((inner, length), BF16),
            shape((length, inner), BF16),
            shape((inner, length), BF16),
            shape((heads, length), F32),
            shape((heads, length), F32),
            shape((inner, LANES), F32),
            shape((inner, model), BF16),
        ],
        scratch_shapes=[
            pltpu.VMEM((inner, model), BF16),
            pltpu.VMEM((inner, span), F32),
            pltpu.VMEM((inner, span), F32),
            pltpu.SemaphoreType.DMA((len(pieces) + 1,)),
        ],
        name="block_gated",
        **kernel_options(15),
    )(places, skip, alive, cotangent, inner_gain, gate, scanned, active, *pieces)


def input_body(alive_ref, tokens_ref, cotangent_ref, gain_ref, d_gate_ref, d_rest_ref, weight_ref, grad_ref, gain_part_ref):
    @pl.when(pl.program_id(0) == 0)
    def _():
        gain_part_ref[...] = jnp.zeros_like(gain_part_ref)

    inner = d_gate_ref.shape[1]
    d_normed = mul_nn(d_gate_ref[...], weight_ref[:inner, :]) + mul_nn(d_rest_ref[...], weight_ref[inner:, :])
    u = tokens_ref[...].astype(F32)
    scale = lax.rsqrt(jnp.mean(u * u, axis=1, keepdims=True) + EPSILON)
    unit = u * scale
    gain_part_ref[...] += eighths(d_normed * unit)
    d_unit = d_normed * gain_ref[...]
    slope = scale * (d_unit - unit * jnp.mean(d_unit * unit, axis=1, keepdims=True))
    grad_ref[...] = cotangent_ref[...].astype(F32) * alive_ref[0] + slope


def input_backward(alive, tokens, cotangent, gain, d_gate, d_rest, weight):
    length, model = tokens.shape
    span = min(SPAN, length)
    down = lambda columns: pl.BlockSpec((span, columns), lambda c: (c, 0))
    shape = jax.ShapeDtypeStruct
    return pl.pallas_call(
        input_body,
        grid=(length // span,),
        in_specs=[
            SCALARS,
            down(model),
            down(model),
            whole(gain.shape),
            down(d_gate.shape[1]),
            down(d_rest.shape[1]),
            whole(weight.shape),
        ],
        out_specs=[down(model), pl.BlockSpec((8, model), lambda c: (0, 0))],
        out_shape=[shape((length, model), F32), shape((8, model), F32)],
        name="input_backward",
        **kernel_options(8),
    )(alive, tokens, cotangent, gain, d_gate, d_rest, weight)


def backward(sizes, first_head, heads, skip, active, mixed, d_scan, raw, row_part, states, taps, heads_in, earlier):
    all_inner, conv, all_heads, state_dim = sizes
    width = all_inner // all_heads
    inner = heads * width
    last = first_head + heads == all_heads
    length = active.shape[1]
    span = min(SPAN, length)
    stretch = min(STRETCH, span)
    parts = span // stretch
    blocks = length // span
    per = span // 16
    at = first_head // heads
    bc = conv - all_inner
    bc_at = all_inner // bc
    along = lambda rows, index: pl.BlockSpec((rows, span), lambda c: (index, blocks - 1 - c))
    down = lambda columns, index: pl.BlockSpec((span, columns), lambda c: (blocks - 1 - c, index))
    ahead = lambda columns, index: pl.BlockSpec(
        (16, columns), lambda c: (jnp.maximum((blocks - 1 - c) * per - 1, 0), index)
    )
    shape = jax.ShapeDtypeStruct
    tiles = (inner + (bc if last else 0)) // LANES
    share = first_head * width if last else inner
    results = pl.pallas_call(
        functools.partial(backward_body, sizes, first_head, last),
        grid=(blocks,),
        in_specs=[SCALARS, along(inner, at), along(bc, bc_at), down(inner, at)]
        + [down(bc, bc_at)] * last
        + [ahead(inner, at)]
        + [ahead(bc, bc_at)] * last
        + [
            along(inner, at),
            along(heads, at),
            along(heads, at),
            pl.BlockSpec((parts, inner, state_dim), lambda c: (blocks - 1 - c, at, 0)),
            whole(taps.shape),
            whole(heads_in.shape),
        ]
        + [along(bc, 0), along(first_head, 0), ANYWHERE] * last,
        out_specs=[down(share, 1 if last else 0)]
        + [along(heads, 0), along(heads, 0), pl.BlockSpec((5, tiles, LANES), lambda c: (0, 0, 0))]
        + [along(bc, 0)] * (not last),
        out_shape=[shape((length, 2 * share), BF16)]
        + [shape((heads, length), F32), shape((heads, length), F32), shape((5, tiles, LANES), F32)]
        + [shape((bc, length), F32)] * (not last),
        scratch_shapes=[
            pltpu.VMEM((inner, state_dim), F32),
            pltpu.VMEM((tiles, span + 8, LANES), F32),
            pltpu.VMEM((tiles, span + 8, LANES), F32),
            pltpu.VMEM((tiles * LANES, span), F32),
            pltpu.VMEM((5, tiles, 8, LANES), F32),
            pltpu.VMEM((inner, stretch), F32),
            pltpu.VMEM((inner, state_dim), F32),
            pltpu.VMEM((inner, stretch), BF16),
            pltpu.VMEM((inner, stretch), BF16),
            pltpu.VMEM((stretch, stretch), F32),
            pltpu.VMEM((heads, state_dim), F32),
            pltpu.VMEM((heads, stretch), F32),
            pltpu.VMEM((heads, stretch), F32),
            pltpu.VMEM((heads, stretch), F32),
            pltpu.VMEM((heads, stretch), F32),
            pltpu.VMEM((heads, LANES), F32),
            pltpu.VMEM((heads, stretch), F32),
            pltpu.VMEM((heads, stretch), F32),
            pltpu.VMEM((heads, stretch), F32),
        ],
        input_output_aliases={3 + 2 * 2 + 6 + 2: 0} if last else {},
        name="block_backward",
        **kernel_options(4 + heads),
    )(
        skip,
        active,
        active,
        *[mixed] * (2 + 2 * last),
        d_scan,
        raw,
        row_part,
        states,
        taps,
        heads_in,
        *((earlier[-1], earlier[1], earlier[0]) if last else ()),
    )
    return results


def powers_of_two(size):
    bits, bit = [], 1
    while bit < size:
        bits.append(bit)
        bit *= 2
    return bits if bit == size else None


def swap(block, axis, bit):
    pairs = [(k, k ^ bit) for k in range(lax.axis_size(axis))]
    return lax.ppermute(block, axis, pairs)


def cut(block, index, pieces, axis=0):
    size = block.shape[axis] // pieces
    return lax.dynamic_slice_in_dim(block, index * size, size, axis)


def halve(block, axis, bit):
    side = (lax.axis_index(axis) // bit) % 2
    got = swap(cut(block, 1 - side, 2), axis, bit)
    return (cut(block, side, 2).astype(F32) + got.astype(F32)).astype(block.dtype)


def double(block, axis, bit):
    side = (lax.axis_index(axis) // bit) % 2
    other = swap(block, axis, bit)
    return jnp.where(
        side == 0, jnp.concatenate([block, other], axis=0), jnp.concatenate([other, block], axis=0)
    )


def pair_sum(product, core):
    return added(product(core), swap(product(1 - core).astype(BF16), "dp", 1))


def after(value, *earlier):
    return lax.optimization_barrier((value, *earlier))[0]


def added(keep, got):
    return (keep.astype(F32) + got.astype(F32)).astype(BF16)


def together(*arrays):
    return lax.optimization_barrier(arrays)


def sides(block, axis, bit):
    side = (lax.axis_index(axis) // bit) % 2
    return cut(block, side, 2), cut(block, 1 - side, 2)


def joined(block, other, side, axis=0):
    return jnp.where(
        side == 0, jnp.concatenate([block, other], axis), jnp.concatenate([other, block], axis)
    )


def pair_sum(product, core):
    return added(product(core), swap(product(1 - core).astype(BF16), "dp", 1))


def after(value, *earlier):
    return lax.optimization_barrier((value, *earlier))[0]


def added(keep, got):
    return (keep.astype(F32) + got.astype(F32)).astype(BF16)


class Chain:
    def __init__(self, keep, give, axis, bit):
        self.keep, self.give, self.axis, self.bit = keep, give, axis, bit

    def start(self):
        self.got = swap(self.give, self.axis, self.bit)
        return self.give

    def finish(self, *beside):
        return added(self.keep, after(self.got, *beside) if beside else self.got)


def halving(block, axis, bit):
    side = (lax.axis_index(axis) // bit) % 2
    return Chain(cut(block, side, 2), cut(block, 1 - side, 2), axis, bit)


def spread(block, bits):
    for bit in reversed(bits):
        block = double(block, "dp", bit)
    return block


class Plain:
    def __init__(self):
        self.groups = lax.axis_size("fsdp")
        self.mine = lax.axis_index("fsdp")

    def gather(self, w_in, packed, w_out, main, prepare):
        by_group = lax.all_gather(w_in.T, "fsdp")
        weight = by_group.transpose(1, 0, 2).reshape(by_group.shape[1], -1)
        out_weight = lax.all_gather(w_out, "fsdp", tiled=True)
        here = jnp.zeros((2,), jnp.int32)
        sizes = [main], [out_weight.shape[0]]
        return (
            ([weight], here, sizes[0]),
            weight[main:],
            prepare(lax.all_gather(packed, "fsdp")),
            ([out_weight], here, sizes[1]),
        )

    def late(self, pieces, places, lengths, earlier):
        return pieces, places, lengths

    def own(self, total, axis):
        return cut(total, self.mine, self.groups, axis).astype(F32)

    def sums(self, low_mixed, incoming, d_gate, normed, kernels, columns, fillers):
        everywhere = lambda term, axis: self.own(lax.psum(term.astype(BF16), ("fsdp", "dp")), axis)
        g_out = everywhere(mul_nn(low_mixed, incoming), 0)
        g_rows, results = [everywhere(mul_tn(d_gate, normed), 1)], []
        for kernel in kernels:
            results.append(kernel(results))
        rest = results[-1][0]
        g_rows.append(everywhere(mul_tn(rest[:, :columns], normed), 1))
        block_out = fillers[0](d_gate)
        input_grad, small = fillers[1](results, rest, d_gate)
        total = cut(lax.psum(small, ("fsdp", "dp")), self.mine, self.groups)[0]
        return g_out, g_rows, fillers[2](total), input_grad, block_out


class Paired:
    def __init__(self):
        self.mine = lax.axis_index("fsdp")
        self.core = lax.axis_index("dp") % 2
        self.bits = powers_of_two(lax.axis_size("dp"))

    def gather(self, w_in, packed, w_out, main, prepare):
        mine, core = self.mine, self.core
        rows = w_in.T
        columns = rows.shape[1]
        last = jnp.pad(rows[main:], ((0, 32 - (rows.shape[0] - main)), (0, 0)))
        half = main // 2
        outer = half // 48 * 16
        middle = half - 2 * outer
        near = self.bits[1]
        side = (lax.axis_index("dp") // near) % 2
        first_row = core * half
        row = lambda where: first_row + jnp.where(side == where, 0, outer + middle)
        part = lambda start, count: lax.dynamic_slice_in_dim(rows, start, count, 0)
        other_packed = swap(packed, "fsdp", 1)
        mine_outer = swap(jnp.concatenate([part(row(0), outer), last], axis=0), "fsdp", 1)
        mine_middle = swap(after(part(first_row + outer, middle), mine_outer), "fsdp", 1)
        near_outer = swap(mine_outer, "dp", near)
        in_order = lambda a, b, axis: jnp.where(
            mine == 0, jnp.concatenate([a, b], axis), jnp.concatenate([b, a], axis)
        )
        raw_weight = in_order(last, mine_outer[outer:], 1)
        prepared = prepare(in_order(packed[None], other_packed[None], 0))
        raw_weight, *prepared = together(raw_weight, *prepared, mine_middle)[:-1]
        core_outer = swap(after(mine_outer, near_outer, mine_middle, raw_weight, *prepared), "dp", 1)
        core_middle = swap(mine_middle, "dp", 1)
        core_near = swap(near_outer, "dp", 1)
        there = (1 - mine) * columns
        across = half - 2 * first_row
        places = [0, mine * columns]
        for start in (row(0), first_row + outer, row(1)):
            places += [start, there, start + across, there]
        places = jnp.stack(places).astype(jnp.int32)
        pieces = [rows, mine_outer, core_outer, mine_middle, core_middle, near_outer, core_near]
        lengths = [main, outer, outer, middle, middle, outer, outer]
        relayed = core_near

        each = w_out.shape[0]
        direct_out = swap(after(cut(w_out, core, 2), relayed), "fsdp", 1)
        other = (1 - mine) * each
        places_out = jnp.stack(
            [mine * each, 0, other + core * (each // 2), 0, other + (1 - core) * (each // 2), 0]
        ).astype(jnp.int32)
        return (
            (pieces, places, lengths),
            raw_weight,
            prepared,
            ([w_out, direct_out], places_out, [each, each // 2, each // 2]),
        )

    def late(self, pieces, places, lengths, earlier):
        own, direct = pieces
        direct = after(direct, earlier)
        return [own, direct, swap(direct, "dp", 1)], places, lengths

    def sums(self, low_mixed, incoming, d_gate, normed, kernels, columns, fillers):
        mine, core, (near, *far) = self.mine, self.core, self.bits[1:]
        near_side = (lax.axis_index("dp") // near) % 2
        owned = lambda block: (cut(block, mine, 2, 1), cut(block, 1 - mine, 2, 1))
        across = lambda give: swap(give, "fsdp", 1)
        over = lambda give, bit: swap(give, "dp", bit)

        def by_cores(term, axis):
            return cut(term, core, 2, axis), swap(cut(term, 1 - core, 2, axis), "dp", 1)

        out_keep, out_got = by_cores(mul_nn(low_mixed, incoming).astype(BF16), 1)
        gate_part = lambda c, left: mul_tn(cut(left, c, 2, 1), normed)
        gate_sent = gate_part(1 - core, d_gate).astype(BF16)
        out_got, gate_sent = together(out_got, gate_sent)
        out_block = added(out_keep, out_got)
        out_give = cut(out_block, 1 - mine, 2)
        got_out = across(out_give)
        gate_got = swap(gate_sent, "dp", 1)
        gate_block = added(gate_part(core, after(d_gate, gate_sent, out_give)), gate_got)
        gate_keep, gate_give = owned(gate_block)
        got_gate = across(gate_give)
        first = kernels[0]([], gate_give)
        got_out, got_gate, _ = together(got_out, got_gate, first[-1])
        keep_a = jnp.concatenate([cut(out_block, mine, 2), gate_keep], axis=0)
        got_a = jnp.concatenate([got_out, got_gate], axis=0)
        keep_a, give_a = sides(added(keep_a, got_a), "dp", near)
        got_a = over(give_a, near)
        second = kernels[1]([first], give_a)
        got_a, rest = together(got_a, second[0])
        keep_b, got_b = by_cores(mul_tn(rest[:, :columns], normed).astype(BF16), 0)
        block_b = added(keep_b, got_b)
        keep_b, give_b = owned(block_b)
        got_b = across(give_b)
        side = lambda bit: (lax.axis_index("dp") // bit) % 2
        results = [first, second]
        turn, wide = far[0], far[1:]

        keep_a, give_a = sides(added(keep_a, after(got_a, give_b)), "dp", turn)
        got_a = over(give_a, turn)
        got_a, give_b = together(got_a, give_b)
        block_a = added(keep_a, got_a)
        sent_a = [over(block_a, bit) for bit in wide[:1]]
        input_grad, small = fillers[1](results, rest, block_a)
        for bit in wide[1:]:
            block_a = added(block_a, sent_a.pop())
            sent_a = [over(block_a, bit)]
        *sent_a, got_b, small = together(*sent_a, got_b, small)
        if sent_a:
            block_a = added(block_a, sent_a[0])
        block_b = added(keep_b, got_b)

        keep_b, give_b = sides(block_b, "dp", near)
        moved = over(give_b, near), over(block_a, turn), over(small, 1)
        block_out = fillers[0](together(give_b, block_a, small)[0])
        got_b, got_a, got_s, block_out = together(*moved, block_out)
        block_a, small = joined(block_a, got_a, side(turn)), small + got_s
        spread_a = over(block_a, near)
        keep_b, give_b = sides(added(keep_b, got_b), "dp", turn)
        got_b, got_s = together(over(give_b, turn), over(small, near))
        block_b, small = added(keep_b, got_b), small + got_s
        for bit in wide:
            got_b, got_s = together(over(block_b, bit), over(small, bit))
            block_b, small = added(block_b, got_b), small + got_s
        got_b, got_s, spread_a = together(over(block_b, turn), over(small, turn), spread_a)
        block_b, small = joined(block_b, got_b, side(turn)), small + got_s
        block_a = joined(block_a, spread_a, side(near))
        got_b, got_s = together(over(block_b, near), across(cut(small, 1 - mine, 2)[0]))
        block_b, total = joined(block_b, got_b, side(near)), cut(small, mine, 2)[0] + got_s
        size = out_block.shape[0] // 2
        swapped_a, swapped_b, *g_small = together(swap(block_a, "dp", 1), swap(block_b, "dp", 1), *fillers[2](total))
        g_out = joined(block_a[:size], swapped_a[:size], core, 1).astype(F32)
        g_rows = [joined(block_a[size:], swapped_a[size:], core), joined(block_b, swapped_b, core)]
        return g_out, [rows.astype(F32) for rows in g_rows], g_small, input_grad, block_out


def shards(
    tokens,
    live,
    norm_gain,
    w_in,
    conv_weight,
    conv_bias,
    dt_bias,
    a_log,
    d_skip,
    inner_gain,
    w_out,
    cotangent,
):
    groups, copies = lax.axis_size("fsdp"), lax.axis_size("dp")
    taps = conv_weight.shape[1]
    heads = dt_bias.shape[0] * groups
    inner, conv = inner_gain.shape[0] * groups, conv_bias.shape[0] * groups
    model = tokens.shape[-1]
    proj = w_in.shape[1]
    main = inner + conv
    sizes = (inner, conv, heads, (conv - inner) // 2)
    paired = groups == 2 and powers_of_two(copies) and copies > 2 and main % 32 == 0
    links = Paired() if paired else Plain()

    rest = jnp.concatenate([norm_gain, dt_bias, a_log, d_skip])
    line = max(conv_bias.shape[0], inner_gain.shape[0], rest.shape[0])
    lined = lambda table: jnp.pad(table, ((0, 0), (0, line - table.shape[1])))
    packed = jnp.concatenate([lined(conv_weight.T), lined(conv_bias[None]), lined(inner_gain[None]), lined(rest[None])])

    def prepare(packed):
        packed = packed.astype(F32)
        pick = lambda row, first, each: packed[:, row, first : first + each].reshape(-1)
        model_each, heads_each = norm_gain.shape[0], dt_bias.shape[0]
        table = packed[:, : taps + 1, : conv // groups].transpose(1, 0, 2).reshape(taps + 1, conv)
        table = jnp.concatenate([table, jnp.zeros((7 - taps, conv), F32)], axis=0)
        taps_in = table.reshape(8, conv // LANES, LANES).transpose(1, 0, 2)
        inner_all = pick(taps + 1, 0, inner // groups)[:, None]
        gain_all = pick(taps + 2, 0, model_each)[None]
        by_head = [pick(taps + 2, model_each + k * heads_each, heads_each) for k in range(3)]
        return [taps_in, inner_all, gain_all, jnp.stack(by_head[:2], axis=1), by_head[2]]

    in_pieces, raw_weight, prepared, out_pieces = links.gather(w_in, packed, w_out, main, prepare)
    raw_weight = jnp.pad(raw_weight, ((0, 32 - raw_weight.shape[0]), (0, 0)))
    taps_in, inner_all, gain_all, heads_in, skip = prepared

    alive = live.astype(F32).reshape(1)
    low_tokens, low_cotangent = tokens[0, 0], cotangent[0, 0]
    normed, mixed, active, raw, states, gate, scanned, weight = forward(
        sizes, in_pieces[1], low_tokens, gain_all, raw_weight, taps_in, heads_in, in_pieces[0], in_pieces[2]
    )
    out_pieces = links.late(*out_pieces, normed)
    low_mixed, d_gate, d_scan, row_part, skip_part, gain_part, out_weight = gated(
        sizes, out_pieces[1], skip, alive, low_cotangent, inner_all, gate, scanned, active, out_pieces[0], out_pieces[2]
    )
    u = low_tokens.astype(F32)
    incoming = low_cotangent.astype(F32) * alive[0]

    def backward_step(first, count):
        def step(earlier, *sent):
            scan = after(d_scan, *sent) if sent else d_scan
            return backward(
                sizes,
                first,
                count,
                skip,
                active,
                mixed,
                scan,
                raw,
                row_part,
                states,
                taps_in,
                heads_in,
                earlier[-1] if earlier else None,
            )

        return step

    kernels = [backward_step(first, count) for first, count in HEAD_RANGES]

    step = 64
    rest_columns = -(-(proj - inner) // step) * step

    def input_part(results, rest, tie):
        d_raw, rate_part = [jnp.concatenate([result[k] for result in results], axis=0) for k in (1, 2)]
        conv_part = jnp.concatenate([result[3] for result in results], axis=1).reshape(taps + 1, conv)
        input_grad, gain_part_in = input_backward(
            alive, low_tokens, low_cotangent, gain_all, d_gate, after(rest, tie), weight
        )
        terms = [
            conv_part,
            jnp.sum(gain_part, axis=1)[None],
            jnp.sum(gain_part_in, axis=0)[None],
            jnp.sum(d_raw, axis=1)[None],
            jnp.sum(rate_part, axis=1)[None],
            jnp.sum(skip_part, axis=1)[None],
        ]
        by_owner = [
            jnp.moveaxis(term.reshape(term.shape[0], groups, -1), 1, 0).reshape(groups, -1) for term in terms
        ]
        count = sum(term.shape[1] for term in by_owner)
        by_owner.append(jnp.zeros((groups, -count % (8 * LANES)), F32))
        return input_grad, jnp.concatenate(by_owner, axis=1).reshape(groups, -1, LANES)

    def out_part(tie):
        branch = mul_tn(after(low_mixed, tie), out_weight)
        return (alive[0] * (u + branch)).astype(BF16)

    def small_grads(total):
        total = total.reshape(-1)
        shapes = [(taps + 1, conv), (1, inner), (1, model), (1, heads), (1, heads), (1, heads)]
        first, parts = 0, []
        for lines, line in shapes:
            size = lines * line // groups
            parts.append(total[first : first + size].reshape(lines, -1))
            first += size
        g_conv, g_inner, g_gain, g_bias, g_rate, g_skip = parts
        return [g_gain[0], g_conv[:taps].T, g_conv[taps], g_bias[0], g_rate[0], g_skip[0], g_inner[0]]

    g_out, g_rows, g_small, input_grad, block_out = links.sums(
        low_mixed,
        incoming.astype(BF16),
        d_gate,
        normed,
        kernels,
        rest_columns,
        [out_part, input_part, small_grads],
    )
    g_proj = jnp.concatenate([g_rows[0], g_rows[1][: proj - inner]], axis=0).T
    return (
        block_out.reshape(tokens.shape),
        input_grad.reshape(cotangent.shape),
        g_small[0],
        g_proj,
        *g_small[1:],
        g_out,
    )


def solution(mesh):
    by_device = P("fsdp", "dp", None, None)
    lines, tables = P("fsdp"), P("fsdp", None)
    return jax.shard_map(
        shards,
        mesh=mesh,
        in_specs=(
            by_device,
            P("fsdp", "dp"),
            lines,
            tables,
            tables,
            lines,
            lines,
            lines,
            lines,
            lines,
            tables,
            by_device,
        ),
        out_specs=(by_device, by_device, lines, tables, tables, lines, lines, lines, lines, lines, tables),
        check_vma=False,
    )
```
